32 devices in a mesh: plane: 16 (over z, y, core), thick: 2 (over x).
Axes of the slice: x: 2, y: 2, z: 4, core: 2. Of those that a mesh axis runs over, the one named last changes fastest.
Arguments:
- solid: int32 [4, 16, 8, 128], P('thick', 'plane'), may hold values 0 or 1
- labels: int32 [4, 16, 8, 128], P('thick', 'plane'), may hold values 0 or 1
- density: float32 [4, 16, 8, 128], P('thick', 'plane'), may hold values from 0.5 to 2
- wettability: float32 [4, 16, 8, 128], P('thick', 'plane'), may hold values from -1 to 1
- direction: float32 [4, 16, 8, 128], P('thick', 'plane'), may hold values from -6 to 6
- pixel_map: int32 [16, 8, 128], P('plane'), may hold values from 0 to 127
Outputs:
- curvature: float32 [4, 16, 8, 128], P('thick', 'plane')
- readings: float32 [16, 8, 128], P('plane')
The draws below stay inside these ranges and needn't reach their ends.
All inputs are finite; a program needn't handle non-finite values. No bound on the sum of `solid` or of `labels` on one device may be relied on, other than what follows from the above.
Results may differ from the reference program's by a relative error of at most 0.0001.
Values sent between devices are 32-bit elements; how exact they have to be, the bound alone decides.
No kernel may reach another device: no remote copies, remote signals or barrier semaphores. Data moves between devices by JAX's collectives and lax.ppermute only.
A program may use at most 64 MiB of HBM per device.

```python
import math
import jax
import jax.numpy as jnp
import numpy as np
from jax import lax

BX = 8
BY = 128
NBX = 8
STEPS = 2
BRICKS = 16
NZ = 4


def with_ends(result, rng, smallest, top_value):
    longest = result.shape.index(max(result.shape))
    spots = []
    for shift in (0, 1):
        where = [jax.random.randint(jax.random.fold_in(rng, axis), (), 0, length) for axis, length in enumerate(result.shape)]
        where[longest] = (where[longest] + shift) % result.shape[longest]
        spots.append(tuple(where))
    return result.at[spots[0]].set(smallest).at[spots[1]].set(top_value)


def block_scale(stream_key, dims, cuts, smallest, high):
    factor_of = 1.0
    for position, parts in cuts:
        draws = jax.random.uniform(jax.random.fold_in(jax.random.fold_in(stream_key, 6), position), (parts,), jnp.float32, smallest / len(cuts), high / len(cuts))
        factor_of = factor_of * jnp.repeat(jnp.exp(draws), dims[position] // parts).reshape((-1,) + (1,) * (len(dims) - 1 - position))
    return factor_of


def centred(own_key, dims, scale, limit, cuts=(), kind=jnp.bfloat16):
    loudness = block_scale(own_key, dims, cuts, -0.22, 0.18) if cuts else 1.0
    drawn = jax.random.normal(own_key, dims, jnp.float32) * scale * loudness
    return jnp.minimum(jnp.maximum(drawn, -limit), limit).astype(kind)


def setup_inputs(seed: int = 0) -> dict:
    arg_keys = jax.random.split(jax.random.key(seed), 7)
    return {
        "solid": with_ends((jax.random.randint(arg_keys[0], (NZ, BRICKS, BX, BY), 0, 4) < 1).astype(jnp.int32), jax.random.fold_in(arg_keys[0], 1), 0, 1),
        "labels": with_ends((jax.random.randint(arg_keys[1], (NZ, BRICKS, BX, BY), 0, 2) < 1).astype(jnp.int32), jax.random.fold_in(arg_keys[1], 1), 0, 1),
        "density": jnp.clip(jnp.exp(math.log(2.0) - 1.3862944 * jax.random.uniform(arg_keys[2], (NZ, BRICKS, BX, BY), jnp.float32) ** block_scale(arg_keys[2], (NZ, BRICKS, BX, BY), ((0, 2), (1, 16)), -0.2, 0.2)), 0.5, 2.0),
        "wettability": jnp.clip(jax.random.uniform(arg_keys[3], (NZ, BRICKS, BX, BY), jnp.float32, -1.0, 1.0) * block_scale(arg_keys[3], (NZ, BRICKS, BX, BY), ((0, 2), (1, 16)), -0.4, 0.0), -1.0, 1.0),
        "direction": centred(arg_keys[4], (NZ, BRICKS, BX, BY), 1.0, 6.0, ((0, 2), (1, 16)), jnp.float32),
        "pixel_map": with_ends(jax.random.randint(arg_keys[5], (BRICKS, BX, BY), 0, BY), jax.random.fold_in(arg_keys[5], 1), 0, BY - 1).astype(jnp.int32),
    }


VELOCITIES = np.array([[0, 0, 0], [1, 0, 0], [-1, 0, 0], [0, 1, 0], [0, -1, 0], [0, 0, 1], [0, 0, -1], [1, 1, 0], [-1, -1, 0], [1, -1, 0], [-1, 1, 0], [1, 0, 1], [-1, 0, -1], [1, 0, -1], [-1, 0, 1], [0, 1, 1], [0, -1, -1], [0, 1, -1], [0, -1, 1]])
WEIGHTS = np.array([1.0 / 3.0] + [1.0 / 18.0] * 6 + [1.0 / 36.0] * 12)
OPPOSITE = [int(np.argmin(np.abs(VELOCITIES + lattice_vec).sum(1))) for lattice_vec in VELOCITIES]
RELAX_RATE = 1.25
SURFACE_TENSION = 0.2
RECOLOURING_PACE = 0.7

def weights_like(array):
    return jnp.asarray(WEIGHTS, jnp.float32).reshape((19,) + (1,) * (array.ndim - 1))

def collide(red_pop, blue_pop, gradient, solid_cell):
    lattice_vel = jnp.asarray(VELOCITIES, jnp.float32)
    weight_column_vec = weights_like(red_pop)
    red_density_total = lax.optimization_barrier(jnp.sum(red_pop, 0))
    blue_density_total = lax.optimization_barrier(jnp.sum(blue_pop, 0))
    density = red_density_total + blue_density_total
    reciprocal_value = 1.0 / (density + solid_cell)
    total_pop = red_pop + blue_pop
    velocity = jnp.einsum('qd,q...->d...', lattice_vel, total_pop, precision=lax.Precision.HIGHEST) * reciprocal_value
    projected = jnp.einsum('qd,d...->q...', lattice_vel, velocity, precision=lax.Precision.HIGHEST)
    speed_sq = lax.optimization_barrier(jnp.sum(velocity * velocity, 0))
    equilibrium = weight_column_vec * density * (1.0 + 3.0 * projected + 4.5 * projected * projected - 1.5 * speed_sq)
    relaxed_populations = total_pop + RELAX_RATE * (equilibrium - total_pop)
    along_gradient_dir = jnp.einsum('qd,d...->q...', lattice_vel, gradient, precision=lax.Precision.HIGHEST)
    grad_sq = lax.optimization_barrier(jnp.sum(gradient * gradient, 0))
    norm_scale_factor = 1.0 / jnp.sqrt(1.0 + grad_sq)
    relaxed_populations = relaxed_populations + SURFACE_TENSION * weight_column_vec * (along_gradient_dir * along_gradient_dir - grad_sq / 3.0) * norm_scale_factor
    red_output_pop = red_density_total * reciprocal_value * relaxed_populations + RECOLOURING_PACE * red_density_total * blue_density_total * reciprocal_value * weight_column_vec * along_gradient_dir * norm_scale_factor
    return (red_output_pop, relaxed_populations - red_output_pop)

def phase_of(red_pop, blue_pop, solid_cell):
    red_density_total = lax.optimization_barrier(jnp.sum(red_pop, 0))
    blue_density_total = lax.optimization_barrier(jnp.sum(blue_pop, 0))
    return (red_density_total - blue_density_total) / (red_density_total + blue_density_total + solid_cell)

def pull_from(padded, offset, extent):
    shift_z, shift_x, shift_y = (int(offset[0]), int(offset[1]), int(offset[2]))
    return padded[..., 1 - shift_z:1 - shift_z + extent[0], 1 - shift_x:1 - shift_x + extent[1], 1 - shift_y:1 - shift_y + extent[2]]

def gradient_of(padded, extent):
    components = [0.0, 0.0, 0.0]
    for number in range(1, 19):
        lattice_vec = VELOCITIES[number]
        pulled = pull_from(padded, -lattice_vec, extent)
        for axis_num in range(3):
            if lattice_vec[axis_num] != 0:
                components[axis_num] = components[axis_num] + 3.0 * WEIGHTS[number] * float(lattice_vec[axis_num]) * pulled
    return jnp.stack(components)

def stream(padded_pop, local_pop, padded_fluid, fluid_cell, extent):
    outgoing = []
    for number in range(19):
        lattice_vec = VELOCITIES[number]
        source_fluid = pull_from(padded_fluid, lattice_vec, extent)
        arrived = pull_from(padded_pop[number], lattice_vec, extent)
        outgoing.append(fluid_cell * (source_fluid * arrived + (1.0 - source_fluid) * local_pop[OPPOSITE[number]]))
    return jnp.stack(outgoing)

def pad_bricks(array):
    bricks_y = BRICKS // NBX
    lead = [(0, 0)] * (array.ndim - 3)
    padded_z = jnp.pad(array, lead + [(1, 1), (0, 0), (0, 0)])
    above = jnp.roll(padded_z, bricks_y, axis=-4)[..., BX - 1:BX, :]
    below = jnp.roll(padded_z, -bricks_y, axis=-4)[..., 0:1, :]
    padded_x = jnp.concatenate([above, padded_z, below], axis=-2)
    before = jnp.roll(padded_x, 1, axis=-4)[..., BY - 1:BY]
    after = jnp.roll(padded_x, -1, axis=-4)[..., 0:1]
    return jnp.concatenate([before, padded_x, after], axis=-1)

def to_bricks(array):
    return jnp.transpose(array, (1, 0, 2, 3))

def reference(solid, labels, density, wettability, direction, pixel_map):
    solid_cell = to_bricks(solid).astype(jnp.float32)
    fluid_cell = 1.0 - solid_cell
    label_cell = to_bricks(labels).astype(jnp.float32)
    density_cell = to_bricks(density)
    weight_column_vec = weights_like(solid_cell[None])
    red_start = weight_column_vec * (density_cell * label_cell * fluid_cell)[None]
    blue_start = weight_column_vec * (density_cell * (1.0 - label_cell) * fluid_cell)[None]
    extent = solid_cell.shape[1:]
    padded_fluid = pad_bricks(fluid_cell)

    def observe(wetting):
        red_pop, blue_pop = (red_start, blue_start)
        for number in range(STEPS):
            phase_field = fluid_cell * phase_of(red_pop, blue_pop, solid_cell) + solid_cell * wetting
            gradient = gradient_of(pad_bricks(phase_field), extent)
            red_post, blue_post = collide(red_pop, blue_pop, gradient, solid_cell)
            red_pop = stream(pad_bricks(red_post), red_post, padded_fluid, fluid_cell, extent)
            blue_pop = stream(pad_bricks(blue_post), blue_post, padded_fluid, fluid_cell, extent)
        column = lax.optimization_barrier(jnp.sum(fluid_cell * phase_of(red_pop, blue_pop, solid_cell), 1))
        return jnp.take_along_axis(column, pixel_map, axis=2)
    wetting = to_bricks(wettability)
    tangent = to_bricks(direction)
    _, readings = jax.jvp(observe, (wetting,), (tangent,))
    _, backward = jax.vjp(observe, wetting)
    hessian_vec, = backward(readings)
    return (to_bricks(hessian_vec), readings)
```

```python
import functools

import jax
import jax.numpy as jnp
import numpy as np
from jax import lax
from jax.experimental import pallas as pl
from jax.experimental.pallas import tpu as pltpu
from jax.sharding import PartitionSpec as P

NBX = 8
STEPS = 2


VELOCITIES = np.array(
    [
        [0, 0, 0],
        [1, 0, 0],
        [-1, 0, 0],
        [0, 1, 0],
        [0, -1, 0],
        [0, 0, 1],
        [0, 0, -1],
        [1, 1, 0],
        [-1, -1, 0],
        [1, -1, 0],
        [-1, 1, 0],
        [1, 0, 1],
        [-1, 0, -1],
        [1, 0, -1],
        [-1, 0, 1],
        [0, 1, 1],
        [0, -1, -1],
        [0, 1, -1],
        [0, -1, 1],
    ]
)
WEIGHTS = np.array([1.0 / 3.0] + [1.0 / 18.0] * 6 + [1.0 / 36.0] * 12)
OPPOSITE = [int(np.argmin(np.abs(VELOCITIES + lattice_vec).sum(1))) for lattice_vec in VELOCITIES]
RELAX_RATE = 1.25
SURFACE_TENSION = 0.2
RECOLOURING_PACE = 0.7


def shifted(array, axis, by):
    devices = lax.axis_size(axis)
    pairs = [(i, i + by) for i in range(devices) if 0 <= i + by < devices]
    return lax.ppermute(array, axis, pairs)


def from_behind(block, axis, distance):
    devices = range(lax.axis_size(axis))
    route = [((i - distance) % len(devices), i) for i in devices]
    return lax.ppermute(block, axis, route)


def weights_like(array):
    return jnp.asarray(WEIGHTS, jnp.float32).reshape((19,) + (1,) * (array.ndim - 1))


def collide(red_pop, blue_pop, gradient, solid_cell):
    lattice_vel = jnp.asarray(VELOCITIES, jnp.float32)
    weight_column_vec = weights_like(red_pop)
    red_density_total = jnp.sum(red_pop, 0)
    blue_density_total = jnp.sum(blue_pop, 0)
    density = red_density_total + blue_density_total
    reciprocal_value = 1.0 / (density + solid_cell)
    total_pop = red_pop + blue_pop
    velocity = (
        jnp.einsum("qd,q...->d...", lattice_vel, total_pop, precision=lax.Precision.HIGHEST)
        * reciprocal_value
    )
    projected = jnp.einsum("qd,d...->q...", lattice_vel, velocity, precision=lax.Precision.HIGHEST)
    speed_sq = jnp.sum(velocity * velocity, 0)
    equilibrium = (
        weight_column_vec
        * density
        * (1.0 + 3.0 * projected + 4.5 * projected * projected - 1.5 * speed_sq)
    )
    relaxed_populations = total_pop + RELAX_RATE * (equilibrium - total_pop)
    along_gradient_dir = jnp.einsum(
        "qd,d...->q...", lattice_vel, gradient, precision=lax.Precision.HIGHEST
    )
    grad_sq = jnp.sum(gradient * gradient, 0)
    norm_scale_factor = 1.0 / jnp.sqrt(1.0 + grad_sq)
    relaxed_populations = (
        relaxed_populations
        + SURFACE_TENSION
        * weight_column_vec
        * (along_gradient_dir * along_gradient_dir - grad_sq / 3.0)
        * norm_scale_factor
    )
    red_output_pop = (
        red_density_total * reciprocal_value * relaxed_populations
        + RECOLOURING_PACE
        * red_density_total
        * blue_density_total
        * reciprocal_value
        * weight_column_vec
        * along_gradient_dir
        * norm_scale_factor
    )
    return (red_output_pop, relaxed_populations - red_output_pop)


def phase_of(red_pop, blue_pop, solid_cell):
    red_density_total = jnp.sum(red_pop, 0)
    blue_density_total = jnp.sum(blue_pop, 0)
    return (red_density_total - blue_density_total) / (
        red_density_total + blue_density_total + solid_cell
    )


def pull_from(padded, offset, extent):
    shift_z, shift_x, shift_y = (int(offset[0]), int(offset[1]), int(offset[2]))
    return padded[
        ...,
        1 - shift_z : 1 - shift_z + extent[0],
        1 - shift_x : 1 - shift_x + extent[1],
        1 - shift_y : 1 - shift_y + extent[2],
    ]


def gradient_of(padded, extent):
    components = [0.0, 0.0, 0.0]
    for number in range(1, 19):
        lattice_vec = VELOCITIES[number]
        pulled = pull_from(padded, -lattice_vec, extent)
        for axis_num in range(3):
            if lattice_vec[axis_num] != 0:
                components[axis_num] = (
                    components[axis_num]
                    + 3.0 * WEIGHTS[number] * float(lattice_vec[axis_num]) * pulled
                )
    return jnp.stack(components)


def spread_back(padded_bar, extent):
    total_bar = 0.0
    for number in range(1, 19):
        lattice_vec = VELOCITIES[number]
        for axis_num in range(3):
            if lattice_vec[axis_num] != 0:
                total_bar = total_bar + 3.0 * WEIGHTS[number] * float(
                    lattice_vec[axis_num]
                ) * pull_from(padded_bar[axis_num], lattice_vec, extent)
    return total_bar


def stream(padded_pop, local_pop, padded_fluid, fluid_cell, extent):
    outgoing = []
    for number in range(19):
        lattice_vec = VELOCITIES[number]
        source_fluid = pull_from(padded_fluid, lattice_vec, extent)
        arrived = pull_from(padded_pop[number], lattice_vec, extent)
        outgoing.append(
            fluid_cell
            * (source_fluid * arrived + (1.0 - source_fluid) * local_pop[OPPOSITE[number]])
        )
    return jnp.stack(outgoing)


def unstream(padded_bar, local_bar, padded_fluid, fluid_cell, extent):
    incoming = []
    for number in range(19):
        lattice_vec = VELOCITIES[number]
        ahead_fluid = pull_from(padded_fluid, -lattice_vec, extent)
        ahead_bar = pull_from(padded_bar[number], -lattice_vec, extent)
        incoming.append(fluid_cell * ahead_bar + (1.0 - ahead_fluid) * local_bar[OPPOSITE[number]])
    return jnp.stack(incoming)


def fill_border(received, chosen, channels):
    if len(chosen) == channels:
        return received
    return (
        jnp.zeros((channels,) + received.shape[1:], received.dtype)
        .at[np.array(chosen)]
        .set(received)
    )


def grow(stacked, axis_dim, chosen_low, chosen_high, sender):
    length = stacked.shape[axis_dim]
    channels = stacked.shape[0]
    borders = []
    for toward in (1, -1):
        chosen = chosen_low if toward == 1 else chosen_high
        source = length - 1 if toward == 1 else 0
        outer_layer = lax.slice_in_dim(stacked, source, source + 1, axis=axis_dim)
        if len(chosen) < channels:
            outer_layer = outer_layer[np.array(chosen)]
        borders.append(fill_border(sender(outer_layer, toward), chosen, channels))
    return jnp.concatenate([borders[0], stacked, borders[1]], axis_dim)


def per_device(solid, labels, density, wettability, direction, pixel_map):
    solid_cell = solid[:, 0].astype(jnp.float32)
    fluid_cell = 1.0 - solid_cell
    label_cell = labels[:, 0].astype(jnp.float32)
    density_cell = density[:, 0]
    wetting = wettability[:, 0]
    tangent = direction[:, 0]
    column_map = pixel_map[0]
    extent = solid_cell.shape
    bricks_y = lax.axis_size("plane") // NBX

    def extend(stacked):
        channels = stacked.shape[0]

        def chosen_for():
            return list(range(channels))

        stacked = grow(
            stacked,
            1,
            chosen_for(),
            chosen_for(),
            lambda outgoing, toward: shifted(outgoing, "thick", toward),
        )
        stacked = grow(
            stacked,
            2,
            chosen_for(),
            chosen_for(),
            lambda outgoing, toward: from_behind(outgoing, "plane", toward * bricks_y),
        )
        stacked = grow(
            stacked,
            3,
            chosen_for(),
            chosen_for(),
            lambda outgoing, toward: from_behind(outgoing, "plane", toward),
        )
        return stacked

    def phase_pair(red_in, blue_in):
        return phase_of(red_in, blue_in, solid_cell)

    def collide_local(red_in, blue_in, gradient):
        return collide(red_in, blue_in, gradient, solid_cell)

    padded_fluid = extend(fluid_cell[None])[0]
    weight_column_vec = weights_like(solid_cell[None])
    red_pop = weight_column_vec * (density_cell * label_cell * fluid_cell)[None]
    blue_pop = weight_column_vec * (density_cell * (1.0 - label_cell) * fluid_cell)[None]
    red_tan = jnp.zeros_like(red_pop)
    blue_tan = jnp.zeros_like(blue_pop)
    checkpoints = []
    for number in range(STEPS):
        phase_val, phase_tan = jax.jvp(phase_pair, (red_pop, blue_pop), (red_tan, blue_tan))
        phase_field = fluid_cell * phase_val + solid_cell * wetting
        field_tan = fluid_cell * phase_tan + solid_cell * tangent
        padded = extend(jnp.stack([phase_field, field_tan]))
        gradient = gradient_of(padded[0], extent)
        gradient_tan = gradient_of(padded[1], extent)
        checkpoints.append((red_pop, blue_pop, gradient))
        (red_post, blue_post), (red_dot, blue_dot) = jax.jvp(
            collide_local, (red_pop, blue_pop, gradient), (red_tan, blue_tan, gradient_tan)
        )
        posted = jnp.concatenate([red_post, blue_post, red_dot, blue_dot])
        moved = extend(posted)
        red_pop, blue_pop, red_tan, blue_tan = [
            stream(
                moved[19 * group : 19 * group + 19],
                posted[19 * group : 19 * group + 19],
                padded_fluid,
                fluid_cell,
                extent,
            )
            for group in range(4)
        ]
    _, phase_tan = jax.jvp(phase_pair, (red_pop, blue_pop), (red_tan, blue_tan))
    partial_sum = jnp.sum(fluid_cell * phase_tan, 0)
    column_sum = lax.psum(partial_sum, "thick")
    found = jnp.take_along_axis(column_sum, column_map, axis=1)
    row_ids = jnp.arange(column_map.shape[0])[:, None]
    seeded = jnp.zeros_like(column_sum).at[row_ids, column_map].add(found)
    _, phase_back = jax.vjp(phase_pair, red_pop, blue_pop)
    red_bar, blue_bar = phase_back(fluid_cell * seeded[None])
    wetting_bar = jnp.zeros_like(wetting)
    for number in reversed(range(STEPS)):
        red_saved, blue_saved, gradient = checkpoints[number]
        outgoing_bar = jnp.concatenate([red_bar, blue_bar]) * fluid_cell
        padded = extend(outgoing_bar)
        red_pre = unstream(padded[:19], outgoing_bar[:19], padded_fluid, fluid_cell, extent)
        blue_pre = unstream(padded[19:], outgoing_bar[19:], padded_fluid, fluid_cell, extent)
        _, collide_back = jax.vjp(collide_local, red_saved, blue_saved, gradient)
        red_bar, blue_bar, gradient_bar = collide_back((red_pre, blue_pre))
        padded_bar = extend(gradient_bar)
        field_bar = spread_back(padded_bar, extent)
        wetting_bar = wetting_bar + solid_cell * field_bar
        if number > 0:
            _, phase_back = jax.vjp(phase_pair, red_saved, blue_saved)
            extra_red, extra_blue = phase_back(fluid_cell * field_bar)
            red_bar = red_bar + extra_red
            blue_bar = blue_bar + extra_blue
    return (wetting_bar[:, None], found[None])


HALF = 128
WIDE = 256
ROW_TILES = 3
Z_AXIS, X_AXIS, Y_AXIS = range(3)
EDGES = [(0, 1, 1), (0, 1, -1), (0, 2, 1), (0, 2, -1), (1, 2, 1), (1, 2, -1)]
CZ = [int(v[0]) for v in VELOCITIES]
CX = [int(v[1]) for v in VELOCITIES]
CY = [int(v[2]) for v in VELOCITIES]
GROUPS = [(gx, gy) for gx in (-1, 0, 1) for gy in (-1, 0, 1)]


def roll_rows(tile, by):
    return pltpu.roll(tile, by % tile.shape[0], 0)


def roll_lanes(tile, by):
    return pltpu.roll(tile, by % tile.shape[1], 1)


def x_shift(tiles, dx):
    row = lax.broadcasted_iota(jnp.int32, tiles[0].shape, 0)
    out = []
    for r in range(ROW_TILES):
        beyond = tiles[(r + dx) % ROW_TILES]
        edge = 0 if dx == 1 else 7
        out.append(roll_rows(jnp.where(row == edge, beyond, tiles[r]), -dx))
    return out


def y_shift(tiles, dy):
    return [roll_lanes(tile, -dy) for tile in tiles]


def each(function, *lists):
    return [function(*items) for items in zip(*lists)]


def add(a, b):
    return a + b


def sub(a, b):
    return a - b


def both_ways(shift, tiles):
    return shift(tiles, 1), shift(tiles, -1)


def plane(ref, zi):
    return [ref[zi, r] for r in range(ROW_TILES)]


def gradient_tiles(ref, zi):
    mid, up, down = plane(ref, zi), plane(ref, zi + 1), plane(ref, zi - 1)
    two = each(lambda m, u, d: 2.0 * m + u + d, mid, up, down)
    slope = each(sub, up, down)
    y_sum = each(add, *both_ways(y_shift, mid))
    x_sum = each(add, *both_ways(x_shift, mid))
    along_x = each(sub, *both_ways(x_shift, each(add, two, y_sum)))
    along_y = each(sub, *both_ways(y_shift, each(add, two, x_sum)))
    sx = each(add, *both_ways(x_shift, slope))
    sy = each(add, *both_ways(y_shift, slope))
    along_z = each(lambda s, a, b: 2.0 * s + a + b, slope, sx, sy)
    return along_z, along_x, along_y


def gradient_back(refs, zi):
    gz, gx, gy = refs
    mid, up, down = plane(gx, zi), plane(gx, zi + 1), plane(gx, zi - 1)
    y_sum = each(add, *both_ways(y_shift, mid))
    total = each(lambda m, u, d, s: 2.0 * m + u + d + s, mid, up, down, y_sum)
    result = each(sub, *both_ways(x_shift, total))
    mid, up, down = plane(gy, zi), plane(gy, zi + 1), plane(gy, zi - 1)
    x_sum = each(add, *both_ways(x_shift, mid))
    total = each(lambda m, u, d, s: 2.0 * m + u + d + s, mid, up, down, x_sum)
    result = each(add, result, each(sub, *both_ways(y_shift, total)))
    slope = each(sub, plane(gz, zi + 1), plane(gz, zi - 1))
    sx = each(add, *both_ways(x_shift, slope))
    sy = each(add, *both_ways(y_shift, slope))
    return each(lambda a, s, b, c: a + 2.0 * s + b + c, result, slope, sx, sy)


def even_part(base, quad):
    zz, xx, yy, zx, zy, xy = quad
    out = [2.0 * (base + zz), 2.0 * (base + xx), 2.0 * (base + yy)]
    for diagonal, cross in ((zz + xx, zx), (zz + yy, zy), (xx + yy, xy)):
        flat = base + diagonal
        out += [flat + cross, flat - cross]
    return out


def odd_part(vector):
    z, x, y = vector
    return [2.0 * z, 2.0 * x, 2.0 * y, z + x, z - x, z + y, z - y, x + y, x - y]


def squares(vector):
    z, x, y = vector
    return [z * z, x * x, y * y, 2.0 * (z * x), 2.0 * (z * y), 2.0 * (x * y)]


def squares_dot(a, b):
    az, ax, ay = a
    bz, bx, by = b
    return [
        2.0 * (az * bz),
        2.0 * (ax * bx),
        2.0 * (ay * by),
        2.0 * (az * bx + ax * bz),
        2.0 * (az * by + ay * bz),
        2.0 * (ax * by + ay * bx),
    ]


def dot(a, b):
    return a[0] * b[0] + a[1] * b[1] + a[2] * b[2]


def first_moment(values):
    d = [values[2 * p + 1] - values[2 * p + 2] for p in range(9)]
    return (
        d[0] + (d[3] + d[4]) + (d[5] + d[6]),
        d[1] + (d[3] - d[4]) + (d[7] + d[8]),
        d[2] + (d[5] - d[6]) + (d[7] - d[8]),
    )


def weighted_first(values):
    d = [values[2 * p + 1] - values[2 * p + 2] for p in range(9)]
    return (
        2.0 * d[0] + (d[3] + d[4]) + (d[5] + d[6]),
        2.0 * d[1] + (d[3] - d[4]) + (d[7] + d[8]),
        2.0 * d[2] + (d[5] - d[6]) + (d[7] - d[8]),
    )


def weighted_even(rest, pairs):
    axis = [2.0 * pairs[0], 2.0 * pairs[1], 2.0 * pairs[2]]
    zx, zy, xy = pairs[3] + pairs[4], pairs[5] + pairs[6], pairs[7] + pairs[8]
    second = [
        axis[0] + zx + zy,
        axis[1] + zx + xy,
        axis[2] + zy + xy,
        pairs[3] - pairs[4],
        pairs[5] - pairs[6],
        pairs[7] - pairs[8],
    ]
    zeroth = 12.0 * rest + axis[0] + axis[1] + axis[2] + zx + zy + xy
    return zeroth, second


def pair_sums(values):
    return [values[2 * p + 1] + values[2 * p + 2] for p in range(9)]


def times(matrix, vector):
    zz, xx, yy, zx, zy, xy = matrix
    z, x, y = vector
    return (zz * z + zx * x + zy * y, zx * z + xx * x + xy * y, zy * z + xy * x + yy * y)


def total(values):
    values = list(values)
    while len(values) > 1:
        values = [
            values[k] + values[k + 1] if k + 1 < len(values) else values[k]
            for k in range(0, len(values), 2)
        ]
    return values[0]


def norm_parts(g):
    g2 = dot(g, g)
    n = lax.rsqrt(1.0 + g2)
    return g2, n


def scatter_groups(acc, zi, r, values, stay):
    for k, (gx, gy) in enumerate(GROUPS):
        here = [i for i in range(1, 19) if (CX[i], CY[i]) == (gx, gy)]
        level = {CZ[i]: values[i] for i in here}
        if (gx, gy) == (0, 0):
            level[0] = values[0] + stay
        if 1 not in level:
            acc[k, zi, r] = level[0]
            continue
        acc[k, zi + 1, r] = level[1]
        acc[k, zi, r] = acc[k, zi, r] + level[0]
        acc[k, zi - 1, r] = acc[k, zi - 1, r] + level[-1]


def gathered_sum(acc, zi):
    by_y = []
    for gy in (-1, 0, 1):
        parts = [plane(acc.at[GROUPS.index((0, gy))], zi)]
        for gx in (-1, 1):
            parts.append(x_shift(plane(acc.at[GROUPS.index((gx, gy))], zi), -gx))
        by_y.append(each(lambda *a: total(a), *parts))
    return each(
        lambda a, b, c: a + b + c, y_shift(by_y[0], 1), by_y[1], y_shift(by_y[2], -1)
    )


def moved(ref, zi, i, sign):
    tiles = plane(ref, zi + sign * CZ[i])
    if CX[i]:
        tiles = x_shift(tiles, sign * CX[i])
    if CY[i]:
        tiles = y_shift(tiles, sign * CY[i])
    return tiles


def all_moved(ref, zi):
    out = [None] * 19
    for cz in (-1, 0, 1):
        base = plane(ref, zi + cz)
        rows = {0: base, 1: x_shift(base, 1), -1: x_shift(base, -1)}
        for i in range(19):
            if CZ[i] == cz:
                tiles = rows[CX[i]]
                out[i] = y_shift(tiles, CY[i]) if CY[i] else tiles
    return out


def main_kernel(nz, local_z, q_ref, qm_ref, qp_ref, sl_ref, map_ref, out_ref, read_ref,
                rho, p1, dp1, cnt, blk, t_st, dt_st, acc, pop, dpop, mac, p2, dp2, g1, g2s,
                a3, b3, col, adj, gbar, pbar2):
    thick = lax.axis_index("thick")
    even = lax.rem(lax.axis_index("plane"), 2) == 0
    per = 3 * local_z + 1
    f32 = jnp.float32
    zero_tile = jnp.zeros((8, WIDE), f32)

    for ref in (rho, p1, dp1, p2, dp2):
        for r in range(ROW_TILES):
            ref[0, r] = zero_tile
            ref[nz + 1, r] = zero_tile
    for k in range(3):
        for r in range(ROW_TILES):
            gbar[k, 0, r] = zero_tile
            gbar[k, nz + 1, r] = zero_tile
    for k in range(36):
        for r in range(ROW_TILES):
            acc[k, 1, r] = zero_tile
    lane = lax.broadcasted_iota(jnp.int32, (8, HALF), 1)
    low = lane < HALF // 2

    def sides(r, k, ks):
        if r == 0:
            middle = q_ref[2 * per + k]
            right = jnp.where(even, q_ref[k], qp_ref[k])
            left = jnp.where(even, qm_ref[k], q_ref[k])
        elif r == 1:
            middle = qp_ref[2 * per + k]
            right = jnp.where(even, qp_ref[k], sl_ref[ks])
            left = jnp.where(even, q_ref[k], qp_ref[k])
        else:
            middle = qm_ref[2 * per + k]
            right = jnp.where(even, qm_ref[k], q_ref[k])
            left = jnp.where(even, sl_ref[ks], qm_ref[k])
        return middle, jnp.where(low, right, left)

    for part in range(2):
        slab = thick if part == 0 else 1 - thick
        for zl in range(local_z):
            zi = 1 + slab * local_z + zl
            for r in range(ROW_TILES):
                for which, ref in enumerate((rho, p1, dp1)):
                    k = which * local_z + zl + part * per
                    middle, side = sides(r, k, k)
                    ref[zi, r, :, :HALF] = middle
                    ref[zi, r, :, HALF:] = side
    for r in range(ROW_TILES):
        middle, side = sides(r, per - 1, per - 1)
        cnt[r, :, :HALF] = middle
        cnt[r, :, HALF:] = side

    def links(z, carry):
        zi = z + 1
        here = each(lambda v: jnp.where(v == 0.0, 1.0, 0.0), plane(rho, zi))
        for cz in (-1, 0, 1):
            base = each(lambda v: jnp.where(v == 0.0, 1.0, 0.0), plane(rho, zi + cz))
            rows = {0: base, 1: x_shift(base, 1), -1: x_shift(base, -1)}
            for i in range(1, 19):
                if CZ[i] == cz:
                    tiles = rows[CX[i]]
                    tiles = y_shift(tiles, CY[i]) if CY[i] else tiles
                    for r in range(ROW_TILES):
                        blk[i - 1, z, r] = jnp.maximum(tiles[r], here[r])
        return carry

    lax.fori_loop(0, nz, links, 0)

    def link(z, r):
        return [None] + [blk[i, z, r] for i in range(18)]

    def collide_first(z, carry):
        zi = z + 1
        grads = gradient_tiles(p1, zi)
        dgrads = gradient_tiles(dp1, zi)
        for r in range(ROW_TILES):
            dens, psi = rho[zi, r], p1[zi, r]
            fluid = jnp.where(dens == 0.0, 0.0, 1.0)
            red = 0.5 * dens * (1.0 + psi)
            blue = 0.5 * dens * (1.0 - psi)
            alpha = red / (dens + (1.0 - fluid))
            beta = RECOLOURING_PACE * alpha * blue
            g = tuple(a[r] * (1.0 / 12.0) for a in grads)
            dg = tuple(a[r] * (1.0 / 12.0) for a in dgrads)
            gg, n = norm_parts(g)
            gdg = dot(g, dg)
            n2g = n * n * gdg
            dn = -n * n2g
            q = (SURFACE_TENSION * fluid) * n
            dq = -q * n2g
            for k in range(3):
                g1[k, zi, r] = g[k]
            sq, dsq = squares(g), squares_dot(g, dg)
            base = dens - q * gg * (1.0 / 3.0)
            dbase = (dq * gg + 2.0 * q * gdg) * (-1.0 / 3.0)
            ev = even_part(base, [q * v for v in sq])
            dev = even_part(dbase, [dq * v + q * d for v, d in zip(sq, dsq)])
            bn, bdn = beta * n, beta * dn
            od = odd_part([bn * v for v in g])
            dod = odd_part([bdn * v + bn * d for v, d in zip(g, dg)])
            for k in range(9):
                t_st[k, zi, r] = ev[k]
                dt_st[k, zi, r] = dev[k]
            pop[0, zi, r] = 12.0 * base
            dpop[0, zi, r] = 12.0 * dbase
            s = link(z, r)
            for first, rest, evens, odds in (
                (0, 12.0 * base, ev, od), (9, 12.0 * dbase, dev, dod)
            ):
                scaled = [alpha * v for v in evens]
                values = [alpha * rest]
                stay = []
                for k in range(9):
                    values += [scaled[k] + odds[k], scaled[k] - odds[k]]
                    stay += [s[2 * k + 1] * values[-2], s[2 * k + 2] * values[-1]]
                scatter_groups(acc.at[pl.ds(first, 9)], zi, r, values, total(stay))
        return carry

    lax.fori_loop(0, nz, collide_first, 0)

    def run_first(z, carry):
        zi = z + 1
        for ref, store in ((t_st, pop), (dt_st, dpop)):
            for i in range(1, 19):
                k = (i - 1) // 2
                arrived = moved(ref.at[k], zi, i, -1)
                for r in range(ROW_TILES):
                    blocked = blk[OPPOSITE[i] - 1, z, r] > 0.5
                    store[i, zi, r] = jnp.where(blocked, ref[k, zi, r], arrived[r])
        red_sum = gathered_sum(acc.at[pl.ds(0, 9)], zi)
        dred_sum = gathered_sum(acc.at[pl.ds(9, 9)], zi)
        for r in range(ROW_TILES):
            fluid = jnp.where(rho[zi, r] == 0.0, 0.0, 1.0)
            is_fluid = fluid > 0.5
            dens = total([pop[i, zi, r] for i in range(19)]) * (1.0 / 36.0)
            ddens = total([dpop[i, zi, r] for i in range(19)]) * (1.0 / 36.0)
            red = red_sum[r] * fluid * (1.0 / 36.0)
            dred = dred_sum[r] * fluid * (1.0 / 36.0)
            inv = 1.0 / (dens + (1.0 - fluid))
            psi = (2.0 * red - dens) * inv
            dpsi = (2.0 * dred - (1.0 + psi) * ddens) * inv
            for k, v in enumerate((dens, ddens, red, dred, inv, psi)):
                mac[k, zi, r] = v
            p2[zi, r] = jnp.where(is_fluid, psi, p1[zi, r])
            dp2[zi, r] = jnp.where(is_fluid, dpsi, dp1[zi, r])
        return carry

    lax.fori_loop(0, nz, run_first, 0)

    for k in range(36):
        for r in range(ROW_TILES):
            acc[k, 1, r] = zero_tile

    def collide_second(z, carry):
        zi = z + 1
        grads = gradient_tiles(p2, zi)
        dgrads = gradient_tiles(dp2, zi)
        for r in range(ROW_TILES):
            dens, ddens, red, dred, inv = [mac[k, zi, r] for k in range(5)]
            fluid = jnp.where(rho[zi, r] == 0.0, 0.0, 1.0)
            t = [pop[i, zi, r] for i in range(19)]
            dt = [dpop[i, zi, r] for i in range(19)]
            m = [v * (1.0 / 36.0) for v in first_moment(t)]
            dm = [v * (1.0 / 36.0) for v in first_moment(dt)]
            u = [inv * v for v in m]
            shrink = inv * ddens
            du = [inv * b - shrink * a for a, b in zip(u, dm)]
            g = tuple(a[r] * (1.0 / 12.0) for a in grads)
            dg = tuple(a[r] * (1.0 / 12.0) for a in dgrads)
            gg, n = norm_parts(g)
            gdg = dot(g, dg)
            n2g = n * n * gdg
            dn = -n * n2g
            q = (SURFACE_TENSION * fluid) * n
            dq = -q * n2g
            for k in range(3):
                g2s[k, zi, r] = g[k]
            base = RELAX_RATE * dens - (1.5 * RELAX_RATE) * dot(m, u) - q * gg * (1.0 / 3.0)
            dbase = (
                RELAX_RATE * ddens
                - (1.5 * RELAX_RATE) * (dot(dm, u) + dot(m, du))
                + (dq * gg + 2.0 * q * gdg) * (-1.0 / 3.0)
            )
            lin = odd_part([(3.0 * RELAX_RATE) * v for v in m])
            dlin = odd_part([(3.0 * RELAX_RATE) * v for v in dm])
            mq = [(4.5 * RELAX_RATE) * v for v in m]
            dmq = [(4.5 * RELAX_RATE) * v for v in dm]
            order = ((0, 0), (1, 1), (2, 2), (0, 1), (0, 2), (1, 2))
            sq, dsq = squares(g), squares_dot(g, dg)
            quad, dquad = [], []
            for k, (a, b) in enumerate(order):
                twice = 1.0 if a == b else 2.0
                flow = mq[a] * u[b]
                dflow = dmq[a] * u[b] + mq[a] * du[b]
                if a != b:
                    flow = 2.0 * flow
                    dflow = 2.0 * dflow
                quad.append(flow + q * sq[k])
                dquad.append(dflow + dq * sq[k] + q * dsq[k])
            ev, dev = even_part(base, quad), even_part(dbase, dquad)
            keep = 1.0 - RELAX_RATE
            after, dafter = [keep * t[0] + 12.0 * base], [keep * dt[0] + 12.0 * dbase]
            for k in range(9):
                after += [keep * t[2 * k + 1] + (ev[k] + lin[k]), keep * t[2 * k + 2] + (ev[k] - lin[k])]
                dafter += [
                    keep * dt[2 * k + 1] + (dev[k] + dlin[k]),
                    keep * dt[2 * k + 2] + (dev[k] - dlin[k]),
                ]
            alpha = red * inv
            dalpha = dred * inv - alpha * shrink
            blue, dblue = dens - red, ddens - dred
            beta = RECOLOURING_PACE * alpha * blue
            dbeta = RECOLOURING_PACE * (dalpha * blue + alpha * dblue)
            bn = beta * n
            dbn = dbeta * n + beta * dn
            od = odd_part([bn * v for v in g])
            dod = odd_part([dbn * v + bn * d for v, d in zip(g, dg)])
            reds, dreds = [alpha * after[0]], [dalpha * after[0] + alpha * dafter[0]]
            for i in range(1, 19):
                k = (i - 1) // 2
                side = od[k] if i % 2 else -od[k]
                dside = dod[k] if i % 2 else -dod[k]
                reds.append(alpha * after[i] + side)
                dreds.append(dalpha * after[i] + alpha * dafter[i] + dside)
            s = link(z, r)
            for k, values in enumerate((reds, dreds, after, dafter)):
                stay = total([s[i] * values[i] for i in range(1, 19)])
                scatter_groups(acc.at[pl.ds(9 * k, 9)], zi, r, values, stay)
        return carry

    lax.fori_loop(0, nz, collide_second, 0)

    for r in range(ROW_TILES):
        col[r] = zero_tile

    def final_phase(z, carry):
        zi = z + 1
        red_s, dred_s, dens_s, ddens_s = [gathered_sum(acc.at[pl.ds(9 * k, 9)], zi) for k in range(4)]
        for r in range(ROW_TILES):
            fluid = jnp.where(rho[zi, r] == 0.0, 0.0, 1.0)
            scale = fluid * (1.0 / 36.0)
            dens = dens_s[r] * scale
            inv = 1.0 / (dens + (1.0 - fluid))
            psi = (2.0 * (red_s[r] * scale) - dens) * inv
            a = 2.0 * (scale * inv)
            b = -(scale * inv) * (1.0 + psi)
            a3[zi, r] = a
            b3[zi, r] = b
            col[r] = col[r] + (a * dred_s[r] + b * ddens_s[r])
        return carry

    lax.fori_loop(0, nz, final_phase, 0)
    read_ref[...] = jnp.take_along_axis(col[0, :, :HALF], map_ref[...], axis=1)

    def seed(z, carry):
        zi = z + 1
        for r in range(ROW_TILES):
            column = col[r] * cnt[r]
            a3[zi, r] = a3[zi, r] * column
            b3[zi, r] = b3[zi, r] * column
        return carry

    lax.fori_loop(0, nz, seed, 0)

    def toward_gradient(g, fluid, zeroth, second, first, beta):
        gg, n = norm_parts(g)
        trace = zeroth * (1.0 / 3.0)
        shifted = [second[0] - trace, second[1] - trace, second[2] - trace] + list(second[3:])
        yg = times(shifted, g)
        gf = dot(g, first)
        nbar = (SURFACE_TENSION * fluid) * dot(g, yg) + beta * gf
        two_q = (2.0 * SURFACE_TENSION * fluid) * n
        bn = beta * n
        fall = nbar * n * n * n
        return [two_q * y + bn * f - fall * v for y, f, v in zip(yg, first, g)], n * gf

    def back_second(z, carry):
        zi = z + 1
        ahead_r = all_moved(a3, zi)
        ahead_t = all_moved(b3, zi)
        for r in range(ROW_TILES):
            s = link(z, r)
            own_r, own_t = a3[zi, r], b3[zi, r]
            dens, _, red, _, inv = [mac[k, zi, r] for k in range(5)]
            fluid = jnp.where(rho[zi, r] == 0.0, 0.0, 1.0)
            alpha = red * inv
            blue = dens - red
            beta = RECOLOURING_PACE * alpha * blue
            r_hat, hat = [own_r], [own_t + alpha * own_r]
            for i in range(1, 19):
                blocked = s[i] > 0.5
                r_i = jnp.where(blocked, own_r, ahead_r[i][r])
                t_i = jnp.where(blocked, own_t, ahead_t[i][r])
                r_hat.append(r_i)
                hat.append(t_i + alpha * r_i)
            t = [pop[i, zi, r] for i in range(19)]
            m = [v * (1.0 / 36.0) for v in first_moment(t)]
            u = [inv * v for v in m]
            g = tuple(g2s[k, zi, r] for k in range(3))
            gg, n = norm_parts(g)
            q = (SURFACE_TENSION * fluid) * n
            h0, h2 = weighted_even(hat[0], pair_sums(hat))
            h1 = weighted_first(hat)
            k0, k2 = weighted_even(r_hat[0], pair_sums(r_hat))
            k1 = weighted_first(r_hat)
            bars, n_gk = toward_gradient(g, fluid, h0, h2, k1, beta)
            for k in range(3):
                gbar[k, zi, r] = bars[k]
            uu = 1.5 * RELAX_RATE
            flow = [(4.5 * RELAX_RATE) * k2[j] - (uu * k0 if j < 3 else 0.0) for j in range(6)]
            surf = [k2[j] - (k0 * (1.0 / 3.0) if j < 3 else 0.0) for j in range(6)]
            alpha_bar = (
                (1.0 - RELAX_RATE) * total([a * b for a, b in zip(r_hat, t)])
                + RELAX_RATE * dens * k0
                + (3.0 * RELAX_RATE) * dot(m, k1)
                + dot(m, times(flow, u))
                + q * dot(g, times(surf, g))
            )
            alpha_bar = alpha_bar + RECOLOURING_PACE * blue * n_gk
            blue_bar = RECOLOURING_PACE * alpha * n_gk
            flow_h = [(4.5 * RELAX_RATE) * h2[j] - (uu * h0 if j < 3 else 0.0) for j in range(6)]
            xu = times(flow_h, u)
            red_bar = inv * alpha_bar - blue_bar
            dens_bar = RELAX_RATE * h0 - dot(u, xu) + blue_bar - alpha * inv * alpha_bar
            adj[19, zi, r] = red_bar
            adj[20, zi, r] = dens_bar
            for k in range(3):
                adj[21 + k, zi, r] = ((3.0 * RELAX_RATE) * h1[k] + 2.0 * xu[k]) * (1.0 / 36.0)
            for i in range(19):
                adj[i, zi, r] = hat[i]
        return carry

    lax.fori_loop(0, nz, back_second, 0)

    def back_phase(z, carry):
        zi = z + 1
        field = gradient_back([gbar.at[k] for k in range(3)], zi)
        for r in range(ROW_TILES):
            fluid = jnp.where(rho[zi, r] == 0.0, 0.0, 1.0)
            inv, psi = mac[4, zi, r], mac[5, zi, r]
            bar = field[r] * (-1.0 / 12.0)
            pbar2[zi, r] = bar
            psi_bar = fluid * bar * inv
            red_bar = adj[19, zi, r] + 2.0 * psi_bar
            dens_bar = (adj[20, zi, r] - (1.0 + psi) * psi_bar) * (1.0 / 36.0)
            push = odd_part([adj[21 + k, zi, r] for k in range(3)])
            push[:3] = [adj[21 + k, zi, r] for k in range(3)]
            keep = 1.0 - RELAX_RATE
            adj[19, zi, r] = red_bar * (1.0 / 36.0)
            adj[0, zi, r] = keep * adj[0, zi, r] + dens_bar
            for k in range(9):
                adj[2 * k + 1, zi, r] = keep * adj[2 * k + 1, zi, r] + (dens_bar + push[k])
                adj[2 * k + 2, zi, r] = keep * adj[2 * k + 2, zi, r] + (dens_bar - push[k])
        return carry

    lax.fori_loop(0, nz, back_phase, 0)

    def back_first(z, carry):
        zi = z + 1
        ahead = [None] + [moved(adj.at[i], zi, i, 1) for i in range(1, 19)]
        ahead_r = all_moved(adj.at[19], zi)
        for r in range(ROW_TILES):
            s = link(z, r)
            dens, psi = rho[zi, r], p1[zi, r]
            fluid = jnp.where(dens == 0.0, 0.0, 1.0)
            red = 0.5 * dens * (1.0 + psi)
            blue = 0.5 * dens * (1.0 - psi)
            alpha = red / (dens + (1.0 - fluid))
            beta = RECOLOURING_PACE * alpha * blue
            own = adj[19, zi, r]
            r_hat, hat = [own], [adj[0, zi, r] + alpha * own]
            for i in range(1, 19):
                blocked = s[i] > 0.5
                r_i = jnp.where(blocked, own, ahead_r[i][r])
                r_hat.append(r_i)
                hat.append(jnp.where(blocked, adj[OPPOSITE[i], zi, r], ahead[i][r]) + alpha * r_i)
            h0, h2 = weighted_even(hat[0], pair_sums(hat))
            g = tuple(g1[k, zi, r] for k in range(3))
            bars, _ = toward_gradient(g, fluid, h0, h2, weighted_first(r_hat), beta)
            for k in range(3):
                gbar[k, zi, r] = bars[k]
        return carry

    lax.fori_loop(0, nz, back_first, 0)

    for zl in range(local_z):
        zi = 1 + thick * local_z + zl
        field = gradient_back([gbar.at[k] for k in range(3)], zi)
        bar = pbar2[zi, 0] + field[0] * (-1.0 / 12.0)
        bar = jnp.where(rho[zi, 0] == 0.0, bar, 0.0)
        out_ref[zl] = bar[:, :HALF]


def pack_kernel(local_z, solid_ref, labels_ref, density_ref, wet_ref, dir_ref, map_ref, out_ref):
    for z in range(local_z):
        solid = solid_ref[z].astype(jnp.float32)
        label = labels_ref[z].astype(jnp.float32)
        fluid = 1.0 - solid
        red = density_ref[z] * label * fluid
        blue = density_ref[z] * (1.0 - label) * fluid
        psi = (red - blue) / (red + blue + solid)
        out_ref[z] = red + blue
        out_ref[local_z + z] = fluid * psi + solid * wet_ref[z]
        out_ref[2 * local_z + z] = solid * dir_ref[z]
    pixels = map_ref[...]
    lane = lax.broadcasted_iota(jnp.int32, pixels.shape, 1)
    counts = jnp.zeros(pixels.shape, jnp.int32)
    for k in range(pixels.shape[1]):
        turned = pltpu.roll(pixels, k, 1) if k else pixels
        counts = counts + (turned == lane).astype(jnp.int32)
    out_ref[3 * local_z] = counts.astype(jnp.float32)


def one_exchange(solid, labels, density, wettability, direction, pixel_map):
    local_z = solid.shape[0]
    planes, slabs = lax.axis_size("plane"), lax.axis_size("thick")
    nz = local_z * slabs
    per = 3 * local_z + 1
    vmem = pl.BlockSpec(memory_space=pltpu.VMEM)
    packed = pl.pallas_call(
        functools.partial(pack_kernel, local_z),
        out_shape=jax.ShapeDtypeStruct((per, 8, HALF), jnp.float32),
        in_specs=[vmem] * 6,
        out_specs=vmem,
    )(solid[:, 0], labels[:, 0], density[:, 0], wettability[:, 0], direction[:, 0], pixel_map[0])

    def send(array, target):
        route = []
        for b in range(planes):
            for t in range(slabs):
                to_b, to_t = target(b, t)
                route.append((b * slabs + t, (to_b % planes) * slabs + to_t))
        return lax.ppermute(array, ("plane", "thick"), route)

    beside_z = send(packed, lambda b, t: (b, 1 - t))
    beside_y = send(packed, lambda b, t: (b ^ 1, t))
    beside_zy = send(packed, lambda b, t: (b ^ 1, 1 - t))
    quad = jnp.concatenate([beside_y, beside_zy, packed, beside_z])
    above = send(quad, lambda b, t: (b + 2, t))
    below = send(quad, lambda b, t: (b - 2, t))
    corner = send(quad[: 2 * per], lambda b, t: (b + 4 if b % 2 == 0 else b - 4, t))

    def field(*lead):
        return pltpu.VMEM(lead + (ROW_TILES, 8, WIDE), jnp.float32)

    padded = nz + 2
    return pl.pallas_call(
        functools.partial(main_kernel, nz, local_z),
        out_shape=(
            jax.ShapeDtypeStruct((local_z, 8, HALF), jnp.float32),
            jax.ShapeDtypeStruct((8, HALF), jnp.float32),
        ),
        in_specs=[vmem] * 5,
        out_specs=(vmem, vmem),
        scratch_shapes=[
            field(padded), field(padded), field(padded), field(),
            field(18, nz), field(9, padded), field(9, padded), field(36, padded),
            field(19, padded), field(19, padded), field(6, padded),
            field(padded), field(padded), field(3, padded), field(3, padded),
            field(padded), field(padded), field(), field(24, padded), field(3, padded),
            field(padded),
        ],
        compiler_params=pltpu.CompilerParams(vmem_limit_bytes=56 * 1024 * 1024),
    )(quad, above, below, corner, pixel_map[0])


def fits_one_exchange(mesh, solid):
    return mesh.shape["plane"] == 2 * NBX and mesh.shape["thick"] == 2 and solid.shape[2:] == (8, HALF)


def solution(mesh):
    specs = (P("thick", "plane", None, None),) * 5 + (P("plane", None, None),)
    out_specs = (P("thick", "plane", None, None), P("plane", None, None))

    def program(solid, *rest):
        def with_bricks(*blocks):
            curvature, readings = one_exchange(*blocks)
            return curvature[:, None], readings[None]

        body = with_bricks if fits_one_exchange(mesh, solid) else per_device
        return jax.shard_map(
            body, mesh=mesh, in_specs=specs, out_specs=out_specs, check_vma=False
        )(solid, *rest)

    return program
```

```python
import functools

import jax
import jax.numpy as jnp
import numpy as np
from jax import lax
from jax.experimental import pallas as pl
from jax.experimental.pallas import tpu as pltpu
from jax.sharding import PartitionSpec as P

NBX = 8
STEPS = 2


VELOCITIES = np.array(
    [
        [0, 0, 0],
        [1, 0, 0],
        [-1, 0, 0],
        [0, 1, 0],
        [0, -1, 0],
        [0, 0, 1],
        [0, 0, -1],
        [1, 1, 0],
        [-1, -1, 0],
        [1, -1, 0],
        [-1, 1, 0],
        [1, 0, 1],
        [-1, 0, -1],
        [1, 0, -1],
        [-1, 0, 1],
        [0, 1, 1],
        [0, -1, -1],
        [0, 1, -1],
        [0, -1, 1],
    ]
)
WEIGHTS = np.array([1.0 / 3.0] + [1.0 / 18.0] * 6 + [1.0 / 36.0] * 12)
OPPOSITE = [int(np.argmin(np.abs(VELOCITIES + lattice_vec).sum(1))) for lattice_vec in VELOCITIES]
RELAX_RATE = 1.25
SURFACE_TENSION = 0.2
RECOLOURING_PACE = 0.7


def shifted(array, axis, by):
    devices = lax.axis_size(axis)
    pairs = [(i, i + by) for i in range(devices) if 0 <= i + by < devices]
    return lax.ppermute(array, axis, pairs)


def from_behind(block, axis, distance):
    devices = range(lax.axis_size(axis))
    route = [((i - distance) % len(devices), i) for i in devices]
    return lax.ppermute(block, axis, route)


def weights_like(array):
    return jnp.asarray(WEIGHTS, jnp.float32).reshape((19,) + (1,) * (array.ndim - 1))


def collide(red_pop, blue_pop, gradient, solid_cell):
    lattice_vel = jnp.asarray(VELOCITIES, jnp.float32)
    weight_column_vec = weights_like(red_pop)
    red_density_total = jnp.sum(red_pop, 0)
    blue_density_total = jnp.sum(blue_pop, 0)
    density = red_density_total + blue_density_total
    reciprocal_value = 1.0 / (density + solid_cell)
    total_pop = red_pop + blue_pop
    velocity = (
        jnp.einsum("qd,q...->d...", lattice_vel, total_pop, precision=lax.Precision.HIGHEST)
        * reciprocal_value
    )
    projected = jnp.einsum("qd,d...->q...", lattice_vel, velocity, precision=lax.Precision.HIGHEST)
    speed_sq = jnp.sum(velocity * velocity, 0)
    equilibrium = (
        weight_column_vec
        * density
        * (1.0 + 3.0 * projected + 4.5 * projected * projected - 1.5 * speed_sq)
    )
    relaxed_populations = total_pop + RELAX_RATE * (equilibrium - total_pop)
    along_gradient_dir = jnp.einsum(
        "qd,d...->q...", lattice_vel, gradient, precision=lax.Precision.HIGHEST
    )
    grad_sq = jnp.sum(gradient * gradient, 0)
    norm_scale_factor = 1.0 / jnp.sqrt(1.0 + grad_sq)
    relaxed_populations = (
        relaxed_populations
        + SURFACE_TENSION
        * weight_column_vec
        * (along_gradient_dir * along_gradient_dir - grad_sq / 3.0)
        * norm_scale_factor
    )
    red_output_pop = (
        red_density_total * reciprocal_value * relaxed_populations
        + RECOLOURING_PACE
        * red_density_total
        * blue_density_total
        * reciprocal_value
        * weight_column_vec
        * along_gradient_dir
        * norm_scale_factor
    )
    return (red_output_pop, relaxed_populations - red_output_pop)


def phase_of(red_pop, blue_pop, solid_cell):
    red_density_total = jnp.sum(red_pop, 0)
    blue_density_total = jnp.sum(blue_pop, 0)
    return (red_density_total - blue_density_total) / (
        red_density_total + blue_density_total + solid_cell
    )


def pull_from(padded, offset, extent):
    shift_z, shift_x, shift_y = (int(offset[0]), int(offset[1]), int(offset[2]))
    return padded[
        ...,
        1 - shift_z : 1 - shift_z + extent[0],
        1 - shift_x : 1 - shift_x + extent[1],
        1 - shift_y : 1 - shift_y + extent[2],
    ]


def gradient_of(padded, extent):
    components = [0.0, 0.0, 0.0]
    for number in range(1, 19):
        lattice_vec = VELOCITIES[number]
        pulled = pull_from(padded, -lattice_vec, extent)
        for axis_num in range(3):
            if lattice_vec[axis_num] != 0:
                components[axis_num] = (
                    components[axis_num]
                    + 3.0 * WEIGHTS[number] * float(lattice_vec[axis_num]) * pulled
                )
    return jnp.stack(components)


def spread_back(padded_bar, extent):
    total_bar = 0.0
    for number in range(1, 19):
        lattice_vec = VELOCITIES[number]
        for axis_num in range(3):
            if lattice_vec[axis_num] != 0:
                total_bar = total_bar + 3.0 * WEIGHTS[number] * float(
                    lattice_vec[axis_num]
                ) * pull_from(padded_bar[axis_num], lattice_vec, extent)
    return total_bar


def stream(padded_pop, local_pop, padded_fluid, fluid_cell, extent):
    outgoing = []
    for number in range(19):
        lattice_vec = VELOCITIES[number]
        source_fluid = pull_from(padded_fluid, lattice_vec, extent)
        arrived = pull_from(padded_pop[number], lattice_vec, extent)
        outgoing.append(
            fluid_cell
            * (source_fluid * arrived + (1.0 - source_fluid) * local_pop[OPPOSITE[number]])
        )
    return jnp.stack(outgoing)


def unstream(padded_bar, local_bar, padded_fluid, fluid_cell, extent):
    incoming = []
    for number in range(19):
        lattice_vec = VELOCITIES[number]
        ahead_fluid = pull_from(padded_fluid, -lattice_vec, extent)
        ahead_bar = pull_from(padded_bar[number], -lattice_vec, extent)
        incoming.append(fluid_cell * ahead_bar + (1.0 - ahead_fluid) * local_bar[OPPOSITE[number]])
    return jnp.stack(incoming)


def fill_border(received, chosen, channels):
    if len(chosen) == channels:
        return received
    return (
        jnp.zeros((channels,) + received.shape[1:], received.dtype)
        .at[np.array(chosen)]
        .set(received)
    )


def grow(stacked, axis_dim, chosen_low, chosen_high, sender):
    length = stacked.shape[axis_dim]
    channels = stacked.shape[0]
    borders = []
    for toward in (1, -1):
        chosen = chosen_low if toward == 1 else chosen_high
        source = length - 1 if toward == 1 else 0
        outer_layer = lax.slice_in_dim(stacked, source, source + 1, axis=axis_dim)
        if len(chosen) < channels:
            outer_layer = outer_layer[np.array(chosen)]
        borders.append(fill_border(sender(outer_layer, toward), chosen, channels))
    return jnp.concatenate([borders[0], stacked, borders[1]], axis_dim)


def per_device(solid, labels, density, wettability, direction, pixel_map):
    solid_cell = solid[:, 0].astype(jnp.float32)
    fluid_cell = 1.0 - solid_cell
    label_cell = labels[:, 0].astype(jnp.float32)
    density_cell = density[:, 0]
    wetting = wettability[:, 0]
    tangent = direction[:, 0]
    column_map = pixel_map[0]
    extent = solid_cell.shape
    bricks_y = lax.axis_size("plane") // NBX

    def extend(stacked):
        channels = stacked.shape[0]

        def chosen_for():
            return list(range(channels))

        stacked = grow(
            stacked,
            1,
            chosen_for(),
            chosen_for(),
            lambda outgoing, toward: shifted(outgoing, "thick", toward),
        )
        stacked = grow(
            stacked,
            2,
            chosen_for(),
            chosen_for(),
            lambda outgoing, toward: from_behind(outgoing, "plane", toward * bricks_y),
        )
        stacked = grow(
            stacked,
            3,
            chosen_for(),
            chosen_for(),
            lambda outgoing, toward: from_behind(outgoing, "plane", toward),
        )
        return stacked

    def phase_pair(red_in, blue_in):
        return phase_of(red_in, blue_in, solid_cell)

    def collide_local(red_in, blue_in, gradient):
        return collide(red_in, blue_in, gradient, solid_cell)

    padded_fluid = extend(fluid_cell[None])[0]
    weight_column_vec = weights_like(solid_cell[None])
    red_pop = weight_column_vec * (density_cell * label_cell * fluid_cell)[None]
    blue_pop = weight_column_vec * (density_cell * (1.0 - label_cell) * fluid_cell)[None]
    red_tan = jnp.zeros_like(red_pop)
    blue_tan = jnp.zeros_like(blue_pop)
    checkpoints = []
    for number in range(STEPS):
        phase_val, phase_tan = jax.jvp(phase_pair, (red_pop, blue_pop), (red_tan, blue_tan))
        phase_field = fluid_cell * phase_val + solid_cell * wetting
        field_tan = fluid_cell * phase_tan + solid_cell * tangent
        padded = extend(jnp.stack([phase_field, field_tan]))
        gradient = gradient_of(padded[0], extent)
        gradient_tan = gradient_of(padded[1], extent)
        checkpoints.append((red_pop, blue_pop, gradient))
        (red_post, blue_post), (red_dot, blue_dot) = jax.jvp(
            collide_local, (red_pop, blue_pop, gradient), (red_tan, blue_tan, gradient_tan)
        )
        posted = jnp.concatenate([red_post, blue_post, red_dot, blue_dot])
        moved = extend(posted)
        red_pop, blue_pop, red_tan, blue_tan = [
            stream(
                moved[19 * group : 19 * group + 19],
                posted[19 * group : 19 * group + 19],
                padded_fluid,
                fluid_cell,
                extent,
            )
            for group in range(4)
        ]
    _, phase_tan = jax.jvp(phase_pair, (red_pop, blue_pop), (red_tan, blue_tan))
    partial_sum = jnp.sum(fluid_cell * phase_tan, 0)
    column_sum = lax.psum(partial_sum, "thick")
    found = jnp.take_along_axis(column_sum, column_map, axis=1)
    row_ids = jnp.arange(column_map.shape[0])[:, None]
    seeded = jnp.zeros_like(column_sum).at[row_ids, column_map].add(found)
    _, phase_back = jax.vjp(phase_pair, red_pop, blue_pop)
    red_bar, blue_bar = phase_back(fluid_cell * seeded[None])
    wetting_bar = jnp.zeros_like(wetting)
    for number in reversed(range(STEPS)):
        red_saved, blue_saved, gradient = checkpoints[number]
        outgoing_bar = jnp.concatenate([red_bar, blue_bar]) * fluid_cell
        padded = extend(outgoing_bar)
        red_pre = unstream(padded[:19], outgoing_bar[:19], padded_fluid, fluid_cell, extent)
        blue_pre = unstream(padded[19:], outgoing_bar[19:], padded_fluid, fluid_cell, extent)
        _, collide_back = jax.vjp(collide_local, red_saved, blue_saved, gradient)
        red_bar, blue_bar, gradient_bar = collide_back((red_pre, blue_pre))
        padded_bar = extend(gradient_bar)
        field_bar = spread_back(padded_bar, extent)
        wetting_bar = wetting_bar + solid_cell * field_bar
        if number > 0:
            _, phase_back = jax.vjp(phase_pair, red_saved, blue_saved)
            extra_red, extra_blue = phase_back(fluid_cell * field_bar)
            red_bar = red_bar + extra_red
            blue_bar = blue_bar + extra_blue
    return (wetting_bar[:, None], found[None])


HALF = 128
WIDE = 256
ROW_TILES = 3
Z_AXIS, X_AXIS, Y_AXIS = range(3)
EDGES = [(0, 1, 1), (0, 1, -1), (0, 2, 1), (0, 2, -1), (1, 2, 1), (1, 2, -1)]
CZ = [int(v[0]) for v in VELOCITIES]
CX = [int(v[1]) for v in VELOCITIES]
CY = [int(v[2]) for v in VELOCITIES]
GROUPS = [(gx, gy) for gx in (-1, 0, 1) for gy in (-1, 0, 1)]


def roll_rows(tile, by):
    return pltpu.roll(tile, by % tile.shape[0], 0)


def roll_lanes(tile, by):
    return pltpu.roll(tile, by % tile.shape[1], 1)


def x_shift(tiles, dx):
    row = lax.broadcasted_iota(jnp.int32, tiles[0].shape, 0)
    out = []
    for r in range(ROW_TILES):
        beyond = tiles[(r + dx) % ROW_TILES]
        edge = 0 if dx == 1 else 7
        out.append(roll_rows(jnp.where(row == edge, beyond, tiles[r]), -dx))
    return out


def y_shift(tiles, dy):
    return [roll_lanes(tile, -dy) for tile in tiles]


def each(function, *lists):
    return [function(*items) for items in zip(*lists)]


def add(a, b):
    return a + b


def sub(a, b):
    return a - b


def both_ways(shift, tiles):
    return shift(tiles, 1), shift(tiles, -1)


def plane(ref, zi):
    return [ref[zi, r] for r in range(ROW_TILES)]


def gradient_tiles(ref, zi):
    mid, up, down = plane(ref, zi), plane(ref, zi + 1), plane(ref, zi - 1)
    two = each(lambda m, u, d: 2.0 * m + u + d, mid, up, down)
    slope = each(sub, up, down)
    y_sum = each(add, *both_ways(y_shift, mid))
    x_sum = each(add, *both_ways(x_shift, mid))
    along_x = each(sub, *both_ways(x_shift, each(add, two, y_sum)))
    along_y = each(sub, *both_ways(y_shift, each(add, two, x_sum)))
    sx = each(add, *both_ways(x_shift, slope))
    sy = each(add, *both_ways(y_shift, slope))
    along_z = each(lambda s, a, b: 2.0 * s + a + b, slope, sx, sy)
    return along_z, along_x, along_y


def gradient_back(refs, zi):
    gz, gx, gy = refs
    mid, up, down = plane(gx, zi), plane(gx, zi + 1), plane(gx, zi - 1)
    y_sum = each(add, *both_ways(y_shift, mid))
    total = each(lambda m, u, d, s: 2.0 * m + u + d + s, mid, up, down, y_sum)
    result = each(sub, *both_ways(x_shift, total))
    mid, up, down = plane(gy, zi), plane(gy, zi + 1), plane(gy, zi - 1)
    x_sum = each(add, *both_ways(x_shift, mid))
    total = each(lambda m, u, d, s: 2.0 * m + u + d + s, mid, up, down, x_sum)
    result = each(add, result, each(sub, *both_ways(y_shift, total)))
    slope = each(sub, plane(gz, zi + 1), plane(gz, zi - 1))
    sx = each(add, *both_ways(x_shift, slope))
    sy = each(add, *both_ways(y_shift, slope))
    return each(lambda a, s, b, c: a + 2.0 * s + b + c, result, slope, sx, sy)


def even_part(base, quad):
    zz, xx, yy, zx, zy, xy = quad
    out = [2.0 * (base + zz), 2.0 * (base + xx), 2.0 * (base + yy)]
    for diagonal, cross in ((zz + xx, zx), (zz + yy, zy), (xx + yy, xy)):
        flat = base + diagonal
        out += [flat + cross, flat - cross]
    return out


def odd_part(vector):
    z, x, y = vector
    return [2.0 * z, 2.0 * x, 2.0 * y, z + x, z - x, z + y, z - y, x + y, x - y]


def squares(vector):
    z, x, y = vector
    return [z * z, x * x, y * y, 2.0 * (z * x), 2.0 * (z * y), 2.0 * (x * y)]


def squares_dot(a, b):
    az, ax, ay = a
    bz, bx, by = b
    return [
        2.0 * (az * bz),
        2.0 * (ax * bx),
        2.0 * (ay * by),
        2.0 * (az * bx + ax * bz),
        2.0 * (az * by + ay * bz),
        2.0 * (ax * by + ay * bx),
    ]


def dot(a, b):
    return a[0] * b[0] + a[1] * b[1] + a[2] * b[2]


def first_moment(values):
    d = [values[2 * p + 1] - values[2 * p + 2] for p in range(9)]
    return (
        d[0] + (d[3] + d[4]) + (d[5] + d[6]),
        d[1] + (d[3] - d[4]) + (d[7] + d[8]),
        d[2] + (d[5] - d[6]) + (d[7] - d[8]),
    )


def weighted_first(values):
    d = [values[2 * p + 1] - values[2 * p + 2] for p in range(9)]
    return (
        2.0 * d[0] + (d[3] + d[4]) + (d[5] + d[6]),
        2.0 * d[1] + (d[3] - d[4]) + (d[7] + d[8]),
        2.0 * d[2] + (d[5] - d[6]) + (d[7] - d[8]),
    )


def weighted_even(rest, pairs):
    axis = [2.0 * pairs[0], 2.0 * pairs[1], 2.0 * pairs[2]]
    zx, zy, xy = pairs[3] + pairs[4], pairs[5] + pairs[6], pairs[7] + pairs[8]
    second = [
        axis[0] + zx + zy,
        axis[1] + zx + xy,
        axis[2] + zy + xy,
        pairs[3] - pairs[4],
        pairs[5] - pairs[6],
        pairs[7] - pairs[8],
    ]
    zeroth = 12.0 * rest + axis[0] + axis[1] + axis[2] + zx + zy + xy
    return zeroth, second


def pair_sums(values):
    return [values[2 * p + 1] + values[2 * p + 2] for p in range(9)]


def times(matrix, vector):
    zz, xx, yy, zx, zy, xy = matrix
    z, x, y = vector
    return (zz * z + zx * x + zy * y, zx * z + xx * x + xy * y, zy * z + xy * x + yy * y)


def total(values):
    values = list(values)
    while len(values) > 1:
        values = [
            values[k] + values[k + 1] if k + 1 < len(values) else values[k]
            for k in range(0, len(values), 2)
        ]
    return values[0]


def norm_parts(g):
    g2 = dot(g, g)
    n = lax.rsqrt(1.0 + g2)
    return g2, n


def scatter_groups(acc, zi, r, values, stay):
    for k, (gx, gy) in enumerate(GROUPS):
        here = [i for i in range(1, 19) if (CX[i], CY[i]) == (gx, gy)]
        level = {CZ[i]: values[i] for i in here}
        if (gx, gy) == (0, 0):
            level[0] = values[0] + stay
        if 1 not in level:
            acc[k, zi, r] = level[0]
            continue
        acc[k, zi + 1, r] = level[1]
        acc[k, zi, r] = acc[k, zi, r] + level[0]
        acc[k, zi - 1, r] = acc[k, zi - 1, r] + level[-1]


def gathered_sum(acc, zi):
    by_y = []
    for gy in (-1, 0, 1):
        parts = [plane(acc.at[GROUPS.index((0, gy))], zi)]
        for gx in (-1, 1):
            parts.append(x_shift(plane(acc.at[GROUPS.index((gx, gy))], zi), -gx))
        by_y.append(each(lambda *a: total(a), *parts))
    return each(
        lambda a, b, c: a + b + c, y_shift(by_y[0], 1), by_y[1], y_shift(by_y[2], -1)
    )


def moved(ref, zi, i, sign):
    tiles = plane(ref, zi + sign * CZ[i])
    if CX[i]:
        tiles = x_shift(tiles, sign * CX[i])
    if CY[i]:
        tiles = y_shift(tiles, sign * CY[i])
    return tiles


def all_moved(ref, zi):
    out = [None] * 19
    for cz in (-1, 0, 1):
        base = plane(ref, zi + cz)
        rows = {0: base, 1: x_shift(base, 1), -1: x_shift(base, -1)}
        for i in range(19):
            if CZ[i] == cz:
                tiles = rows[CX[i]]
                out[i] = y_shift(tiles, CY[i]) if CY[i] else tiles
    return out


def main_kernel(nz, local_z, q_ref, qm_ref, qp_ref, sl_ref, map_ref, out_ref, read_ref,
                rho, p1, dp1, cnt, blk, t_st, dt_st, acc, pop, dpop, mac, p2, dp2, g1, g2s,
                a3, b3, col, adj, gbar, pbar2):
    thick = lax.axis_index("thick")
    even = lax.rem(lax.axis_index("plane"), 2) == 0
    per = 3 * local_z + 1
    f32 = jnp.float32
    zero_tile = jnp.zeros((8, WIDE), f32)

    for ref in (rho, p1, dp1, p2, dp2):
        for r in range(ROW_TILES):
            ref[0, r] = zero_tile
            ref[nz + 1, r] = zero_tile
    for k in range(3):
        for r in range(ROW_TILES):
            gbar[k, 0, r] = zero_tile
            gbar[k, nz + 1, r] = zero_tile
    for k in range(36):
        for r in range(ROW_TILES):
            acc[k, 1, r] = zero_tile
    lane = lax.broadcasted_iota(jnp.int32, (8, HALF), 1)
    low = lane < HALF // 2

    def sides(r, k, ks):
        if r == 0:
            middle = q_ref[2 * per + k]
            right = jnp.where(even, q_ref[k], qp_ref[k])
            left = jnp.where(even, qm_ref[k], q_ref[k])
        elif r == 1:
            middle = qp_ref[2 * per + k]
            right = jnp.where(even, qp_ref[k], sl_ref[ks])
            left = jnp.where(even, q_ref[k], qp_ref[k])
        else:
            middle = qm_ref[2 * per + k]
            right = jnp.where(even, qm_ref[k], q_ref[k])
            left = jnp.where(even, sl_ref[ks], qm_ref[k])
        return middle, jnp.where(low, right, left)

    for part in range(2):
        slab = thick if part == 0 else 1 - thick
        for zl in range(local_z):
            zi = 1 + slab * local_z + zl
            for r in range(ROW_TILES):
                for which, ref in enumerate((rho, p1, dp1)):
                    k = which * local_z + zl + part * per
                    middle, side = sides(r, k, k)
                    ref[zi, r, :, :HALF] = middle
                    ref[zi, r, :, HALF:] = side
    for r in range(ROW_TILES):
        middle, side = sides(r, per - 1, per - 1)
        cnt[r, :, :HALF] = middle
        cnt[r, :, HALF:] = side

    def links(z, carry):
        zi = z + 1
        here = each(lambda v: jnp.where(v == 0.0, 1.0, 0.0), plane(rho, zi))
        for cz in (-1, 0, 1):
            base = each(lambda v: jnp.where(v == 0.0, 1.0, 0.0), plane(rho, zi + cz))
            rows = {0: base, 1: x_shift(base, 1), -1: x_shift(base, -1)}
            for i in range(1, 19):
                if CZ[i] == cz:
                    tiles = rows[CX[i]]
                    tiles = y_shift(tiles, CY[i]) if CY[i] else tiles
                    for r in range(ROW_TILES):
                        blk[i - 1, z, r] = jnp.maximum(tiles[r], here[r])
        return carry

    lax.fori_loop(0, nz, links, 0, unroll=True)

    def link(z, r):
        return [None] + [blk[i, z, r] for i in range(18)]

    def collide_first(z, carry):
        zi = z + 1
        grads = gradient_tiles(p1, zi)
        dgrads = gradient_tiles(dp1, zi)
        for r in range(ROW_TILES):
            dens, psi = rho[zi, r], p1[zi, r]
            fluid = jnp.where(dens == 0.0, 0.0, 1.0)
            red = 0.5 * dens * (1.0 + psi)
            blue = 0.5 * dens * (1.0 - psi)
            alpha = red / (dens + (1.0 - fluid))
            beta = RECOLOURING_PACE * alpha * blue
            g = tuple(a[r] * (1.0 / 12.0) for a in grads)
            dg = tuple(a[r] * (1.0 / 12.0) for a in dgrads)
            gg, n = norm_parts(g)
            gdg = dot(g, dg)
            n2g = n * n * gdg
            dn = -n * n2g
            q = (SURFACE_TENSION * fluid) * n
            dq = -q * n2g
            for k in range(3):
                g1[k, zi, r] = g[k]
            sq, dsq = squares(g), squares_dot(g, dg)
            base = dens - q * gg * (1.0 / 3.0)
            dbase = (dq * gg + 2.0 * q * gdg) * (-1.0 / 3.0)
            ev = even_part(base, [q * v for v in sq])
            dev = even_part(dbase, [dq * v + q * d for v, d in zip(sq, dsq)])
            bn, bdn = beta * n, beta * dn
            od = odd_part([bn * v for v in g])
            dod = odd_part([bdn * v + bn * d for v, d in zip(g, dg)])
            for k in range(9):
                t_st[k, zi, r] = ev[k]
                dt_st[k, zi, r] = dev[k]
            pop[0, zi, r] = 12.0 * base
            dpop[0, zi, r] = 12.0 * dbase
            s = link(z, r)
            for first, rest, evens, odds in (
                (0, 12.0 * base, ev, od), (9, 12.0 * dbase, dev, dod)
            ):
                scaled = [alpha * v for v in evens]
                values = [alpha * rest]
                stay = []
                for k in range(9):
                    values += [scaled[k] + odds[k], scaled[k] - odds[k]]
                    stay += [s[2 * k + 1] * values[-2], s[2 * k + 2] * values[-1]]
                scatter_groups(acc.at[pl.ds(first, 9)], zi, r, values, total(stay))
        return carry

    lax.fori_loop(0, nz, collide_first, 0, unroll=True)

    def run_first(z, carry):
        zi = z + 1
        for ref, store in ((t_st, pop), (dt_st, dpop)):
            for i in range(1, 19):
                k = (i - 1) // 2
                arrived = moved(ref.at[k], zi, i, -1)
                for r in range(ROW_TILES):
                    blocked = blk[OPPOSITE[i] - 1, z, r] > 0.5
                    store[i, zi, r] = jnp.where(blocked, ref[k, zi, r], arrived[r])
        red_sum = gathered_sum(acc.at[pl.ds(0, 9)], zi)
        dred_sum = gathered_sum(acc.at[pl.ds(9, 9)], zi)
        for r in range(ROW_TILES):
            fluid = jnp.where(rho[zi, r] == 0.0, 0.0, 1.0)
            is_fluid = fluid > 0.5
            dens = total([pop[i, zi, r] for i in range(19)]) * (1.0 / 36.0)
            ddens = total([dpop[i, zi, r] for i in range(19)]) * (1.0 / 36.0)
            red = red_sum[r] * fluid * (1.0 / 36.0)
            dred = dred_sum[r] * fluid * (1.0 / 36.0)
            inv = 1.0 / (dens + (1.0 - fluid))
            psi = (2.0 * red - dens) * inv
            dpsi = (2.0 * dred - (1.0 + psi) * ddens) * inv
            for k, v in enumerate((dens, ddens, red, dred, inv, psi)):
                mac[k, zi, r] = v
            p2[zi, r] = jnp.where(is_fluid, psi, p1[zi, r])
            dp2[zi, r] = jnp.where(is_fluid, dpsi, dp1[zi, r])
        return carry

    lax.fori_loop(0, nz, run_first, 0, unroll=True)

    for k in range(36):
        for r in range(ROW_TILES):
            acc[k, 1, r] = zero_tile

    def collide_second(z, carry):
        zi = z + 1
        grads = gradient_tiles(p2, zi)
        dgrads = gradient_tiles(dp2, zi)
        for r in range(ROW_TILES):
            dens, ddens, red, dred, inv = [mac[k, zi, r] for k in range(5)]
            fluid = jnp.where(rho[zi, r] == 0.0, 0.0, 1.0)
            t = [pop[i, zi, r] for i in range(19)]
            dt = [dpop[i, zi, r] for i in range(19)]
            m = [v * (1.0 / 36.0) for v in first_moment(t)]
            dm = [v * (1.0 / 36.0) for v in first_moment(dt)]
            u = [inv * v for v in m]
            shrink = inv * ddens
            du = [inv * b - shrink * a for a, b in zip(u, dm)]
            g = tuple(a[r] * (1.0 / 12.0) for a in grads)
            dg = tuple(a[r] * (1.0 / 12.0) for a in dgrads)
            gg, n = norm_parts(g)
            gdg = dot(g, dg)
            n2g = n * n * gdg
            dn = -n * n2g
            q = (SURFACE_TENSION * fluid) * n
            dq = -q * n2g
            for k in range(3):
                g2s[k, zi, r] = g[k]
            base = RELAX_RATE * dens - (1.5 * RELAX_RATE) * dot(m, u) - q * gg * (1.0 / 3.0)
            dbase = (
                RELAX_RATE * ddens
                - (1.5 * RELAX_RATE) * (dot(dm, u) + dot(m, du))
                + (dq * gg + 2.0 * q * gdg) * (-1.0 / 3.0)
            )
            lin = odd_part([(3.0 * RELAX_RATE) * v for v in m])
            dlin = odd_part([(3.0 * RELAX_RATE) * v for v in dm])
            mq = [(4.5 * RELAX_RATE) * v for v in m]
            dmq = [(4.5 * RELAX_RATE) * v for v in dm]
            order = ((0, 0), (1, 1), (2, 2), (0, 1), (0, 2), (1, 2))
            sq, dsq = squares(g), squares_dot(g, dg)
            quad, dquad = [], []
            for k, (a, b) in enumerate(order):
                twice = 1.0 if a == b else 2.0
                flow = mq[a] * u[b]
                dflow = dmq[a] * u[b] + mq[a] * du[b]
                if a != b:
                    flow = 2.0 * flow
                    dflow = 2.0 * dflow
                quad.append(flow + q * sq[k])
                dquad.append(dflow + dq * sq[k] + q * dsq[k])
            ev, dev = even_part(base, quad), even_part(dbase, dquad)
            keep = 1.0 - RELAX_RATE
            after, dafter = [keep * t[0] + 12.0 * base], [keep * dt[0] + 12.0 * dbase]
            for k in range(9):
                after += [keep * t[2 * k + 1] + (ev[k] + lin[k]), keep * t[2 * k + 2] + (ev[k] - lin[k])]
                dafter += [
                    keep * dt[2 * k + 1] + (dev[k] + dlin[k]),
                    keep * dt[2 * k + 2] + (dev[k] - dlin[k]),
                ]
            alpha = red * inv
            dalpha = dred * inv - alpha * shrink
            blue, dblue = dens - red, ddens - dred
            beta = RECOLOURING_PACE * alpha * blue
            dbeta = RECOLOURING_PACE * (dalpha * blue + alpha * dblue)
            bn = beta * n
            dbn = dbeta * n + beta * dn
            od = odd_part([bn * v for v in g])
            dod = odd_part([dbn * v + bn * d for v, d in zip(g, dg)])
            reds, dreds = [alpha * after[0]], [dalpha * after[0] + alpha * dafter[0]]
            for i in range(1, 19):
                k = (i - 1) // 2
                side = od[k] if i % 2 else -od[k]
                dside = dod[k] if i % 2 else -dod[k]
                reds.append(alpha * after[i] + side)
                dreds.append(dalpha * after[i] + alpha * dafter[i] + dside)
            s = link(z, r)
            for k, values in enumerate((reds, dreds, after, dafter)):
                stay = total([s[i] * values[i] for i in range(1, 19)])
                scatter_groups(acc.at[pl.ds(9 * k, 9)], zi, r, values, stay)
        return carry

    lax.fori_loop(0, nz, collide_second, 0, unroll=True)

    for r in range(ROW_TILES):
        col[r] = zero_tile

    def final_phase(z, carry):
        zi = z + 1
        red_s, dred_s, dens_s, ddens_s = [gathered_sum(acc.at[pl.ds(9 * k, 9)], zi) for k in range(4)]
        for r in range(ROW_TILES):
            fluid = jnp.where(rho[zi, r] == 0.0, 0.0, 1.0)
            scale = fluid * (1.0 / 36.0)
            dens = dens_s[r] * scale
            inv = 1.0 / (dens + (1.0 - fluid))
            psi = (2.0 * (red_s[r] * scale) - dens) * inv
            a = 2.0 * (scale * inv)
            b = -(scale * inv) * (1.0 + psi)
            a3[zi, r] = a
            b3[zi, r] = b
            col[r] = col[r] + (a * dred_s[r] + b * ddens_s[r])
        return carry

    lax.fori_loop(0, nz, final_phase, 0, unroll=True)
    read_ref[...] = jnp.take_along_axis(col[0, :, :HALF], map_ref[...], axis=1)

    def seed(z, carry):
        zi = z + 1
        for r in range(ROW_TILES):
            column = col[r] * cnt[r]
            a3[zi, r] = a3[zi, r] * column
            b3[zi, r] = b3[zi, r] * column
        return carry

    lax.fori_loop(0, nz, seed, 0, unroll=True)

    def toward_gradient(g, fluid, zeroth, second, first, beta):
        gg, n = norm_parts(g)
        trace = zeroth * (1.0 / 3.0)
        shifted = [second[0] - trace, second[1] - trace, second[2] - trace] + list(second[3:])
        yg = times(shifted, g)
        gf = dot(g, first)
        nbar = (SURFACE_TENSION * fluid) * dot(g, yg) + beta * gf
        two_q = (2.0 * SURFACE_TENSION * fluid) * n
        bn = beta * n
        fall = nbar * n * n * n
        return [two_q * y + bn * f - fall * v for y, f, v in zip(yg, first, g)], n * gf

    def back_second(z, carry):
        zi = z + 1
        ahead_r = all_moved(a3, zi)
        ahead_t = all_moved(b3, zi)
        for r in range(ROW_TILES):
            s = link(z, r)
            own_r, own_t = a3[zi, r], b3[zi, r]
            dens, _, red, _, inv = [mac[k, zi, r] for k in range(5)]
            fluid = jnp.where(rho[zi, r] == 0.0, 0.0, 1.0)
            alpha = red * inv
            blue = dens - red
            beta = RECOLOURING_PACE * alpha * blue
            r_hat, hat = [own_r], [own_t + alpha * own_r]
            for i in range(1, 19):
                blocked = s[i] > 0.5
                r_i = jnp.where(blocked, own_r, ahead_r[i][r])
                t_i = jnp.where(blocked, own_t, ahead_t[i][r])
                r_hat.append(r_i)
                hat.append(t_i + alpha * r_i)
            t = [pop[i, zi, r] for i in range(19)]
            m = [v * (1.0 / 36.0) for v in first_moment(t)]
            u = [inv * v for v in m]
            g = tuple(g2s[k, zi, r] for k in range(3))
            gg, n = norm_parts(g)
            q = (SURFACE_TENSION * fluid) * n
            h0, h2 = weighted_even(hat[0], pair_sums(hat))
            h1 = weighted_first(hat)
            k0, k2 = weighted_even(r_hat[0], pair_sums(r_hat))
            k1 = weighted_first(r_hat)
            bars, n_gk = toward_gradient(g, fluid, h0, h2, k1, beta)
            for k in range(3):
                gbar[k, zi, r] = bars[k]
            uu = 1.5 * RELAX_RATE
            flow = [(4.5 * RELAX_RATE) * k2[j] - (uu * k0 if j < 3 else 0.0) for j in range(6)]
            surf = [k2[j] - (k0 * (1.0 / 3.0) if j < 3 else 0.0) for j in range(6)]
            alpha_bar = (
                (1.0 - RELAX_RATE) * total([a * b for a, b in zip(r_hat, t)])
                + RELAX_RATE * dens * k0
                + (3.0 * RELAX_RATE) * dot(m, k1)
                + dot(m, times(flow, u))
                + q * dot(g, times(surf, g))
            )
            alpha_bar = alpha_bar + RECOLOURING_PACE * blue * n_gk
            blue_bar = RECOLOURING_PACE * alpha * n_gk
            flow_h = [(4.5 * RELAX_RATE) * h2[j] - (uu * h0 if j < 3 else 0.0) for j in range(6)]
            xu = times(flow_h, u)
            red_bar = inv * alpha_bar - blue_bar
            dens_bar = RELAX_RATE * h0 - dot(u, xu) + blue_bar - alpha * inv * alpha_bar
            adj[19, zi, r] = red_bar
            adj[20, zi, r] = dens_bar
            for k in range(3):
                adj[21 + k, zi, r] = ((3.0 * RELAX_RATE) * h1[k] + 2.0 * xu[k]) * (1.0 / 36.0)
            for i in range(19):
                adj[i, zi, r] = hat[i]
        return carry

    lax.fori_loop(0, nz, back_second, 0, unroll=True)

    def back_phase(z, carry):
        zi = z + 1
        field = gradient_back([gbar.at[k] for k in range(3)], zi)
        for r in range(ROW_TILES):
            fluid = jnp.where(rho[zi, r] == 0.0, 0.0, 1.0)
            inv, psi = mac[4, zi, r], mac[5, zi, r]
            bar = field[r] * (-1.0 / 12.0)
            pbar2[zi, r] = bar
            psi_bar = fluid * bar * inv
            red_bar = adj[19, zi, r] + 2.0 * psi_bar
            dens_bar = (adj[20, zi, r] - (1.0 + psi) * psi_bar) * (1.0 / 36.0)
            push = odd_part([adj[21 + k, zi, r] for k in range(3)])
            push[:3] = [adj[21 + k, zi, r] for k in range(3)]
            keep = 1.0 - RELAX_RATE
            adj[19, zi, r] = red_bar * (1.0 / 36.0)
            adj[0, zi, r] = keep * adj[0, zi, r] + dens_bar
            for k in range(9):
                adj[2 * k + 1, zi, r] = keep * adj[2 * k + 1, zi, r] + (dens_bar + push[k])
                adj[2 * k + 2, zi, r] = keep * adj[2 * k + 2, zi, r] + (dens_bar - push[k])
        return carry

    lax.fori_loop(0, nz, back_phase, 0, unroll=True)

    def back_first(z, carry):
        zi = z + 1
        ahead = [None] + [moved(adj.at[i], zi, i, 1) for i in range(1, 19)]
        ahead_r = all_moved(adj.at[19], zi)
        for r in range(ROW_TILES):
            s = link(z, r)
            dens, psi = rho[zi, r], p1[zi, r]
            fluid = jnp.where(dens == 0.0, 0.0, 1.0)
            red = 0.5 * dens * (1.0 + psi)
            blue = 0.5 * dens * (1.0 - psi)
            alpha = red / (dens + (1.0 - fluid))
            beta = RECOLOURING_PACE * alpha * blue
            own = adj[19, zi, r]
            r_hat, hat = [own], [adj[0, zi, r] + alpha * own]
            for i in range(1, 19):
                blocked = s[i] > 0.5
                r_i = jnp.where(blocked, own, ahead_r[i][r])
                r_hat.append(r_i)
                hat.append(jnp.where(blocked, adj[OPPOSITE[i], zi, r], ahead[i][r]) + alpha * r_i)
            h0, h2 = weighted_even(hat[0], pair_sums(hat))
            g = tuple(g1[k, zi, r] for k in range(3))
            bars, _ = toward_gradient(g, fluid, h0, h2, weighted_first(r_hat), beta)
            for k in range(3):
                gbar[k, zi, r] = bars[k]
        return carry

    lax.fori_loop(0, nz, back_first, 0, unroll=True)

    for zl in range(local_z):
        zi = 1 + thick * local_z + zl
        field = gradient_back([gbar.at[k] for k in range(3)], zi)
        bar = pbar2[zi, 0] + field[0] * (-1.0 / 12.0)
        bar = jnp.where(rho[zi, 0] == 0.0, bar, 0.0)
        out_ref[zl] = bar[:, :HALF]


def pack_kernel(local_z, solid_ref, labels_ref, density_ref, wet_ref, dir_ref, map_ref, out_ref):
    for z in range(local_z):
        solid = solid_ref[z].astype(jnp.float32)
        label = labels_ref[z].astype(jnp.float32)
        fluid = 1.0 - solid
        red = density_ref[z] * label * fluid
        blue = density_ref[z] * (1.0 - label) * fluid
        psi = (red - blue) / (red + blue + solid)
        out_ref[z] = red + blue
        out_ref[local_z + z] = fluid * psi + solid * wet_ref[z]
        out_ref[2 * local_z + z] = solid * dir_ref[z]
    pixels = map_ref[...]
    lane = lax.broadcasted_iota(jnp.int32, pixels.shape, 1)
    counts = jnp.zeros(pixels.shape, jnp.int32)
    for k in range(pixels.shape[1]):
        turned = pltpu.roll(pixels, k, 1) if k else pixels
        counts = counts + (turned == lane).astype(jnp.int32)
    out_ref[3 * local_z] = counts.astype(jnp.float32)


def one_exchange(solid, labels, density, wettability, direction, pixel_map):
    local_z = solid.shape[0]
    planes, slabs = lax.axis_size("plane"), lax.axis_size("thick")
    nz = local_z * slabs
    per = 3 * local_z + 1
    vmem = pl.BlockSpec(memory_space=pltpu.VMEM)
    packed = pl.pallas_call(
        functools.partial(pack_kernel, local_z),
        out_shape=jax.ShapeDtypeStruct((per, 8, HALF), jnp.float32),
        in_specs=[vmem] * 6,
        out_specs=vmem,
    )(solid[:, 0], labels[:, 0], density[:, 0], wettability[:, 0], direction[:, 0], pixel_map[0])

    def send(array, target):
        route = []
        for b in range(planes):
            for t in range(slabs):
                to_b, to_t = target(b, t)
                route.append((b * slabs + t, (to_b % planes) * slabs + to_t))
        return lax.ppermute(array, ("plane", "thick"), route)

    beside_z = send(packed, lambda b, t: (b, 1 - t))
    beside_y = send(packed, lambda b, t: (b ^ 1, t))
    beside_zy = send(packed, lambda b, t: (b ^ 1, 1 - t))
    quad = jnp.concatenate([beside_y, beside_zy, packed, beside_z])
    above = send(quad, lambda b, t: (b + 2, t))
    below = send(quad, lambda b, t: (b - 2, t))
    corner = send(quad[: 2 * per], lambda b, t: (b + 4 if b % 2 == 0 else b - 4, t))

    def field(*lead):
        return pltpu.VMEM(lead + (ROW_TILES, 8, WIDE), jnp.float32)

    padded = nz + 2
    return pl.pallas_call(
        functools.partial(main_kernel, nz, local_z),
        out_shape=(
            jax.ShapeDtypeStruct((local_z, 8, HALF), jnp.float32),
            jax.ShapeDtypeStruct((8, HALF), jnp.float32),
        ),
        in_specs=[vmem] * 5,
        out_specs=(vmem, vmem),
        scratch_shapes=[
            field(padded), field(padded), field(padded), field(),
            field(18, nz), field(9, padded), field(9, padded), field(36, padded),
            field(19, padded), field(19, padded), field(6, padded),
            field(padded), field(padded), field(3, padded), field(3, padded),
            field(padded), field(padded), field(), field(24, padded), field(3, padded),
            field(padded),
        ],
        compiler_params=pltpu.CompilerParams(vmem_limit_bytes=30 * 1024 * 1024),
    )(quad, above, below, corner, pixel_map[0])


def fits_one_exchange(mesh, solid):
    return mesh.shape["plane"] == 2 * NBX and mesh.shape["thick"] == 2 and solid.shape[2:] == (8, HALF)


def solution(mesh):
    specs = (P("thick", "plane", None, None),) * 5 + (P("plane", None, None),)
    out_specs = (P("thick", "plane", None, None), P("plane", None, None))

    def program(solid, *rest):
        def with_bricks(*blocks):
            curvature, readings = one_exchange(*blocks)
            return curvature[:, None], readings[None]

        body = with_bricks if fits_one_exchange(mesh, solid) else per_device
        return jax.shard_map(
            body, mesh=mesh, in_specs=specs, out_specs=out_specs, check_vma=False
        )(solid, *rest)

    return program
```

```python
import functools

import jax
import jax.numpy as jnp
import numpy as np
from jax import lax
from jax.experimental import pallas as pl
from jax.experimental.pallas import tpu as pltpu
from jax.sharding import PartitionSpec as P

NBX = 8
STEPS = 2


VELOCITIES = np.array(
    [
        [0, 0, 0],
        [1, 0, 0],
        [-1, 0, 0],
        [0, 1, 0],
        [0, -1, 0],
        [0, 0, 1],
        [0, 0, -1],
        [1, 1, 0],
        [-1, -1, 0],
        [1, -1, 0],
        [-1, 1, 0],
        [1, 0, 1],
        [-1, 0, -1],
        [1, 0, -1],
        [-1, 0, 1],
        [0, 1, 1],
        [0, -1, -1],
        [0, 1, -1],
        [0, -1, 1],
    ]
)
WEIGHTS = np.array([1.0 / 3.0] + [1.0 / 18.0] * 6 + [1.0 / 36.0] * 12)
OPPOSITE = [int(np.argmin(np.abs(VELOCITIES + lattice_vec).sum(1))) for lattice_vec in VELOCITIES]
RELAX_RATE = 1.25
SURFACE_TENSION = 0.2
RECOLOURING_PACE = 0.7


def shifted(array, axis, by):
    devices = lax.axis_size(axis)
    pairs = [(i, i + by) for i in range(devices) if 0 <= i + by < devices]
    return lax.ppermute(array, axis, pairs)


def from_behind(block, axis, distance):
    devices = range(lax.axis_size(axis))
    route = [((i - distance) % len(devices), i) for i in devices]
    return lax.ppermute(block, axis, route)


def weights_like(array):
    return jnp.asarray(WEIGHTS, jnp.float32).reshape((19,) + (1,) * (array.ndim - 1))


def collide(red_pop, blue_pop, gradient, solid_cell):
    lattice_vel = jnp.asarray(VELOCITIES, jnp.float32)
    weight_column_vec = weights_like(red_pop)
    red_density_total = jnp.sum(red_pop, 0)
    blue_density_total = jnp.sum(blue_pop, 0)
    density = red_density_total + blue_density_total
    reciprocal_value = 1.0 / (density + solid_cell)
    total_pop = red_pop + blue_pop
    velocity = (
        jnp.einsum("qd,q...->d...", lattice_vel, total_pop, precision=lax.Precision.HIGHEST)
        * reciprocal_value
    )
    projected = jnp.einsum("qd,d...->q...", lattice_vel, velocity, precision=lax.Precision.HIGHEST)
    speed_sq = jnp.sum(velocity * velocity, 0)
    equilibrium = (
        weight_column_vec
        * density
        * (1.0 + 3.0 * projected + 4.5 * projected * projected - 1.5 * speed_sq)
    )
    relaxed_populations = total_pop + RELAX_RATE * (equilibrium - total_pop)
    along_gradient_dir = jnp.einsum(
        "qd,d...->q...", lattice_vel, gradient, precision=lax.Precision.HIGHEST
    )
    grad_sq = jnp.sum(gradient * gradient, 0)
    norm_scale_factor = 1.0 / jnp.sqrt(1.0 + grad_sq)
    relaxed_populations = (
        relaxed_populations
        + SURFACE_TENSION
        * weight_column_vec
        * (along_gradient_dir * along_gradient_dir - grad_sq / 3.0)
        * norm_scale_factor
    )
    red_output_pop = (
        red_density_total * reciprocal_value * relaxed_populations
        + RECOLOURING_PACE
        * red_density_total
        * blue_density_total
        * reciprocal_value
        * weight_column_vec
        * along_gradient_dir
        * norm_scale_factor
    )
    return (red_output_pop, relaxed_populations - red_output_pop)


def phase_of(red_pop, blue_pop, solid_cell):
    red_density_total = jnp.sum(red_pop, 0)
    blue_density_total = jnp.sum(blue_pop, 0)
    return (red_density_total - blue_density_total) / (
        red_density_total + blue_density_total + solid_cell
    )


def pull_from(padded, offset, extent):
    shift_z, shift_x, shift_y = (int(offset[0]), int(offset[1]), int(offset[2]))
    return padded[
        ...,
        1 - shift_z : 1 - shift_z + extent[0],
        1 - shift_x : 1 - shift_x + extent[1],
        1 - shift_y : 1 - shift_y + extent[2],
    ]


def gradient_of(padded, extent):
    components = [0.0, 0.0, 0.0]
    for number in range(1, 19):
        lattice_vec = VELOCITIES[number]
        pulled = pull_from(padded, -lattice_vec, extent)
        for axis_num in range(3):
            if lattice_vec[axis_num] != 0:
                components[axis_num] = (
                    components[axis_num]
                    + 3.0 * WEIGHTS[number] * float(lattice_vec[axis_num]) * pulled
                )
    return jnp.stack(components)


def spread_back(padded_bar, extent):
    total_bar = 0.0
    for number in range(1, 19):
        lattice_vec = VELOCITIES[number]
        for axis_num in range(3):
            if lattice_vec[axis_num] != 0:
                total_bar = total_bar + 3.0 * WEIGHTS[number] * float(
                    lattice_vec[axis_num]
                ) * pull_from(padded_bar[axis_num], lattice_vec, extent)
    return total_bar


def stream(padded_pop, local_pop, padded_fluid, fluid_cell, extent):
    outgoing = []
    for number in range(19):
        lattice_vec = VELOCITIES[number]
        source_fluid = pull_from(padded_fluid, lattice_vec, extent)
        arrived = pull_from(padded_pop[number], lattice_vec, extent)
        outgoing.append(
            fluid_cell
            * (source_fluid * arrived + (1.0 - source_fluid) * local_pop[OPPOSITE[number]])
        )
    return jnp.stack(outgoing)


def unstream(padded_bar, local_bar, padded_fluid, fluid_cell, extent):
    incoming = []
    for number in range(19):
        lattice_vec = VELOCITIES[number]
        ahead_fluid = pull_from(padded_fluid, -lattice_vec, extent)
        ahead_bar = pull_from(padded_bar[number], -lattice_vec, extent)
        incoming.append(fluid_cell * ahead_bar + (1.0 - ahead_fluid) * local_bar[OPPOSITE[number]])
    return jnp.stack(incoming)


def fill_border(received, chosen, channels):
    if len(chosen) == channels:
        return received
    return (
        jnp.zeros((channels,) + received.shape[1:], received.dtype)
        .at[np.array(chosen)]
        .set(received)
    )


def grow(stacked, axis_dim, chosen_low, chosen_high, sender):
    length = stacked.shape[axis_dim]
    channels = stacked.shape[0]
    borders = []
    for toward in (1, -1):
        chosen = chosen_low if toward == 1 else chosen_high
        source = length - 1 if toward == 1 else 0
        outer_layer = lax.slice_in_dim(stacked, source, source + 1, axis=axis_dim)
        if len(chosen) < channels:
            outer_layer = outer_layer[np.array(chosen)]
        borders.append(fill_border(sender(outer_layer, toward), chosen, channels))
    return jnp.concatenate([borders[0], stacked, borders[1]], axis_dim)


def per_device(solid, labels, density, wettability, direction, pixel_map):
    solid_cell = solid[:, 0].astype(jnp.float32)
    fluid_cell = 1.0 - solid_cell
    label_cell = labels[:, 0].astype(jnp.float32)
    density_cell = density[:, 0]
    wetting = wettability[:, 0]
    tangent = direction[:, 0]
    column_map = pixel_map[0]
    extent = solid_cell.shape
    bricks_y = lax.axis_size("plane") // NBX

    def extend(stacked):
        channels = stacked.shape[0]

        def chosen_for():
            return list(range(channels))

        stacked = grow(
            stacked,
            1,
            chosen_for(),
            chosen_for(),
            lambda outgoing, toward: shifted(outgoing, "thick", toward),
        )
        stacked = grow(
            stacked,
            2,
            chosen_for(),
            chosen_for(),
            lambda outgoing, toward: from_behind(outgoing, "plane", toward * bricks_y),
        )
        stacked = grow(
            stacked,
            3,
            chosen_for(),
            chosen_for(),
            lambda outgoing, toward: from_behind(outgoing, "plane", toward),
        )
        return stacked

    def phase_pair(red_in, blue_in):
        return phase_of(red_in, blue_in, solid_cell)

    def collide_local(red_in, blue_in, gradient):
        return collide(red_in, blue_in, gradient, solid_cell)

    padded_fluid = extend(fluid_cell[None])[0]
    weight_column_vec = weights_like(solid_cell[None])
    red_pop = weight_column_vec * (density_cell * label_cell * fluid_cell)[None]
    blue_pop = weight_column_vec * (density_cell * (1.0 - label_cell) * fluid_cell)[None]
    red_tan = jnp.zeros_like(red_pop)
    blue_tan = jnp.zeros_like(blue_pop)
    checkpoints = []
    for number in range(STEPS):
        phase_val, phase_tan = jax.jvp(phase_pair, (red_pop, blue_pop), (red_tan, blue_tan))
        phase_field = fluid_cell * phase_val + solid_cell * wetting
        field_tan = fluid_cell * phase_tan + solid_cell * tangent
        padded = extend(jnp.stack([phase_field, field_tan]))
        gradient = gradient_of(padded[0], extent)
        gradient_tan = gradient_of(padded[1], extent)
        checkpoints.append((red_pop, blue_pop, gradient))
        (red_post, blue_post), (red_dot, blue_dot) = jax.jvp(
            collide_local, (red_pop, blue_pop, gradient), (red_tan, blue_tan, gradient_tan)
        )
        posted = jnp.concatenate([red_post, blue_post, red_dot, blue_dot])
        moved = extend(posted)
        red_pop, blue_pop, red_tan, blue_tan = [
            stream(
                moved[19 * group : 19 * group + 19],
                posted[19 * group : 19 * group + 19],
                padded_fluid,
                fluid_cell,
                extent,
            )
            for group in range(4)
        ]
    _, phase_tan = jax.jvp(phase_pair, (red_pop, blue_pop), (red_tan, blue_tan))
    partial_sum = jnp.sum(fluid_cell * phase_tan, 0)
    column_sum = lax.psum(partial_sum, "thick")
    found = jnp.take_along_axis(column_sum, column_map, axis=1)
    row_ids = jnp.arange(column_map.shape[0])[:, None]
    seeded = jnp.zeros_like(column_sum).at[row_ids, column_map].add(found)
    _, phase_back = jax.vjp(phase_pair, red_pop, blue_pop)
    red_bar, blue_bar = phase_back(fluid_cell * seeded[None])
    wetting_bar = jnp.zeros_like(wetting)
    for number in reversed(range(STEPS)):
        red_saved, blue_saved, gradient = checkpoints[number]
        outgoing_bar = jnp.concatenate([red_bar, blue_bar]) * fluid_cell
        padded = extend(outgoing_bar)
        red_pre = unstream(padded[:19], outgoing_bar[:19], padded_fluid, fluid_cell, extent)
        blue_pre = unstream(padded[19:], outgoing_bar[19:], padded_fluid, fluid_cell, extent)
        _, collide_back = jax.vjp(collide_local, red_saved, blue_saved, gradient)
        red_bar, blue_bar, gradient_bar = collide_back((red_pre, blue_pre))
        padded_bar = extend(gradient_bar)
        field_bar = spread_back(padded_bar, extent)
        wetting_bar = wetting_bar + solid_cell * field_bar
        if number > 0:
            _, phase_back = jax.vjp(phase_pair, red_saved, blue_saved)
            extra_red, extra_blue = phase_back(fluid_cell * field_bar)
            red_bar = red_bar + extra_red
            blue_bar = blue_bar + extra_blue
    return (wetting_bar[:, None], found[None])


HALF = 128
GROUP = 32
EDGE = 8
ROW_TILES = 3
CZ = [int(v[0]) for v in VELOCITIES]
CX = [int(v[1]) for v in VELOCITIES]
CY = [int(v[2]) for v in VELOCITIES]
GROUPS = [(gx, gy) for gx in (-1, 0, 1) for gy in (-1, 0, 1)]


def lanes():
    return lax.broadcasted_iota(jnp.int32, (8, HALF), 1)


def rows():
    return lax.broadcasted_iota(jnp.int32, (8, HALF), 0)


def turn(tile, by):
    by = by % HALF
    return pltpu.roll(tile, by, 1) if by else tile


def each(function, *fields):
    return [[function(*tiles) for tiles in zip(*units)] for units in zip(*fields)]


def add(a, b):
    return a + b


def sub(a, b):
    return a - b


def read(ref):
    return [[ref[r, u] for u in range(ref.shape[1])] for r in range(ref.shape[0])]


def narrow(field):
    near = rows() < 4
    return [field[0], [jnp.where(near, a, b) for a, b in zip(field[1], field[2])]]


def read_narrow(ref):
    return narrow(read(ref))


def z_shift(field, dz, fill=True):
    out = []
    for units in field:
        layers, side = units[:-1], units[-1]
        zero = jnp.zeros((8, HALF), jnp.float32)
        moved = layers[1:] + [zero] if dz == 1 else [zero] + layers[:-1]
        side = turn(side, -GROUP * dz)
        if fill:
            inside = lanes() < HALF - GROUP if dz == 1 else lanes() >= GROUP
            side = jnp.where(inside, side, 0.0)
        out.append(moved + [side])
    return out


def x_shift(field, dx):
    count = len(field)
    at_edge = rows() == (0 if dx == 1 else 7)
    return [
        [
            pltpu.roll(jnp.where(at_edge, beyond, here), (-dx) % 8, 0)
            for here, beyond in zip(field[r], field[(r + dx) % count])
        ]
        for r in range(count)
    ]


def y_shift(field, dy):
    lane = lanes()
    out = []
    for units in field:
        layers, side = units[:-1], units[-1]
        moved = []
        if dy == 1:
            inner = turn(side, -1)
            for z, tile in enumerate(layers):
                beyond = turn(side, HALF - 1 - (GROUP * z + GROUP - EDGE))
                moved.append(jnp.where(lane == HALF - 1, beyond, turn(tile, -1)))
                at = GROUP * z + EDGE - 1
                inner = jnp.where(lane == at, turn(tile, at), inner)
        else:
            inner = turn(side, 1)
            for z, tile in enumerate(layers):
                beyond = turn(side, -(GROUP * z + EDGE - 1))
                moved.append(jnp.where(lane == 0, beyond, turn(tile, 1)))
                at = GROUP * z + GROUP - EDGE
                inner = jnp.where(lane == at, turn(tile, at + 1), inner)
        out.append(moved + [inner])
    return out


def y_both(field):
    lane = lanes()
    spot = lane & (GROUP - 1)
    ahead, behind = [], []
    for units in field:
        layers, side = units[:-1], units[-1]
        edges = None
        up, down = [], []
        for z, tile in enumerate(layers):
            at = GROUP * z + EDGE - 1
            turned = turn(tile, at)
            edges = turned if edges is None else jnp.where(lane >= GROUP * z, turned, edges)
            beyond = turn(side, HALF - 1 - (GROUP * z + GROUP - EDGE))
            up.append(jnp.where(lane == HALF - 1, beyond, turn(tile, -1)))
            beyond = turn(side, -(GROUP * z + EDGE - 1))
            down.append(jnp.where(lane == 0, beyond, turn(tile, 1)))
        up.append(jnp.where(spot == EDGE - 1, edges, turn(side, -1)))
        lifted = turn(edges, GROUP - EDGE - (EDGE - 2))
        down.append(jnp.where(spot == GROUP - EDGE, lifted, turn(side, 1)))
        ahead.append(up)
        behind.append(down)
    return ahead, behind


def x_both(field):
    return x_shift(field, 1), x_shift(field, -1)


def z_both(field):
    return z_shift(field, 1), z_shift(field, -1)


def gradient(field):
    ahead, behind = z_both(field)
    two = each(lambda m, u, d: 2.0 * m + (u + d), field, ahead, behind)
    y_sum = each(add, *y_both(field))
    x_sum = each(add, *x_both(field))
    along_x = each(sub, *x_both(each(add, two, y_sum)))
    along_y = each(sub, *y_both(each(add, two, x_sum)))
    flat = each(lambda m, a, b: 2.0 * m + (a + b), field, x_sum, y_sum)
    along_z = each(sub, *z_both(flat))
    return along_z, along_x, along_y


def gradient_back(gz, gx, gy):
    def around(field, first, second):
        s = each(add, *first(field))
        t = each(add, *second(field))
        return each(lambda m, a, b: 2.0 * m + (a + b), field, s, t)

    result = each(sub, *x_both(around(gx, z_both, y_both)))
    result = each(add, result, each(sub, *y_both(around(gy, z_both, x_both))))
    return each(add, result, each(sub, *z_both(around(gz, x_both, y_both))))


def all_moved(field):
    ym = {0: field}
    ym[1], ym[-1] = y_both(field)
    xy = {(0, dy): ym[dy] for dy in ym}
    for dy in ym:
        xy[(1, dy)], xy[(-1, dy)] = x_both(ym[dy])
    out = []
    for i in range(19):
        moved = xy[(CX[i], CY[i])]
        out.append(z_shift(moved, CZ[i], fill=False) if CZ[i] else moved)
    return out


def moved_by(field, dz, dx, dy):
    if dy:
        field = y_shift(field, dy)
    if dx:
        field = x_shift(field, dx)
    if dz:
        field = z_shift(field, dz, fill=False)
    return field


def even_part(base, quad):
    zz, xx, yy, zx, zy, xy = quad
    out = [2.0 * (base + zz), 2.0 * (base + xx), 2.0 * (base + yy)]
    for diagonal, cross in ((zz + xx, zx), (zz + yy, zy), (xx + yy, xy)):
        flat = base + diagonal
        out += [flat + cross, flat - cross]
    return out


def odd_part(vector):
    z, x, y = vector
    return [2.0 * z, 2.0 * x, 2.0 * y, z + x, z - x, z + y, z - y, x + y, x - y]


def squares(vector):
    z, x, y = vector
    return [z * z, x * x, y * y, 2.0 * (z * x), 2.0 * (z * y), 2.0 * (x * y)]


def squares_dot(a, b):
    az, ax, ay = a
    bz, bx, by = b
    return [
        2.0 * (az * bz),
        2.0 * (ax * bx),
        2.0 * (ay * by),
        2.0 * (az * bx + ax * bz),
        2.0 * (az * by + ay * bz),
        2.0 * (ax * by + ay * bx),
    ]


def dot(a, b):
    return a[0] * b[0] + a[1] * b[1] + a[2] * b[2]


def first_moment(values):
    d = [values[2 * p + 1] - values[2 * p + 2] for p in range(9)]
    return (
        d[0] + (d[3] + d[4]) + (d[5] + d[6]),
        d[1] + (d[3] - d[4]) + (d[7] + d[8]),
        d[2] + (d[5] - d[6]) + (d[7] - d[8]),
    )


def weighted_first(values):
    d = [values[2 * p + 1] - values[2 * p + 2] for p in range(9)]
    return (
        2.0 * d[0] + (d[3] + d[4]) + (d[5] + d[6]),
        2.0 * d[1] + (d[3] - d[4]) + (d[7] + d[8]),
        2.0 * d[2] + (d[5] - d[6]) + (d[7] - d[8]),
    )


def weighted_even(rest, pairs):
    axis = [2.0 * pairs[0], 2.0 * pairs[1], 2.0 * pairs[2]]
    zx, zy, xy = pairs[3] + pairs[4], pairs[5] + pairs[6], pairs[7] + pairs[8]
    second = [
        axis[0] + zx + zy,
        axis[1] + zx + xy,
        axis[2] + zy + xy,
        pairs[3] - pairs[4],
        pairs[5] - pairs[6],
        pairs[7] - pairs[8],
    ]
    zeroth = 12.0 * rest + axis[0] + axis[1] + axis[2] + zx + zy + xy
    return zeroth, second


def pair_sums(values):
    return [values[2 * p + 1] + values[2 * p + 2] for p in range(9)]


def times(matrix, vector):
    zz, xx, yy, zx, zy, xy = matrix
    z, x, y = vector
    return (zz * z + zx * x + zy * y, zx * z + xx * x + xy * y, zy * z + xy * x + yy * y)


def total(values):
    values = list(values)
    while len(values) > 1:
        values = [
            values[k] + values[k + 1] if k + 1 < len(values) else values[k]
            for k in range(0, len(values), 2)
        ]
    return values[0]


def norm_parts(g):
    g2 = dot(g, g)
    return g2, lax.rsqrt(1.0 + g2)


def fluid_of(dens):
    return jnp.where(dens == 0.0, 0.0, 1.0)


def scatter_groups(acc, r, u, values, stay):
    side = acc.shape[2] - 1
    for k, (gx, gy) in enumerate(GROUPS):
        level = {CZ[i]: values[i] for i in range(1, 19) if (CX[i], CY[i]) == (gx, gy)}
        if (gx, gy) == (0, 0):
            level[0] = values[0] + stay
        if 1 not in level:
            acc[k, r, u] = level[0]
        elif u == side:
            lane = lanes()
            up = jnp.where(lane >= GROUP, turn(level[1], GROUP), 0.0)
            down = jnp.where(lane < HALF - GROUP, turn(level[-1], -GROUP), 0.0)
            acc[k, r, u] = level[0] + (up + down)
        else:
            acc[k, r, u] = acc[k, r, u] + level[0] if u else level[0]
            if u + 1 < side:
                acc[k, r, u + 1] = level[1]
            if u:
                acc[k, r, u - 1] = acc[k, r, u - 1] + level[-1]


def gathered_sum(acc, first, after_x=lambda field: field):
    by_y = []
    for gy in (-1, 0, 1):
        parts = [read(acc.at[first + GROUPS.index((0, gy))])]
        for gx in (-1, 1):
            parts.append(x_shift(read(acc.at[first + GROUPS.index((gx, gy))]), -gx))
        by_y.append(after_x(each(lambda a, b, c: a + (b + c), *parts)))
    return each(
        lambda a, b, c: b + (a + c), y_shift(by_y[0], 1), by_y[1], y_shift(by_y[2], -1)
    )


def toward_gradient(g, fluid, zeroth, second, first, beta):
    _, n = norm_parts(g)
    trace = zeroth * (1.0 / 3.0)
    shifted = [second[0] - trace, second[1] - trace, second[2] - trace] + list(second[3:])
    yg = times(shifted, g)
    gf = dot(g, first)
    nbar = (SURFACE_TENSION * fluid) * dot(g, yg) + beta * gf
    two_q = (2.0 * SURFACE_TENSION * fluid) * n
    bn = beta * n
    fall = nbar * n * n * n
    return [two_q * y + bn * f - fall * v for y, f, v in zip(yg, first, g)], n * gf


def main_kernel(nz, local_z, qp_ref, sl_ref, qm_ref, q_ref, map_ref, out_ref, read_ref,
                rho, p1, dp1, blk, t_st, dt_st, acc, pop, dpop, mac, p2, dp2, g1, g2, dg,
                a3, b3, adj, gbar, pbar2):
    thick = lax.axis_index("thick")
    even = lax.rem(lax.axis_index("plane"), 2) == 0
    units = nz + 1
    side = nz
    per = 3 * local_z + 1
    edge0 = 2 * per
    spot = lanes() & (GROUP - 1)
    left_part = spot < GROUP // 2

    def edge(ref, k):
        if k == 3:
            return ref[edge0 + k]
        return ref[edge0 + k] + ref[edge0 + 4 + k]

    def beside(r, k):
        own, minus, plus = [functools.partial(edge, ref, k) for ref in (q_ref, qm_ref, qp_ref)]
        corner = functools.partial(edge, sl_ref, k)
        if r == 0:
            right, left = jnp.where(even, own(), plus()), jnp.where(even, minus(), own())
        elif r == 1:
            right, left = jnp.where(even, plus(), corner()), jnp.where(even, own(), plus())
        else:
            right, left = jnp.where(even, minus(), own()), jnp.where(even, corner(), minus())
        return jnp.where(left_part, left, right)

    counts = []
    for r, source in enumerate((q_ref, qp_ref, qm_ref)):
        for which, ref in enumerate((rho, p1, dp1)):
            for z in range(nz):
                slab, zl = divmod(z, local_z)
                start = jnp.where(thick == slab, 0, per)
                ref[r, z] = source[start + which * local_z + zl]
            ref[r, side] = beside(r, which)
        counts.append([source[per - 1], beside(r, 3)])
    counts = narrow(counts)

    fluid_field = each(fluid_of, read(rho))
    ym = {0: fluid_field}
    ym[1], ym[-1] = y_both(fluid_field)
    xy = {(0, dy): ym[dy] for dy in ym}
    for dy in ym:
        xy[(1, dy)], xy[(-1, dy)] = x_both(ym[dy])
    for i in range(1, 19):
        there = xy[(CX[i], CY[i])]
        if CZ[i]:
            there = z_shift(there, CZ[i])
        for r in range(ROW_TILES):
            for u in range(units):
                blk[i - 1, r, u] = 1.0 - fluid_field[r][u] * there[r][u]

    def store_gradient(ref, first, field):
        for k, part in enumerate(gradient(field)):
            for r in range(ROW_TILES):
                for u in range(units):
                    ref[first + k, r, u] = part[r][u] * (1.0 / 12.0)

    store_gradient(g1, 0, read(p1))
    store_gradient(dg, 0, read(dp1))
    for r in range(ROW_TILES):
        for u in range(units):
            dens, psi = rho[r, u], p1[r, u]
            fluid = fluid_of(dens)
            red = 0.5 * dens * (1.0 + psi)
            blue = 0.5 * dens * (1.0 - psi)
            alpha = red / (dens + (1.0 - fluid))
            beta = RECOLOURING_PACE * alpha * blue
            g = [g1[k, r, u] for k in range(3)]
            gd = [dg[k, r, u] for k in range(3)]
            gg, n = norm_parts(g)
            gdg = dot(g, gd)
            n2g = n * n * gdg
            dn = -n * n2g
            q = (SURFACE_TENSION * fluid) * n
            dq = -q * n2g
            sq, dsq = squares(g), squares_dot(g, gd)
            base = dens - q * gg * (1.0 / 3.0)
            dbase = (dq * gg + 2.0 * q * gdg) * (-1.0 / 3.0)
            ev = even_part(base, [q * v for v in sq])
            dev = even_part(dbase, [dq * v + q * d for v, d in zip(sq, dsq)])
            bn, bdn = beta * n, beta * dn
            od = odd_part([bn * v for v in g])
            dod = odd_part([bdn * v + bn * d for v, d in zip(g, gd)])
            for k in range(9):
                t_st[k, r, u] = ev[k]
                dt_st[k, r, u] = dev[k]
            pop[0, r, u] = 12.0 * base
            dpop[0, r, u] = 12.0 * dbase
            s = [None] + [blk[i, r, u] for i in range(18)]
            for first, rest, evens, odds in (
                (0, 12.0 * base, ev, od), (9, 12.0 * dbase, dev, dod)
            ):
                scaled = [alpha * v for v in evens]
                values = [alpha * rest]
                stay = []
                for k in range(9):
                    values += [scaled[k] + odds[k], scaled[k] - odds[k]]
                    stay += [s[2 * k + 1] * values[-2], s[2 * k + 2] * values[-1]]
                scatter_groups(acc.at[pl.ds(first, 9)], r, u, values, total(stay))

    for ref, store in ((t_st, pop), (dt_st, dpop)):
        for k in range(9):
            i = 2 * k + 1
            field = read(ref.at[k])
            ahead, behind = field, field
            if CY[i]:
                ahead, behind = y_both(field)
                if CY[i] == -1:
                    ahead, behind = behind, ahead
            if CX[i]:
                ahead, behind = x_shift(ahead, CX[i]), x_shift(behind, -CX[i])
            if CZ[i]:
                ahead = z_shift(ahead, CZ[i], fill=False)
                behind = z_shift(behind, -CZ[i], fill=False)
            for r in range(ROW_TILES):
                for u in range(units):
                    here = field[r][u]
                    pop_i = jnp.where(blk[i, r, u] > 0.5, here, behind[r][u])
                    pop_o = jnp.where(blk[i - 1, r, u] > 0.5, here, ahead[r][u])
                    store[i, r, u] = pop_i
                    store[i + 1, r, u] = pop_o
    red_sum = gathered_sum(acc, 0)
    dred_sum = gathered_sum(acc, 9)
    for r in range(ROW_TILES):
        for u in range(units):
            fluid = fluid_of(rho[r, u])
            dens = total([pop[i, r, u] for i in range(19)]) * (1.0 / 36.0)
            ddens = total([dpop[i, r, u] for i in range(19)]) * (1.0 / 36.0)
            scale = fluid * (1.0 / 36.0)
            red = red_sum[r][u] * scale
            dred = dred_sum[r][u] * scale
            inv = 1.0 / (dens + (1.0 - fluid))
            psi = (2.0 * red - dens) * inv
            dpsi = (2.0 * dred - (1.0 + psi) * ddens) * inv
            for k, v in enumerate((dens, ddens, red, dred, inv, psi)):
                mac[k, r, u] = v
            p2[r, u] = jnp.where(fluid > 0.5, psi, p1[r, u])
            dp2[r, u] = jnp.where(fluid > 0.5, dpsi, dp1[r, u])

    store_gradient(g2, 0, read(p2))
    store_gradient(dg, 0, read(dp2))
    for r in range(ROW_TILES):
        for u in range(units):
            dens, ddens, red, dred, inv = [mac[k, r, u] for k in range(5)]
            fluid = fluid_of(rho[r, u])
            t = [pop[i, r, u] for i in range(19)]
            dt = [dpop[i, r, u] for i in range(19)]
            m = [v * (1.0 / 36.0) for v in first_moment(t)]
            dm = [v * (1.0 / 36.0) for v in first_moment(dt)]
            vel = [inv * v for v in m]
            shrink = inv * ddens
            dvel = [inv * b - shrink * a for a, b in zip(vel, dm)]
            g = [g2[k, r, u] for k in range(3)]
            gd = [dg[k, r, u] for k in range(3)]
            gg, n = norm_parts(g)
            gdg = dot(g, gd)
            n2g = n * n * gdg
            dn = -n * n2g
            q = (SURFACE_TENSION * fluid) * n
            dq = -q * n2g
            base = RELAX_RATE * dens - (1.5 * RELAX_RATE) * dot(m, vel) - q * gg * (1.0 / 3.0)
            dbase = (
                RELAX_RATE * ddens
                - (1.5 * RELAX_RATE) * (dot(dm, vel) + dot(m, dvel))
                + (dq * gg + 2.0 * q * gdg) * (-1.0 / 3.0)
            )
            lin = odd_part([(3.0 * RELAX_RATE) * v for v in m])
            dlin = odd_part([(3.0 * RELAX_RATE) * v for v in dm])
            mq = [(4.5 * RELAX_RATE) * v for v in m]
            dmq = [(4.5 * RELAX_RATE) * v for v in dm]
            order = ((0, 0), (1, 1), (2, 2), (0, 1), (0, 2), (1, 2))
            sq, dsq = squares(g), squares_dot(g, gd)
            quad, dquad = [], []
            for k, (a, b) in enumerate(order):
                flow = mq[a] * vel[b]
                dflow = dmq[a] * vel[b] + mq[a] * dvel[b]
                if a != b:
                    flow = 2.0 * flow
                    dflow = 2.0 * dflow
                quad.append(flow + q * sq[k])
                dquad.append(dflow + dq * sq[k] + q * dsq[k])
            ev, dev = even_part(base, quad), even_part(dbase, dquad)
            keep = 1.0 - RELAX_RATE
            after, dafter = [keep * t[0] + 12.0 * base], [keep * dt[0] + 12.0 * dbase]
            for k in range(9):
                after += [keep * t[2 * k + 1] + (ev[k] + lin[k]), keep * t[2 * k + 2] + (ev[k] - lin[k])]
                dafter += [
                    keep * dt[2 * k + 1] + (dev[k] + dlin[k]),
                    keep * dt[2 * k + 2] + (dev[k] - dlin[k]),
                ]
            alpha = red * inv
            dalpha = dred * inv - alpha * shrink
            blue, dblue = dens - red, ddens - dred
            beta = RECOLOURING_PACE * alpha * blue
            dbeta = RECOLOURING_PACE * (dalpha * blue + alpha * dblue)
            bn = beta * n
            dbn = dbeta * n + beta * dn
            od = odd_part([bn * v for v in g])
            dod = odd_part([dbn * v + bn * d for v, d in zip(g, gd)])
            reds, dreds = [alpha * after[0]], [dalpha * after[0] + alpha * dafter[0]]
            for i in range(1, 19):
                k = (i - 1) // 2
                side = od[k] if i % 2 else -od[k]
                dside = dod[k] if i % 2 else -dod[k]
                reds.append(alpha * after[i] + side)
                dreds.append(dalpha * after[i] + alpha * dafter[i] + dside)
            s = [None] + [blk[i, r, u] for i in range(18)]
            for k, values in enumerate((reds, dreds, after, dafter)):
                stay = total([s[i] * values[i] for i in range(1, 19)])
                scatter_groups(acc.at[pl.ds(9 * k, 9)], r, u, values, stay)

    red_s = gathered_sum(acc, 0, narrow)
    dred_s = gathered_sum(acc, 9, narrow)
    dens_s = gathered_sum(acc, 18, narrow)
    ddens_s = gathered_sum(acc, 27, narrow)
    rho_n = read_narrow(rho)
    seeds = []
    for r in range(2):
        found, pulls = [], []
        for u in range(units):
            fluid = fluid_of(rho_n[r][u])
            scale = fluid * (1.0 / 36.0)
            dens = dens_s[r][u] * scale
            inv = 1.0 / (dens + (1.0 - fluid))
            psi = (2.0 * (red_s[r][u] * scale) - dens) * inv
            a = 2.0 * (scale * inv)
            b = -(scale * inv) * (1.0 + psi)
            pulls.append((a, b))
            found.append(a * dred_s[r][u] + b * ddens_s[r][u])
        column = total(found[:-1])
        if r == 0:
            read_ref[...] = jnp.take_along_axis(column, map_ref[...], axis=1)
        beside_sum = found[-1] + turn(found[-1], GROUP)
        beside_sum = beside_sum + turn(beside_sum, 2 * GROUP)
        seed = [column * counts[r][0]] * nz + [beside_sum * counts[r][1]]
        for u in range(units):
            a3[r, u] = pulls[u][0] * seed[u]
            b3[r, u] = pulls[u][1] * seed[u]

    def pick(ref, k, r, u):
        if r == 0:
            return ref[k, 0, u]
        return jnp.where(rows() < 4, ref[k, 1, u], ref[k, 2, u])

    ahead_r = all_moved(read(a3))
    ahead_t = all_moved(read(b3))
    for r in range(2):
        for u in range(units):
            own_r, own_t = a3[r, u], b3[r, u]
            dens, red, inv = [pick(mac, k, r, u) for k in (0, 2, 4)]
            fluid = fluid_of(rho_n[r][u])
            alpha = red * inv
            blue = dens - red
            beta = RECOLOURING_PACE * alpha * blue
            r_hat, hat = [own_r], [own_t + alpha * own_r]
            for i in range(1, 19):
                blocked = pick(blk, i - 1, r, u) > 0.5
                r_i = jnp.where(blocked, own_r, ahead_r[i][r][u])
                t_i = jnp.where(blocked, own_t, ahead_t[i][r][u])
                r_hat.append(r_i)
                hat.append(t_i + alpha * r_i)
            t = [pick(pop, i, r, u) for i in range(19)]
            m = [v * (1.0 / 36.0) for v in first_moment(t)]
            vel = [inv * v for v in m]
            g = [pick(g2, k, r, u) for k in range(3)]
            _, n = norm_parts(g)
            q = (SURFACE_TENSION * fluid) * n
            h0, h2 = weighted_even(hat[0], pair_sums(hat))
            h1 = weighted_first(hat)
            k0, k2 = weighted_even(r_hat[0], pair_sums(r_hat))
            k1 = weighted_first(r_hat)
            bars, n_gk = toward_gradient(g, fluid, h0, h2, k1, beta)
            for k in range(3):
                gbar[k, r, u] = bars[k]
            uu = 1.5 * RELAX_RATE
            flow = [(4.5 * RELAX_RATE) * k2[j] - (uu * k0 if j < 3 else 0.0) for j in range(6)]
            surf = [k2[j] - (k0 * (1.0 / 3.0) if j < 3 else 0.0) for j in range(6)]
            alpha_bar = (
                (1.0 - RELAX_RATE) * total([a * b for a, b in zip(r_hat, t)])
                + RELAX_RATE * dens * k0
                + (3.0 * RELAX_RATE) * dot(m, k1)
                + dot(m, times(flow, vel))
                + q * dot(g, times(surf, g))
            )
            alpha_bar = alpha_bar + RECOLOURING_PACE * blue * n_gk
            blue_bar = RECOLOURING_PACE * alpha * n_gk
            flow_h = [(4.5 * RELAX_RATE) * h2[j] - (uu * h0 if j < 3 else 0.0) for j in range(6)]
            xu = times(flow_h, vel)
            red_bar = inv * alpha_bar - blue_bar
            dens_bar = RELAX_RATE * h0 - dot(vel, xu) + blue_bar - alpha * inv * alpha_bar
            adj[19, r, u] = red_bar
            adj[20, r, u] = dens_bar
            for k in range(3):
                adj[21 + k, r, u] = ((3.0 * RELAX_RATE) * h1[k] + 2.0 * xu[k]) * (1.0 / 36.0)
            for i in range(19):
                adj[i, r, u] = hat[i]

    field = gradient_back(*[read(gbar.at[k]) for k in range(3)])
    for r in range(2):
        for u in range(units):
            fluid = fluid_of(rho_n[r][u])
            inv, psi = pick(mac, 4, r, u), pick(mac, 5, r, u)
            bar = field[r][u] * (-1.0 / 12.0)
            if r == 0 and u < nz:
                pbar2[u] = bar
            psi_bar = fluid * bar * inv
            red_bar = adj[19, r, u] + 2.0 * psi_bar
            dens_bar = (adj[20, r, u] - (1.0 + psi) * psi_bar) * (1.0 / 36.0)
            pull = [adj[21 + k, r, u] for k in range(3)]
            push = pull + odd_part(pull)[3:]
            keep = 1.0 - RELAX_RATE
            adj[19, r, u] = red_bar * (1.0 / 36.0)
            adj[0, r, u] = keep * adj[0, r, u] + dens_bar
            for k in range(9):
                adj[2 * k + 1, r, u] = keep * adj[2 * k + 1, r, u] + (dens_bar + push[k])
                adj[2 * k + 2, r, u] = keep * adj[2 * k + 2, r, u] + (dens_bar - push[k])

    ahead_r = all_moved(read(adj.at[19]))
    ahead = [None] + [moved_by(read(adj.at[i]), CZ[i], CX[i], CY[i]) for i in range(1, 19)]
    for r in range(2):
        for u in range(units):
            dens = rho_n[r][u]
            psi = jnp.where(rows() < 4, p1[1, u], p1[2, u]) if r else p1[0, u]
            fluid = fluid_of(dens)
            red = 0.5 * dens * (1.0 + psi)
            blue = 0.5 * dens * (1.0 - psi)
            alpha = red / (dens + (1.0 - fluid))
            beta = RECOLOURING_PACE * alpha * blue
            own = adj[19, r, u]
            r_hat, hat = [own], [adj[0, r, u] + alpha * own]
            for i in range(1, 19):
                blocked = pick(blk, i - 1, r, u) > 0.5
                r_i = jnp.where(blocked, own, ahead_r[i][r][u])
                r_hat.append(r_i)
                hat.append(
                    jnp.where(blocked, adj[OPPOSITE[i], r, u], ahead[i][r][u]) + alpha * r_i
                )
            h0, h2 = weighted_even(hat[0], pair_sums(hat))
            g = [pick(g1, k, r, u) for k in range(3)]
            bars, _ = toward_gradient(g, fluid, h0, h2, weighted_first(r_hat), beta)
            for k in range(3):
                gbar[k, r, u] = bars[k]

    field = gradient_back(*[read(gbar.at[k]) for k in range(3)])
    result = []
    for z in range(nz):
        bar = pbar2[z] + field[0][z] * (-1.0 / 12.0)
        result.append(jnp.where(rho[0, z] == 0.0, bar, 0.0))
    for zl in range(local_z):
        chosen = result[zl]
        for slab in range(1, nz // local_z):
            chosen = jnp.where(thick == slab, result[slab * local_z + zl], chosen)
        out_ref[zl] = chosen


def pack_kernel(nz, local_z, solid_ref, labels_ref, density_ref, wet_ref, dir_ref, map_ref,
                out_ref, edge_ref):
    thick = lax.axis_index("thick")
    lane = lanes()
    spot = lane & (GROUP - 1)
    ends = (spot < EDGE, spot >= GROUP - EDGE)
    zero = jnp.zeros((8, HALF), jnp.float32)
    edges = [zero, zero, zero]

    def place(tile, z, into):
        here = (lane >= GROUP * z) & (lane < GROUP * z + GROUP)
        last = pltpu.roll(tile, lax.rem(GROUP * z + EDGE, HALF), 1)
        first = pltpu.roll(tile, lax.rem(GROUP * z + GROUP - EDGE, HALF), 1)
        into = jnp.where(here & ends[0], last, into)
        return jnp.where(here & ends[1], first, into)

    for zl in range(local_z):
        solid = solid_ref[zl].astype(jnp.float32)
        label = labels_ref[zl].astype(jnp.float32)
        fluid = 1.0 - solid
        red = density_ref[zl] * label * fluid
        blue = density_ref[zl] * (1.0 - label) * fluid
        psi = (red - blue) / (red + blue + solid)
        values = (red + blue, fluid * psi + solid * wet_ref[zl], solid * dir_ref[zl])
        for k, value in enumerate(values):
            out_ref[k * local_z + zl] = value
            edges[k] = place(value, thick * local_z + zl, edges[k])
    pixels = map_ref[...]
    counts = jnp.zeros(pixels.shape, jnp.int32)
    for k in range(pixels.shape[1]):
        counts = counts + (turn(pixels, k) == lane).astype(jnp.int32)
    counts = counts.astype(jnp.float32)
    out_ref[3 * local_z] = counts
    by_layer = zero
    for z in range(nz):
        by_layer = jnp.where(
            (lane >= GROUP * z) & ends[0], turn(counts, GROUP * z + EDGE), by_layer
        )
        by_layer = jnp.where(
            (lane >= GROUP * z) & ends[1], turn(counts, GROUP * z + GROUP - EDGE), by_layer
        )
    for k, tile in enumerate(edges + [by_layer]):
        edge_ref[k] = tile


def one_exchange(solid, labels, density, wettability, direction, pixel_map):
    local_z = solid.shape[0]
    planes, slabs = lax.axis_size("plane"), lax.axis_size("thick")
    nz = local_z * slabs
    per = 3 * local_z + 1
    vmem = pl.BlockSpec(memory_space=pltpu.VMEM)
    packed, edges = pl.pallas_call(
        functools.partial(pack_kernel, nz, local_z),
        out_shape=(
            jax.ShapeDtypeStruct((per, 8, HALF), jnp.float32),
            jax.ShapeDtypeStruct((4, 8, HALF), jnp.float32),
        ),
        in_specs=[vmem] * 6,
        out_specs=(vmem, vmem),
    )(solid[:, 0], labels[:, 0], density[:, 0], wettability[:, 0], direction[:, 0], pixel_map[0])

    def send(array, target):
        route = []
        for b in range(planes):
            for t in range(slabs):
                to_b, to_t = target(b, t)
                route.append((b * slabs + t, (to_b % planes) * slabs + to_t))
        return lax.ppermute(array, ("plane", "thick"), route)

    beside_z = send(packed, lambda b, t: (b, 1 - t))
    beside_y = send(edges, lambda b, t: (b ^ 1, t))
    beside_zy = send(edges, lambda b, t: (b ^ 1, 1 - t))
    quad = jnp.concatenate([packed, beside_z, beside_y, beside_zy])
    above = send(quad, lambda b, t: (b + 2, t))
    below = send(quad, lambda b, t: (b - 2, t))
    corner = send(quad, lambda b, t: (b + 4 if b % 2 == 0 else b - 4, t))

    def field(*lead, tiles=ROW_TILES):
        return pltpu.VMEM(lead + (tiles, nz + 1, 8, HALF), jnp.float32)

    return pl.pallas_call(
        functools.partial(main_kernel, nz, local_z),
        out_shape=(
            jax.ShapeDtypeStruct((local_z, 8, HALF), jnp.float32),
            jax.ShapeDtypeStruct((8, HALF), jnp.float32),
        ),
        in_specs=[vmem] * 5,
        out_specs=(vmem, vmem),
        scratch_shapes=[
            field(), field(), field(), field(18), field(9), field(9), field(36),
            field(19), field(19), field(6), field(), field(), field(3), field(3), field(3),
            field(tiles=2), field(tiles=2), field(24, tiles=2), field(3, tiles=2),
            pltpu.VMEM((nz, 8, HALF), jnp.float32),
        ],
        compiler_params=pltpu.CompilerParams(vmem_limit_bytes=24 * 1024 * 1024),
    )(below, corner, above, quad, pixel_map[0])


def fits_one_exchange(mesh, solid):
    sizes = (mesh.shape["plane"], mesh.shape["thick"])
    return sizes == (2 * NBX, 2) and solid.shape[2:] == (8, HALF) and solid.shape[0] * GROUP == HALF


def solution(mesh):
    specs = (P("thick", "plane", None, None),) * 5 + (P("plane", None, None),)
    out_specs = (P("thick", "plane", None, None), P("plane", None, None))

    def program(solid, *rest):
        def with_bricks(*blocks):
            curvature, readings = one_exchange(*blocks)
            return curvature[:, None], readings[None]

        body = with_bricks if fits_one_exchange(mesh, solid) else per_device
        return jax.shard_map(
            body, mesh=mesh, in_specs=specs, out_specs=out_specs, check_vma=False
        )(solid, *rest)

    return program
```

```python
import functools

import jax
import jax.numpy as jnp
import numpy as np
from jax import lax
from jax.experimental import pallas as pl
from jax.experimental.pallas import tpu as pltpu
from jax.sharding import PartitionSpec as P

NBX = 8
STEPS = 2


VELOCITIES = np.array(
    [
        [0, 0, 0],
        [1, 0, 0],
        [-1, 0, 0],
        [0, 1, 0],
        [0, -1, 0],
        [0, 0, 1],
        [0, 0, -1],
        [1, 1, 0],
        [-1, -1, 0],
        [1, -1, 0],
        [-1, 1, 0],
        [1, 0, 1],
        [-1, 0, -1],
        [1, 0, -1],
        [-1, 0, 1],
        [0, 1, 1],
        [0, -1, -1],
        [0, 1, -1],
        [0, -1, 1],
    ]
)
WEIGHTS = np.array([1.0 / 3.0] + [1.0 / 18.0] * 6 + [1.0 / 36.0] * 12)
OPPOSITE = [int(np.argmin(np.abs(VELOCITIES + lattice_vec).sum(1))) for lattice_vec in VELOCITIES]
RELAX_RATE = 1.25
SURFACE_TENSION = 0.2
RECOLOURING_PACE = 0.7


def shifted(array, axis, by):
    devices = lax.axis_size(axis)
    pairs = [(i, i + by) for i in range(devices) if 0 <= i + by < devices]
    return lax.ppermute(array, axis, pairs)


def from_behind(block, axis, distance):
    devices = range(lax.axis_size(axis))
    route = [((i - distance) % len(devices), i) for i in devices]
    return lax.ppermute(block, axis, route)


def weights_like(array):
    return jnp.asarray(WEIGHTS, jnp.float32).reshape((19,) + (1,) * (array.ndim - 1))


def collide(red_pop, blue_pop, gradient, solid_cell):
    lattice_vel = jnp.asarray(VELOCITIES, jnp.float32)
    weight_column_vec = weights_like(red_pop)
    red_density_total = jnp.sum(red_pop, 0)
    blue_density_total = jnp.sum(blue_pop, 0)
    density = red_density_total + blue_density_total
    reciprocal_value = 1.0 / (density + solid_cell)
    total_pop = red_pop + blue_pop
    velocity = (
        jnp.einsum("qd,q...->d...", lattice_vel, total_pop, precision=lax.Precision.HIGHEST)
        * reciprocal_value
    )
    projected = jnp.einsum("qd,d...->q...", lattice_vel, velocity, precision=lax.Precision.HIGHEST)
    speed_sq = jnp.sum(velocity * velocity, 0)
    equilibrium = (
        weight_column_vec
        * density
        * (1.0 + 3.0 * projected + 4.5 * projected * projected - 1.5 * speed_sq)
    )
    relaxed_populations = total_pop + RELAX_RATE * (equilibrium - total_pop)
    along_gradient_dir = jnp.einsum(
        "qd,d...->q...", lattice_vel, gradient, precision=lax.Precision.HIGHEST
    )
    grad_sq = jnp.sum(gradient * gradient, 0)
    norm_scale_factor = 1.0 / jnp.sqrt(1.0 + grad_sq)
    relaxed_populations = (
        relaxed_populations
        + SURFACE_TENSION
        * weight_column_vec
        * (along_gradient_dir * along_gradient_dir - grad_sq / 3.0)
        * norm_scale_factor
    )
    red_output_pop = (
        red_density_total * reciprocal_value * relaxed_populations
        + RECOLOURING_PACE
        * red_density_total
        * blue_density_total
        * reciprocal_value
        * weight_column_vec
        * along_gradient_dir
        * norm_scale_factor
    )
    return (red_output_pop, relaxed_populations - red_output_pop)


def phase_of(red_pop, blue_pop, solid_cell):
    red_density_total = jnp.sum(red_pop, 0)
    blue_density_total = jnp.sum(blue_pop, 0)
    return (red_density_total - blue_density_total) / (
        red_density_total + blue_density_total + solid_cell
    )


def pull_from(padded, offset, extent):
    shift_z, shift_x, shift_y = (int(offset[0]), int(offset[1]), int(offset[2]))
    return padded[
        ...,
        1 - shift_z : 1 - shift_z + extent[0],
        1 - shift_x : 1 - shift_x + extent[1],
        1 - shift_y : 1 - shift_y + extent[2],
    ]


def gradient_of(padded, extent):
    components = [0.0, 0.0, 0.0]
    for number in range(1, 19):
        lattice_vec = VELOCITIES[number]
        pulled = pull_from(padded, -lattice_vec, extent)
        for axis_num in range(3):
            if lattice_vec[axis_num] != 0:
                components[axis_num] = (
                    components[axis_num]
                    + 3.0 * WEIGHTS[number] * float(lattice_vec[axis_num]) * pulled
                )
    return jnp.stack(components)


def spread_back(padded_bar, extent):
    total_bar = 0.0
    for number in range(1, 19):
        lattice_vec = VELOCITIES[number]
        for axis_num in range(3):
            if lattice_vec[axis_num] != 0:
                total_bar = total_bar + 3.0 * WEIGHTS[number] * float(
                    lattice_vec[axis_num]
                ) * pull_from(padded_bar[axis_num], lattice_vec, extent)
    return total_bar


def stream(padded_pop, local_pop, padded_fluid, fluid_cell, extent):
    outgoing = []
    for number in range(19):
        lattice_vec = VELOCITIES[number]
        source_fluid = pull_from(padded_fluid, lattice_vec, extent)
        arrived = pull_from(padded_pop[number], lattice_vec, extent)
        outgoing.append(
            fluid_cell
            * (source_fluid * arrived + (1.0 - source_fluid) * local_pop[OPPOSITE[number]])
        )
    return jnp.stack(outgoing)


def unstream(padded_bar, local_bar, padded_fluid, fluid_cell, extent):
    incoming = []
    for number in range(19):
        lattice_vec = VELOCITIES[number]
        ahead_fluid = pull_from(padded_fluid, -lattice_vec, extent)
        ahead_bar = pull_from(padded_bar[number], -lattice_vec, extent)
        incoming.append(fluid_cell * ahead_bar + (1.0 - ahead_fluid) * local_bar[OPPOSITE[number]])
    return jnp.stack(incoming)


def fill_border(received, chosen, channels):
    if len(chosen) == channels:
        return received
    return (
        jnp.zeros((channels,) + received.shape[1:], received.dtype)
        .at[np.array(chosen)]
        .set(received)
    )


def grow(stacked, axis_dim, chosen_low, chosen_high, sender):
    length = stacked.shape[axis_dim]
    channels = stacked.shape[0]
    borders = []
    for toward in (1, -1):
        chosen = chosen_low if toward == 1 else chosen_high
        source = length - 1 if toward == 1 else 0
        outer_layer = lax.slice_in_dim(stacked, source, source + 1, axis=axis_dim)
        if len(chosen) < channels:
            outer_layer = outer_layer[np.array(chosen)]
        borders.append(fill_border(sender(outer_layer, toward), chosen, channels))
    return jnp.concatenate([borders[0], stacked, borders[1]], axis_dim)


def per_device(solid, labels, density, wettability, direction, pixel_map):
    solid_cell = solid[:, 0].astype(jnp.float32)
    fluid_cell = 1.0 - solid_cell
    label_cell = labels[:, 0].astype(jnp.float32)
    density_cell = density[:, 0]
    wetting = wettability[:, 0]
    tangent = direction[:, 0]
    column_map = pixel_map[0]
    extent = solid_cell.shape
    bricks_y = lax.axis_size("plane") // NBX

    def extend(stacked):
        channels = stacked.shape[0]

        def chosen_for():
            return list(range(channels))

        stacked = grow(
            stacked,
            1,
            chosen_for(),
            chosen_for(),
            lambda outgoing, toward: shifted(outgoing, "thick", toward),
        )
        stacked = grow(
            stacked,
            2,
            chosen_for(),
            chosen_for(),
            lambda outgoing, toward: from_behind(outgoing, "plane", toward * bricks_y),
        )
        stacked = grow(
            stacked,
            3,
            chosen_for(),
            chosen_for(),
            lambda outgoing, toward: from_behind(outgoing, "plane", toward),
        )
        return stacked

    def phase_pair(red_in, blue_in):
        return phase_of(red_in, blue_in, solid_cell)

    def collide_local(red_in, blue_in, gradient):
        return collide(red_in, blue_in, gradient, solid_cell)

    padded_fluid = extend(fluid_cell[None])[0]
    weight_column_vec = weights_like(solid_cell[None])
    red_pop = weight_column_vec * (density_cell * label_cell * fluid_cell)[None]
    blue_pop = weight_column_vec * (density_cell * (1.0 - label_cell) * fluid_cell)[None]
    red_tan = jnp.zeros_like(red_pop)
    blue_tan = jnp.zeros_like(blue_pop)
    checkpoints = []
    for number in range(STEPS):
        phase_val, phase_tan = jax.jvp(phase_pair, (red_pop, blue_pop), (red_tan, blue_tan))
        phase_field = fluid_cell * phase_val + solid_cell * wetting
        field_tan = fluid_cell * phase_tan + solid_cell * tangent
        padded = extend(jnp.stack([phase_field, field_tan]))
        gradient = gradient_of(padded[0], extent)
        gradient_tan = gradient_of(padded[1], extent)
        checkpoints.append((red_pop, blue_pop, gradient))
        (red_post, blue_post), (red_dot, blue_dot) = jax.jvp(
            collide_local, (red_pop, blue_pop, gradient), (red_tan, blue_tan, gradient_tan)
        )
        posted = jnp.concatenate([red_post, blue_post, red_dot, blue_dot])
        moved = extend(posted)
        red_pop, blue_pop, red_tan, blue_tan = [
            stream(
                moved[19 * group : 19 * group + 19],
                posted[19 * group : 19 * group + 19],
                padded_fluid,
                fluid_cell,
                extent,
            )
            for group in range(4)
        ]
    _, phase_tan = jax.jvp(phase_pair, (red_pop, blue_pop), (red_tan, blue_tan))
    partial_sum = jnp.sum(fluid_cell * phase_tan, 0)
    column_sum = lax.psum(partial_sum, "thick")
    found = jnp.take_along_axis(column_sum, column_map, axis=1)
    row_ids = jnp.arange(column_map.shape[0])[:, None]
    seeded = jnp.zeros_like(column_sum).at[row_ids, column_map].add(found)
    _, phase_back = jax.vjp(phase_pair, red_pop, blue_pop)
    red_bar, blue_bar = phase_back(fluid_cell * seeded[None])
    wetting_bar = jnp.zeros_like(wetting)
    for number in reversed(range(STEPS)):
        red_saved, blue_saved, gradient = checkpoints[number]
        outgoing_bar = jnp.concatenate([red_bar, blue_bar]) * fluid_cell
        padded = extend(outgoing_bar)
        red_pre = unstream(padded[:19], outgoing_bar[:19], padded_fluid, fluid_cell, extent)
        blue_pre = unstream(padded[19:], outgoing_bar[19:], padded_fluid, fluid_cell, extent)
        _, collide_back = jax.vjp(collide_local, red_saved, blue_saved, gradient)
        red_bar, blue_bar, gradient_bar = collide_back((red_pre, blue_pre))
        padded_bar = extend(gradient_bar)
        field_bar = spread_back(padded_bar, extent)
        wetting_bar = wetting_bar + solid_cell * field_bar
        if number > 0:
            _, phase_back = jax.vjp(phase_pair, red_saved, blue_saved)
            extra_red, extra_blue = phase_back(fluid_cell * field_bar)
            red_bar = red_bar + extra_red
            blue_bar = blue_bar + extra_blue
    return (wetting_bar[:, None], found[None])


HALF = 128
GROUP = 32
ROW_TILES = 3
CZ = [int(v[0]) for v in VELOCITIES]
CX = [int(v[1]) for v in VELOCITIES]
CY = [int(v[2]) for v in VELOCITIES]
GROUPS = [(gx, gy) for gx in (-1, 0, 1) for gy in (-1, 0, 1)]


def lanes():
    return lax.broadcasted_iota(jnp.int32, (8, HALF), 1)


def places():
    return (lanes() + GROUP // 2) & (HALF - 1)


def rows():
    return lax.broadcasted_iota(jnp.int32, (8, HALF), 0)


def turn(tile, by):
    by = by % HALF
    return pltpu.roll(tile, by, 1) if by else tile


def each(function, *fields):
    return [[function(*tiles) for tiles in zip(*units)] for units in zip(*fields)]


def add(a, b):
    return a + b


def sub(a, b):
    return a - b


def read(ref):
    return [[ref[r, u] for u in range(ref.shape[1])] for r in range(ref.shape[0])]


def narrow(field):
    near = rows() < 4
    return [field[0], [jnp.where(near, a, b) for a, b in zip(field[1], field[2])]]


def read_narrow(ref):
    return narrow(read(ref))


def z_shift(field, dz, fill=True):
    out = []
    for units in field:
        layers, side = units[:-1], units[-1]
        zero = jnp.zeros((8, HALF), jnp.float32)
        moved = layers[1:] + [zero] if dz == 1 else [zero] + layers[:-1]
        side = turn(side, -GROUP * dz)
        if fill:
            inside = places() < HALF - GROUP if dz == 1 else places() >= GROUP
            side = jnp.where(inside, side, 0.0)
        out.append(moved + [side])
    return out


def x_shift(field, dx):
    count = len(field)
    at_edge = rows() == (0 if dx == 1 else 7)
    return [
        [
            pltpu.roll(jnp.where(at_edge, beyond, here), (-dx) % 8, 0)
            for here, beyond in zip(field[r], field[(r + dx) % count])
        ]
        for r in range(count)
    ]


def y_ends(units):
    layers, side = units[:-1], units[-1]
    place = places()
    beyond, ends = [], None
    for z, tile in enumerate(layers):
        beyond.append(turn(side, -(GROUP * z + 1)))
        turned = turn(tile, GROUP * z + 1)
        ends = turned if ends is None else jnp.where(place >= GROUP * z, turned, ends)
    return beyond, ends


def y_step(units, ready, dy):
    beyond, ends = ready
    at_end = lanes() == (HALF - 1 if dy == 1 else 0)
    at_side = (places() & (GROUP - 1)) == (GROUP // 2 + 1 if dy == 1 else GROUP // 2)
    out = [jnp.where(at_end, b, turn(t, -dy)) for t, b in zip(units, beyond)]
    return out + [jnp.where(at_side, ends, turn(units[-1], dy))]


def y_shift(field, dy):
    return [y_step(units, y_ends(units), dy) for units in field]


def y_both(field):
    ready = [y_ends(units) for units in field]
    return tuple([y_step(u, e, dy) for u, e in zip(field, ready)] for dy in (1, -1))


def x_both(field):
    return x_shift(field, 1), x_shift(field, -1)


def z_both(field):
    return z_shift(field, 1), z_shift(field, -1)


def gradient(field):
    two = each(lambda m, u, d: 2.0 * m + (u + d), field, *z_both(field))
    y_up, y_down = y_both(field)
    y_sum, y_slope = each(add, y_up, y_down), each(sub, y_up, y_down)
    x_sum = each(add, *x_both(field))
    along_x = each(sub, *x_both(each(add, two, y_sum)))
    flat = each(lambda m, a, b: 2.0 * m + (a + b), field, x_sum, y_sum)
    along_z = each(sub, *z_both(flat))
    along_y = each(
        lambda m, a, b, c, d: 2.0 * m + ((a + b) + (c + d)),
        y_slope, *z_both(y_slope), *x_both(y_slope),
    )
    return along_z, along_x, along_y


def gradient_back(gz, gx, gy):
    dx, dz = each(sub, *x_both(gx)), each(sub, *z_both(gz))
    level = each(
        lambda a, b, c, d, e, f: 2.0 * (a + b) + ((c + d) + (e + f)),
        dx, dz, *z_both(dx), *x_both(dz),
    )
    across = each(add, dx, dz)
    along = each(
        lambda m, a, b, c, d: 2.0 * m + ((a + b) + (c + d)), gy, *z_both(gy), *x_both(gy)
    )
    ahead = y_shift(each(add, across, along), 1)
    behind = y_shift(each(sub, across, along), -1)
    return each(lambda a, b, c: a + (b + c), level, ahead, behind)


def all_moved(field):
    ym = {0: field}
    ym[1], ym[-1] = y_both(field)
    xy = {(0, dy): ym[dy] for dy in ym}
    for dy in ym:
        xy[(1, dy)], xy[(-1, dy)] = x_both(ym[dy])
    out = []
    for i in range(19):
        moved = xy[(CX[i], CY[i])]
        out.append(z_shift(moved, CZ[i], fill=False) if CZ[i] else moved)
    return out


def moved_by(field, dz, dx):
    if dx:
        field = x_shift(field, dx)
    if dz:
        field = z_shift(field, dz, fill=False)
    return field


def even_part(base, quad):
    zz, xx, yy, zx, zy, xy = quad
    out = [2.0 * (base + zz), 2.0 * (base + xx), 2.0 * (base + yy)]
    for diagonal, cross in ((zz + xx, zx), (zz + yy, zy), (xx + yy, xy)):
        flat = base + diagonal
        out += [flat + cross, flat - cross]
    return out


def odd_part(vector):
    z, x, y = vector
    return [2.0 * z, 2.0 * x, 2.0 * y, z + x, z - x, z + y, z - y, x + y, x - y]


def squares(vector):
    z, x, y = vector
    return [z * z, x * x, y * y, 2.0 * (z * x), 2.0 * (z * y), 2.0 * (x * y)]


def squares_dot(a, b):
    az, ax, ay = a
    bz, bx, by = b
    return [
        2.0 * (az * bz),
        2.0 * (ax * bx),
        2.0 * (ay * by),
        2.0 * (az * bx + ax * bz),
        2.0 * (az * by + ay * bz),
        2.0 * (ax * by + ay * bx),
    ]


def dot(a, b):
    return a[0] * b[0] + a[1] * b[1] + a[2] * b[2]


def first_moment(values):
    d = [values[2 * p + 1] - values[2 * p + 2] for p in range(9)]
    return (
        d[0] + (d[3] + d[4]) + (d[5] + d[6]),
        d[1] + (d[3] - d[4]) + (d[7] + d[8]),
        d[2] + (d[5] - d[6]) + (d[7] - d[8]),
    )


def weighted_first(values):
    d = [values[2 * p + 1] - values[2 * p + 2] for p in range(9)]
    return (
        2.0 * d[0] + (d[3] + d[4]) + (d[5] + d[6]),
        2.0 * d[1] + (d[3] - d[4]) + (d[7] + d[8]),
        2.0 * d[2] + (d[5] - d[6]) + (d[7] - d[8]),
    )


def weighted_even(rest, pairs):
    axis = [2.0 * pairs[0], 2.0 * pairs[1], 2.0 * pairs[2]]
    zx, zy, xy = pairs[3] + pairs[4], pairs[5] + pairs[6], pairs[7] + pairs[8]
    second = [
        axis[0] + zx + zy,
        axis[1] + zx + xy,
        axis[2] + zy + xy,
        pairs[3] - pairs[4],
        pairs[5] - pairs[6],
        pairs[7] - pairs[8],
    ]
    zeroth = 12.0 * rest + axis[0] + axis[1] + axis[2] + zx + zy + xy
    return zeroth, second


def pair_sums(values):
    return [values[2 * p + 1] + values[2 * p + 2] for p in range(9)]


def times(matrix, vector):
    zz, xx, yy, zx, zy, xy = matrix
    z, x, y = vector
    return (zz * z + zx * x + zy * y, zx * z + xx * x + xy * y, zy * z + xy * x + yy * y)


def total(values):
    values = list(values)
    while len(values) > 1:
        values = [
            values[k] + values[k + 1] if k + 1 < len(values) else values[k]
            for k in range(0, len(values), 2)
        ]
    return values[0]


def norm_parts(g):
    g2 = dot(g, g)
    return g2, lax.rsqrt(1.0 + g2)


def fluid_of(dens):
    return jnp.where(dens == 0.0, 0.0, 1.0)


def scatter_groups(acc, r, u, values, stay):
    side = acc.shape[2] - 1
    for k, (gx, gy) in enumerate(GROUPS):
        level = {CZ[i]: values[i] for i in range(1, 19) if (CX[i], CY[i]) == (gx, gy)}
        if (gx, gy) == (0, 0):
            level[0] = values[0] + stay
        if 1 not in level:
            acc[k, r, u] = level[0]
        elif u == side:
            place = places()
            up = jnp.where(place >= GROUP, turn(level[1], GROUP), 0.0)
            down = jnp.where(place < HALF - GROUP, turn(level[-1], -GROUP), 0.0)
            acc[k, r, u] = level[0] + (up + down)
        else:
            acc[k, r, u] = acc[k, r, u] + level[0] if u else level[0]
            if u + 1 < side:
                acc[k, r, u + 1] = level[1]
            if u:
                acc[k, r, u - 1] = acc[k, r, u - 1] + level[-1]


def gathered_sum(acc, first, after_x=lambda field: field):
    by_y = []
    for gy in (-1, 0, 1):
        parts = [read(acc.at[first + GROUPS.index((0, gy))])]
        for gx in (-1, 1):
            parts.append(x_shift(read(acc.at[first + GROUPS.index((gx, gy))]), -gx))
        by_y.append(after_x(each(lambda a, b, c: a + (b + c), *parts)))
    return each(
        lambda a, b, c: b + (a + c), y_shift(by_y[0], 1), by_y[1], y_shift(by_y[2], -1)
    )


def toward_gradient(g, fluid, zeroth, second, first, beta):
    _, n = norm_parts(g)
    trace = zeroth * (1.0 / 3.0)
    shifted = [second[0] - trace, second[1] - trace, second[2] - trace] + list(second[3:])
    yg = times(shifted, g)
    gf = dot(g, first)
    nbar = (SURFACE_TENSION * fluid) * dot(g, yg) + beta * gf
    two_q = (2.0 * SURFACE_TENSION * fluid) * n
    bn = beta * n
    fall = nbar * n * n * n
    return [two_q * y + bn * f - fall * v for y, f, v in zip(yg, first, g)], n * gf


def main_kernel(nz, local_z, qp_ref, sl_ref, qm_ref, q_ref, map_ref, out_ref, read_ref,
                rho, p1, dp1, blk, t_st, dt_st, acc, pop, dpop, mac, p2, dp2, g1, g2, dg,
                a3, b3, adj, gbar, pbar2):
    thick = lax.axis_index("thick")
    even = lax.rem(lax.axis_index("plane"), 2) == 0
    units = nz + 1
    side = nz
    per = 3 * local_z + 1
    edge0 = 2 * per
    left_part = (places() & (GROUP - 1)) > GROUP // 2

    def edge(ref, k):
        if k == 3:
            return ref[edge0 + k]
        return ref[edge0 + k] + ref[edge0 + 4 + k]

    def beside(r, k):
        own, minus, plus = [functools.partial(edge, ref, k) for ref in (q_ref, qm_ref, qp_ref)]
        corner = functools.partial(edge, sl_ref, k)
        if r == 0:
            right, left = jnp.where(even, own(), plus()), jnp.where(even, minus(), own())
        elif r == 1:
            right, left = jnp.where(even, plus(), corner()), jnp.where(even, own(), plus())
        else:
            right, left = jnp.where(even, minus(), own()), jnp.where(even, corner(), minus())
        return jnp.where(left_part, left, right)

    counts = []
    for r, source in enumerate((q_ref, qp_ref, qm_ref)):
        for which, ref in enumerate((rho, p1, dp1)):
            for z in range(nz):
                slab, zl = divmod(z, local_z)
                start = jnp.where(thick == slab, 0, per)
                ref[r, z] = source[start + which * local_z + zl]
            ref[r, side] = beside(r, which)
        counts.append([source[per - 1], beside(r, 3)])
    counts = narrow(counts)

    fluid_field = each(fluid_of, read(rho))
    ym = {0: fluid_field}
    ym[1], ym[-1] = y_both(fluid_field)
    xy = {(0, dy): ym[dy] for dy in ym}
    for dy in ym:
        xy[(1, dy)], xy[(-1, dy)] = x_both(ym[dy])
    for i in range(1, 19):
        there = xy[(CX[i], CY[i])]
        if CZ[i]:
            there = z_shift(there, CZ[i])
        for r in range(ROW_TILES):
            for u in range(units):
                blk[i - 1, r, u] = 1.0 - fluid_field[r][u] * there[r][u]

    def store_gradient(ref, first, field):
        for k, part in enumerate(gradient(field)):
            for r in range(ROW_TILES):
                for u in range(units):
                    ref[first + k, r, u] = part[r][u] * (1.0 / 12.0)

    store_gradient(g1, 0, read(p1))
    store_gradient(dg, 0, read(dp1))
    across = {}
    for r in range(ROW_TILES):
        for u in range(units):
            dens, psi = rho[r, u], p1[r, u]
            fluid = fluid_of(dens)
            red = 0.5 * dens * (1.0 + psi)
            blue = 0.5 * dens * (1.0 - psi)
            alpha = red / (dens + (1.0 - fluid))
            beta = RECOLOURING_PACE * alpha * blue
            g = [g1[k, r, u] for k in range(3)]
            gd = [dg[k, r, u] for k in range(3)]
            gg, n = norm_parts(g)
            gdg = dot(g, gd)
            n2g = n * n * gdg
            dn = -n * n2g
            q = (SURFACE_TENSION * fluid) * n
            dq = -q * n2g
            sq, dsq = squares(g), squares_dot(g, gd)
            base = dens - q * gg * (1.0 / 3.0)
            dbase = (dq * gg + 2.0 * q * gdg) * (-1.0 / 3.0)
            ev = even_part(base, [q * v for v in sq])
            dev = even_part(dbase, [dq * v + q * d for v, d in zip(sq, dsq)])
            bn, bdn = beta * n, beta * dn
            od = odd_part([bn * v for v in g])
            dod = odd_part([bdn * v + bn * d for v, d in zip(g, gd)])
            for k in range(9):
                t_st[k, r, u] = ev[k]
                dt_st[k, r, u] = dev[k]
            pop[0, r, u] = 12.0 * base
            dpop[0, r, u] = 12.0 * dbase
            s = [None] + [blk[i, r, u] for i in range(18)]
            for first, rest, evens, odds in (
                (0, 12.0 * base, ev, od), (9, 12.0 * dbase, dev, dod)
            ):
                scaled = [alpha * v for v in evens]
                values = [alpha * rest]
                stay = []
                for k in range(9):
                    values += [scaled[k] + odds[k], scaled[k] - odds[k]]
                    stay += [s[2 * k + 1] * values[-2], s[2 * k + 2] * values[-1]]
                scatter_groups(acc.at[pl.ds(first, 9)], r, u, values, total(stay))
        for ref in (t_st, dt_st):
            for k in range(9):
                if CY[2 * k + 1]:
                    across[ref is t_st, k, r] = y_both([[ref[k, r, u] for u in range(units)]])

    for ref, store in ((t_st, pop), (dt_st, dpop)):
        for k in range(9):
            i = 2 * k + 1
            field = read(ref.at[k])
            ahead, behind = field, field
            if CY[i]:
                shifted = [across[ref is t_st, k, r] for r in range(ROW_TILES)]
                ahead, behind = [[pair[j][0] for pair in shifted] for j in (0, 1)]
                if CY[i] == -1:
                    ahead, behind = behind, ahead
            if CX[i]:
                ahead, behind = x_shift(ahead, CX[i]), x_shift(behind, -CX[i])
            if CZ[i]:
                ahead = z_shift(ahead, CZ[i], fill=False)
                behind = z_shift(behind, -CZ[i], fill=False)
            for r in range(ROW_TILES):
                for u in range(units):
                    here = field[r][u]
                    pop_i = jnp.where(blk[i, r, u] > 0.5, here, behind[r][u])
                    pop_o = jnp.where(blk[i - 1, r, u] > 0.5, here, ahead[r][u])
                    store[i, r, u] = pop_i
                    store[i + 1, r, u] = pop_o
    red_sum = gathered_sum(acc, 0)
    dred_sum = gathered_sum(acc, 9)
    for r in range(ROW_TILES):
        for u in range(units):
            fluid = fluid_of(rho[r, u])
            dens = total([pop[i, r, u] for i in range(19)]) * (1.0 / 36.0)
            ddens = total([dpop[i, r, u] for i in range(19)]) * (1.0 / 36.0)
            scale = fluid * (1.0 / 36.0)
            red = red_sum[r][u] * scale
            dred = dred_sum[r][u] * scale
            inv = 1.0 / (dens + (1.0 - fluid))
            psi = (2.0 * red - dens) * inv
            dpsi = (2.0 * dred - (1.0 + psi) * ddens) * inv
            for k, v in enumerate((dens, ddens, red, dred, inv, psi)):
                mac[k, r, u] = v
            p2[r, u] = jnp.where(fluid > 0.5, psi, p1[r, u])
            dp2[r, u] = jnp.where(fluid > 0.5, dpsi, dp1[r, u])

    store_gradient(g2, 0, read(p2))
    store_gradient(dg, 0, read(dp2))
    for r in range(ROW_TILES):
        for u in range(units):
            dens, ddens, red, dred, inv = [mac[k, r, u] for k in range(5)]
            fluid = fluid_of(rho[r, u])
            t = [pop[i, r, u] for i in range(19)]
            dt = [dpop[i, r, u] for i in range(19)]
            m = [v * (1.0 / 36.0) for v in first_moment(t)]
            dm = [v * (1.0 / 36.0) for v in first_moment(dt)]
            vel = [inv * v for v in m]
            shrink = inv * ddens
            dvel = [inv * b - shrink * a for a, b in zip(vel, dm)]
            g = [g2[k, r, u] for k in range(3)]
            gd = [dg[k, r, u] for k in range(3)]
            gg, n = norm_parts(g)
            gdg = dot(g, gd)
            n2g = n * n * gdg
            dn = -n * n2g
            q = (SURFACE_TENSION * fluid) * n
            dq = -q * n2g
            base = RELAX_RATE * dens - (1.5 * RELAX_RATE) * dot(m, vel) - q * gg * (1.0 / 3.0)
            dbase = (
                RELAX_RATE * ddens
                - (1.5 * RELAX_RATE) * (dot(dm, vel) + dot(m, dvel))
                + (dq * gg + 2.0 * q * gdg) * (-1.0 / 3.0)
            )
            lin = odd_part([(3.0 * RELAX_RATE) * v for v in m])
            dlin = odd_part([(3.0 * RELAX_RATE) * v for v in dm])
            mq = [(4.5 * RELAX_RATE) * v for v in m]
            dmq = [(4.5 * RELAX_RATE) * v for v in dm]
            order = ((0, 0), (1, 1), (2, 2), (0, 1), (0, 2), (1, 2))
            sq, dsq = squares(g), squares_dot(g, gd)
            quad, dquad = [], []
            for k, (a, b) in enumerate(order):
                flow = mq[a] * vel[b]
                dflow = dmq[a] * vel[b] + mq[a] * dvel[b]
                if a != b:
                    flow = 2.0 * flow
                    dflow = 2.0 * dflow
                quad.append(flow + q * sq[k])
                dquad.append(dflow + dq * sq[k] + q * dsq[k])
            ev, dev = even_part(base, quad), even_part(dbase, dquad)
            keep = 1.0 - RELAX_RATE
            after, dafter = [keep * t[0] + 12.0 * base], [keep * dt[0] + 12.0 * dbase]
            for k in range(9):
                after += [keep * t[2 * k + 1] + (ev[k] + lin[k]), keep * t[2 * k + 2] + (ev[k] - lin[k])]
                dafter += [
                    keep * dt[2 * k + 1] + (dev[k] + dlin[k]),
                    keep * dt[2 * k + 2] + (dev[k] - dlin[k]),
                ]
            alpha = red * inv
            dalpha = dred * inv - alpha * shrink
            blue, dblue = dens - red, ddens - dred
            beta = RECOLOURING_PACE * alpha * blue
            dbeta = RECOLOURING_PACE * (dalpha * blue + alpha * dblue)
            bn = beta * n
            dbn = dbeta * n + beta * dn
            od = odd_part([bn * v for v in g])
            dod = odd_part([dbn * v + bn * d for v, d in zip(g, gd)])
            reds, dreds = [alpha * after[0]], [dalpha * after[0] + alpha * dafter[0]]
            for i in range(1, 19):
                k = (i - 1) // 2
                side = od[k] if i % 2 else -od[k]
                dside = dod[k] if i % 2 else -dod[k]
                reds.append(alpha * after[i] + side)
                dreds.append(dalpha * after[i] + alpha * dafter[i] + dside)
            s = [None] + [blk[i, r, u] for i in range(18)]
            for k, values in enumerate((reds, dreds, after, dafter)):
                stay = total([s[i] * values[i] for i in range(1, 19)])
                scatter_groups(acc.at[pl.ds(9 * k, 9)], r, u, values, stay)

    red_s = gathered_sum(acc, 0, narrow)
    dred_s = gathered_sum(acc, 9, narrow)
    dens_s = gathered_sum(acc, 18, narrow)
    ddens_s = gathered_sum(acc, 27, narrow)
    rho_n = read_narrow(rho)
    seeds = []
    for r in range(2):
        found, pulls = [], []
        for u in range(units):
            fluid = fluid_of(rho_n[r][u])
            scale = fluid * (1.0 / 36.0)
            dens = dens_s[r][u] * scale
            inv = 1.0 / (dens + (1.0 - fluid))
            psi = (2.0 * (red_s[r][u] * scale) - dens) * inv
            a = 2.0 * (scale * inv)
            b = -(scale * inv) * (1.0 + psi)
            pulls.append((a, b))
            found.append(a * dred_s[r][u] + b * ddens_s[r][u])
        column = total(found[:-1])
        if r == 0:
            read_ref[...] = jnp.take_along_axis(column, map_ref[...], axis=1)
        beside_sum = found[-1] + turn(found[-1], GROUP)
        beside_sum = beside_sum + turn(beside_sum, 2 * GROUP)
        seed = [column * counts[r][0]] * nz + [beside_sum * counts[r][1]]
        for u in range(units):
            a3[r, u] = pulls[u][0] * seed[u]
            b3[r, u] = pulls[u][1] * seed[u]

    def pick(ref, k, r, u):
        if r == 0:
            return ref[k, 0, u]
        return jnp.where(rows() < 4, ref[k, 1, u], ref[k, 2, u])

    ahead_r = all_moved(read(a3))
    ahead_t = all_moved(read(b3))
    for r in range(2):
        for u in range(units):
            own_r, own_t = a3[r, u], b3[r, u]
            dens, red, inv = [pick(mac, k, r, u) for k in (0, 2, 4)]
            fluid = fluid_of(rho_n[r][u])
            alpha = red * inv
            blue = dens - red
            beta = RECOLOURING_PACE * alpha * blue
            r_hat, hat = [own_r], [own_t + alpha * own_r]
            for i in range(1, 19):
                blocked = pick(blk, i - 1, r, u) > 0.5
                r_i = jnp.where(blocked, own_r, ahead_r[i][r][u])
                t_i = jnp.where(blocked, own_t, ahead_t[i][r][u])
                r_hat.append(r_i)
                hat.append(t_i + alpha * r_i)
            t = [pick(pop, i, r, u) for i in range(19)]
            m = [v * (1.0 / 36.0) for v in first_moment(t)]
            vel = [inv * v for v in m]
            g = [pick(g2, k, r, u) for k in range(3)]
            _, n = norm_parts(g)
            q = (SURFACE_TENSION * fluid) * n
            h0, h2 = weighted_even(hat[0], pair_sums(hat))
            h1 = weighted_first(hat)
            k0, k2 = weighted_even(r_hat[0], pair_sums(r_hat))
            k1 = weighted_first(r_hat)
            bars, n_gk = toward_gradient(g, fluid, h0, h2, k1, beta)
            for k in range(3):
                gbar[k, r, u] = bars[k]
            uu = 1.5 * RELAX_RATE
            flow = [(4.5 * RELAX_RATE) * k2[j] - (uu * k0 if j < 3 else 0.0) for j in range(6)]
            surf = [k2[j] - (k0 * (1.0 / 3.0) if j < 3 else 0.0) for j in range(6)]
            alpha_bar = (
                (1.0 - RELAX_RATE) * total([a * b for a, b in zip(r_hat, t)])
                + RELAX_RATE * dens * k0
                + (3.0 * RELAX_RATE) * dot(m, k1)
                + dot(m, times(flow, vel))
                + q * dot(g, times(surf, g))
            )
            alpha_bar = alpha_bar + RECOLOURING_PACE * blue * n_gk
            blue_bar = RECOLOURING_PACE * alpha * n_gk
            flow_h = [(4.5 * RELAX_RATE) * h2[j] - (uu * h0 if j < 3 else 0.0) for j in range(6)]
            xu = times(flow_h, vel)
            red_bar = inv * alpha_bar - blue_bar
            dens_bar = RELAX_RATE * h0 - dot(vel, xu) + blue_bar - alpha * inv * alpha_bar
            adj[19, r, u] = red_bar
            adj[20, r, u] = dens_bar
            for k in range(3):
                adj[21 + k, r, u] = ((3.0 * RELAX_RATE) * h1[k] + 2.0 * xu[k]) * (1.0 / 36.0)
            for i in range(19):
                adj[i, r, u] = hat[i]

    field = gradient_back(*[read(gbar.at[k]) for k in range(3)])
    ahead = {i: [] for i in range(1, 19)}
    for r in range(2):
        for u in range(units):
            fluid = fluid_of(rho_n[r][u])
            inv, psi = pick(mac, 4, r, u), pick(mac, 5, r, u)
            bar = field[r][u] * (-1.0 / 12.0)
            if r == 0 and u < nz:
                pbar2[u] = bar
            psi_bar = fluid * bar * inv
            red_bar = adj[19, r, u] + 2.0 * psi_bar
            dens_bar = (adj[20, r, u] - (1.0 + psi) * psi_bar) * (1.0 / 36.0)
            pull = [adj[21 + k, r, u] for k in range(3)]
            push = pull + odd_part(pull)[3:]
            keep = 1.0 - RELAX_RATE
            adj[19, r, u] = red_bar * (1.0 / 36.0)
            adj[0, r, u] = keep * adj[0, r, u] + dens_bar
            for k in range(9):
                adj[2 * k + 1, r, u] = keep * adj[2 * k + 1, r, u] + (dens_bar + push[k])
                adj[2 * k + 2, r, u] = keep * adj[2 * k + 2, r, u] + (dens_bar - push[k])
        for i in range(1, 19):
            tiles = [[adj[i, r, u] for u in range(units)]]
            ahead[i] += y_shift(tiles, CY[i]) if CY[i] else tiles

    ahead_r = all_moved(read(adj.at[19]))
    ahead = {i: moved_by(ahead[i], CZ[i], CX[i]) for i in range(1, 19)}
    for r in range(2):
        for u in range(units):
            dens = rho_n[r][u]
            psi = jnp.where(rows() < 4, p1[1, u], p1[2, u]) if r else p1[0, u]
            fluid = fluid_of(dens)
            red = 0.5 * dens * (1.0 + psi)
            blue = 0.5 * dens * (1.0 - psi)
            alpha = red / (dens + (1.0 - fluid))
            beta = RECOLOURING_PACE * alpha * blue
            own = adj[19, r, u]
            r_hat, hat = [own], [adj[0, r, u] + alpha * own]
            for i in range(1, 19):
                blocked = pick(blk, i - 1, r, u) > 0.5
                r_i = jnp.where(blocked, own, ahead_r[i][r][u])
                r_hat.append(r_i)
                hat.append(
                    jnp.where(blocked, adj[OPPOSITE[i], r, u], ahead[i][r][u]) + alpha * r_i
                )
            h0, h2 = weighted_even(hat[0], pair_sums(hat))
            g = [pick(g1, k, r, u) for k in range(3)]
            bars, _ = toward_gradient(g, fluid, h0, h2, weighted_first(r_hat), beta)
            for k in range(3):
                gbar[k, r, u] = bars[k]

    field = gradient_back(*[read(gbar.at[k]) for k in range(3)])
    result = []
    for z in range(nz):
        bar = pbar2[z] + field[0][z] * (-1.0 / 12.0)
        result.append(jnp.where(rho[0, z] == 0.0, bar, 0.0))
    for zl in range(local_z):
        chosen = result[zl]
        for slab in range(1, nz // local_z):
            chosen = jnp.where(thick == slab, result[slab * local_z + zl], chosen)
        out_ref[zl] = chosen


def pack_kernel(nz, local_z, solid_ref, labels_ref, density_ref, wet_ref, dir_ref, map_ref,
                out_ref, edge_ref):
    thick = lax.axis_index("thick")
    lane = lanes()
    place = places()
    spot = place & (GROUP - 1)
    source = jnp.where(spot > GROUP // 2, HALF + GROUP // 2 - spot, GROUP // 2 - spot)
    zero = jnp.zeros((8, HALF), jnp.float32)
    edges = [zero, zero, zero]

    def ends(tile):
        return jnp.take_along_axis(tile, source, axis=1)

    for zl in range(local_z):
        solid = solid_ref[zl].astype(jnp.float32)
        label = labels_ref[zl].astype(jnp.float32)
        fluid = 1.0 - solid
        red = density_ref[zl] * label * fluid
        blue = density_ref[zl] * (1.0 - label) * fluid
        psi = (red - blue) / (red + blue + solid)
        values = (red + blue, fluid * psi + solid * wet_ref[zl], solid * dir_ref[zl])
        for k, value in enumerate(values):
            out_ref[k * local_z + zl] = value
            here = (place // GROUP) == thick * local_z + zl
            edges[k] = jnp.where(here, ends(value), edges[k])
    pixels = map_ref[...]
    counts = jnp.zeros(pixels.shape, jnp.int32)
    for k in range(pixels.shape[1]):
        counts = counts + (turn(pixels, k) == lane).astype(jnp.int32)
    counts = counts.astype(jnp.float32)
    out_ref[3 * local_z] = counts
    for k, tile in enumerate(edges + [ends(counts)]):
        edge_ref[k] = tile


def one_exchange(solid, labels, density, wettability, direction, pixel_map):
    local_z = solid.shape[0]
    planes, slabs = lax.axis_size("plane"), lax.axis_size("thick")
    nz = local_z * slabs
    per = 3 * local_z + 1
    vmem = pl.BlockSpec(memory_space=pltpu.VMEM)
    packed, edges = pl.pallas_call(
        functools.partial(pack_kernel, nz, local_z),
        out_shape=(
            jax.ShapeDtypeStruct((per, 8, HALF), jnp.float32),
            jax.ShapeDtypeStruct((4, 8, HALF), jnp.float32),
        ),
        in_specs=[vmem] * 6,
        out_specs=(vmem, vmem),
    )(solid[:, 0], labels[:, 0], density[:, 0], wettability[:, 0], direction[:, 0], pixel_map[0])

    def send(array, target):
        route = []
        for b in range(planes):
            for t in range(slabs):
                to_b, to_t = target(b, t)
                route.append((b * slabs + t, (to_b % planes) * slabs + to_t))
        return lax.ppermute(array, ("plane", "thick"), route)

    beside_z = send(packed, lambda b, t: (b, 1 - t))
    beside_y = send(edges, lambda b, t: (b ^ 1, t))
    beside_zy = send(edges, lambda b, t: (b ^ 1, 1 - t))
    quad = jnp.concatenate([packed, beside_z, beside_y, beside_zy])
    above = send(quad, lambda b, t: (b + 2, t))
    below = send(quad, lambda b, t: (b - 2, t))
    corner = send(quad, lambda b, t: (b + 4 if b % 2 == 0 else b - 4, t))

    def field(*lead, tiles=ROW_TILES):
        return pltpu.VMEM(lead + (tiles, nz + 1, 8, HALF), jnp.float32)

    return pl.pallas_call(
        functools.partial(main_kernel, nz, local_z),
        out_shape=(
            jax.ShapeDtypeStruct((local_z, 8, HALF), jnp.float32),
            jax.ShapeDtypeStruct((8, HALF), jnp.float32),
        ),
        in_specs=[vmem] * 5,
        out_specs=(vmem, vmem),
        scratch_shapes=[
            field(), field(), field(), field(18), field(9), field(9), field(36),
            field(19), field(19), field(6), field(), field(), field(3), field(3), field(3),
            field(tiles=2), field(tiles=2), field(24, tiles=2), field(3, tiles=2),
            pltpu.VMEM((nz, 8, HALF), jnp.float32),
        ],
        compiler_params=pltpu.CompilerParams(vmem_limit_bytes=24 * 1024 * 1024),
    )(below, corner, above, quad, pixel_map[0])


def fits_one_exchange(mesh, solid):
    sizes = (mesh.shape["plane"], mesh.shape["thick"])
    return sizes == (2 * NBX, 2) and solid.shape[2:] == (8, HALF) and solid.shape[0] * GROUP == HALF


def solution(mesh):
    specs = (P("thick", "plane", None, None),) * 5 + (P("plane", None, None),)
    out_specs = (P("thick", "plane", None, None), P("plane", None, None))

    def program(solid, *rest):
        def with_bricks(*blocks):
            curvature, readings = one_exchange(*blocks)
            return curvature[:, None], readings[None]

        body = with_bricks if fits_one_exchange(mesh, solid) else per_device
        return jax.shard_map(
            body, mesh=mesh, in_specs=specs, out_specs=out_specs, check_vma=False
        )(solid, *rest)

    return program
```

```python
import functools

import jax
import jax.numpy as jnp
import numpy as np
from jax import lax
from jax.experimental import pallas as pl
from jax.experimental.pallas import tpu as pltpu
from jax.sharding import PartitionSpec as P

NBX = 8
STEPS = 2


VELOCITIES = np.array(
    [
        [0, 0, 0],
        [1, 0, 0],
        [-1, 0, 0],
        [0, 1, 0],
        [0, -1, 0],
        [0, 0, 1],
        [0, 0, -1],
        [1, 1, 0],
        [-1, -1, 0],
        [1, -1, 0],
        [-1, 1, 0],
        [1, 0, 1],
        [-1, 0, -1],
        [1, 0, -1],
        [-1, 0, 1],
        [0, 1, 1],
        [0, -1, -1],
        [0, 1, -1],
        [0, -1, 1],
    ]
)
WEIGHTS = np.array([1.0 / 3.0] + [1.0 / 18.0] * 6 + [1.0 / 36.0] * 12)
OPPOSITE = [int(np.argmin(np.abs(VELOCITIES + lattice_vec).sum(1))) for lattice_vec in VELOCITIES]
RELAX_RATE = 1.25
SURFACE_TENSION = 0.2
RECOLOURING_PACE = 0.7


def shifted(array, axis, by):
    devices = lax.axis_size(axis)
    pairs = [(i, i + by) for i in range(devices) if 0 <= i + by < devices]
    return lax.ppermute(array, axis, pairs)


def from_behind(block, axis, distance):
    devices = range(lax.axis_size(axis))
    route = [((i - distance) % len(devices), i) for i in devices]
    return lax.ppermute(block, axis, route)


def weights_like(array):
    return jnp.asarray(WEIGHTS, jnp.float32).reshape((19,) + (1,) * (array.ndim - 1))


def collide(red_pop, blue_pop, gradient, solid_cell):
    lattice_vel = jnp.asarray(VELOCITIES, jnp.float32)
    weight_column_vec = weights_like(red_pop)
    red_density_total = jnp.sum(red_pop, 0)
    blue_density_total = jnp.sum(blue_pop, 0)
    density = red_density_total + blue_density_total
    reciprocal_value = 1.0 / (density + solid_cell)
    total_pop = red_pop + blue_pop
    velocity = (
        jnp.einsum("qd,q...->d...", lattice_vel, total_pop, precision=lax.Precision.HIGHEST)
        * reciprocal_value
    )
    projected = jnp.einsum("qd,d...->q...", lattice_vel, velocity, precision=lax.Precision.HIGHEST)
    speed_sq = jnp.sum(velocity * velocity, 0)
    equilibrium = (
        weight_column_vec
        * density
        * (1.0 + 3.0 * projected + 4.5 * projected * projected - 1.5 * speed_sq)
    )
    relaxed_populations = total_pop + RELAX_RATE * (equilibrium - total_pop)
    along_gradient_dir = jnp.einsum(
        "qd,d...->q...", lattice_vel, gradient, precision=lax.Precision.HIGHEST
    )
    grad_sq = jnp.sum(gradient * gradient, 0)
    norm_scale_factor = 1.0 / jnp.sqrt(1.0 + grad_sq)
    relaxed_populations = (
        relaxed_populations
        + SURFACE_TENSION
        * weight_column_vec
        * (along_gradient_dir * along_gradient_dir - grad_sq / 3.0)
        * norm_scale_factor
    )
    red_output_pop = (
        red_density_total * reciprocal_value * relaxed_populations
        + RECOLOURING_PACE
        * red_density_total
        * blue_density_total
        * reciprocal_value
        * weight_column_vec
        * along_gradient_dir
        * norm_scale_factor
    )
    return (red_output_pop, relaxed_populations - red_output_pop)


def phase_of(red_pop, blue_pop, solid_cell):
    red_density_total = jnp.sum(red_pop, 0)
    blue_density_total = jnp.sum(blue_pop, 0)
    return (red_density_total - blue_density_total) / (
        red_density_total + blue_density_total + solid_cell
    )


def pull_from(padded, offset, extent):
    shift_z, shift_x, shift_y = (int(offset[0]), int(offset[1]), int(offset[2]))
    return padded[
        ...,
        1 - shift_z : 1 - shift_z + extent[0],
        1 - shift_x : 1 - shift_x + extent[1],
        1 - shift_y : 1 - shift_y + extent[2],
    ]


def gradient_of(padded, extent):
    components = [0.0, 0.0, 0.0]
    for number in range(1, 19):
        lattice_vec = VELOCITIES[number]
        pulled = pull_from(padded, -lattice_vec, extent)
        for axis_num in range(3):
            if lattice_vec[axis_num] != 0:
                components[axis_num] = (
                    components[axis_num]
                    + 3.0 * WEIGHTS[number] * float(lattice_vec[axis_num]) * pulled
                )
    return jnp.stack(components)


def spread_back(padded_bar, extent):
    total_bar = 0.0
    for number in range(1, 19):
        lattice_vec = VELOCITIES[number]
        for axis_num in range(3):
            if lattice_vec[axis_num] != 0:
                total_bar = total_bar + 3.0 * WEIGHTS[number] * float(
                    lattice_vec[axis_num]
                ) * pull_from(padded_bar[axis_num], lattice_vec, extent)
    return total_bar


def stream(padded_pop, local_pop, padded_fluid, fluid_cell, extent):
    outgoing = []
    for number in range(19):
        lattice_vec = VELOCITIES[number]
        source_fluid = pull_from(padded_fluid, lattice_vec, extent)
        arrived = pull_from(padded_pop[number], lattice_vec, extent)
        outgoing.append(
            fluid_cell
            * (source_fluid * arrived + (1.0 - source_fluid) * local_pop[OPPOSITE[number]])
        )
    return jnp.stack(outgoing)


def unstream(padded_bar, local_bar, padded_fluid, fluid_cell, extent):
    incoming = []
    for number in range(19):
        lattice_vec = VELOCITIES[number]
        ahead_fluid = pull_from(padded_fluid, -lattice_vec, extent)
        ahead_bar = pull_from(padded_bar[number], -lattice_vec, extent)
        incoming.append(fluid_cell * ahead_bar + (1.0 - ahead_fluid) * local_bar[OPPOSITE[number]])
    return jnp.stack(incoming)


def fill_border(received, chosen, channels):
    if len(chosen) == channels:
        return received
    return (
        jnp.zeros((channels,) + received.shape[1:], received.dtype)
        .at[np.array(chosen)]
        .set(received)
    )


def grow(stacked, axis_dim, chosen_low, chosen_high, sender):
    length = stacked.shape[axis_dim]
    channels = stacked.shape[0]
    borders = []
    for toward in (1, -1):
        chosen = chosen_low if toward == 1 else chosen_high
        source = length - 1 if toward == 1 else 0
        outer_layer = lax.slice_in_dim(stacked, source, source + 1, axis=axis_dim)
        if len(chosen) < channels:
            outer_layer = outer_layer[np.array(chosen)]
        borders.append(fill_border(sender(outer_layer, toward), chosen, channels))
    return jnp.concatenate([borders[0], stacked, borders[1]], axis_dim)


def per_device(solid, labels, density, wettability, direction, pixel_map):
    solid_cell = solid[:, 0].astype(jnp.float32)
    fluid_cell = 1.0 - solid_cell
    label_cell = labels[:, 0].astype(jnp.float32)
    density_cell = density[:, 0]
    wetting = wettability[:, 0]
    tangent = direction[:, 0]
    column_map = pixel_map[0]
    extent = solid_cell.shape
    bricks_y = lax.axis_size("plane") // NBX

    def extend(stacked):
        channels = stacked.shape[0]

        def chosen_for():
            return list(range(channels))

        stacked = grow(
            stacked,
            1,
            chosen_for(),
            chosen_for(),
            lambda outgoing, toward: shifted(outgoing, "thick", toward),
        )
        stacked = grow(
            stacked,
            2,
            chosen_for(),
            chosen_for(),
            lambda outgoing, toward: from_behind(outgoing, "plane", toward * bricks_y),
        )
        stacked = grow(
            stacked,
            3,
            chosen_for(),
            chosen_for(),
            lambda outgoing, toward: from_behind(outgoing, "plane", toward),
        )
        return stacked

    def phase_pair(red_in, blue_in):
        return phase_of(red_in, blue_in, solid_cell)

    def collide_local(red_in, blue_in, gradient):
        return collide(red_in, blue_in, gradient, solid_cell)

    padded_fluid = extend(fluid_cell[None])[0]
    weight_column_vec = weights_like(solid_cell[None])
    red_pop = weight_column_vec * (density_cell * label_cell * fluid_cell)[None]
    blue_pop = weight_column_vec * (density_cell * (1.0 - label_cell) * fluid_cell)[None]
    red_tan = jnp.zeros_like(red_pop)
    blue_tan = jnp.zeros_like(blue_pop)
    checkpoints = []
    for number in range(STEPS):
        phase_val, phase_tan = jax.jvp(phase_pair, (red_pop, blue_pop), (red_tan, blue_tan))
        phase_field = fluid_cell * phase_val + solid_cell * wetting
        field_tan = fluid_cell * phase_tan + solid_cell * tangent
        padded = extend(jnp.stack([phase_field, field_tan]))
        gradient = gradient_of(padded[0], extent)
        gradient_tan = gradient_of(padded[1], extent)
        checkpoints.append((red_pop, blue_pop, gradient))
        (red_post, blue_post), (red_dot, blue_dot) = jax.jvp(
            collide_local, (red_pop, blue_pop, gradient), (red_tan, blue_tan, gradient_tan)
        )
        posted = jnp.concatenate([red_post, blue_post, red_dot, blue_dot])
        moved = extend(posted)
        red_pop, blue_pop, red_tan, blue_tan = [
            stream(
                moved[19 * group : 19 * group + 19],
                posted[19 * group : 19 * group + 19],
                padded_fluid,
                fluid_cell,
                extent,
            )
            for group in range(4)
        ]
    _, phase_tan = jax.jvp(phase_pair, (red_pop, blue_pop), (red_tan, blue_tan))
    partial_sum = jnp.sum(fluid_cell * phase_tan, 0)
    column_sum = lax.psum(partial_sum, "thick")
    found = jnp.take_along_axis(column_sum, column_map, axis=1)
    row_ids = jnp.arange(column_map.shape[0])[:, None]
    seeded = jnp.zeros_like(column_sum).at[row_ids, column_map].add(found)
    _, phase_back = jax.vjp(phase_pair, red_pop, blue_pop)
    red_bar, blue_bar = phase_back(fluid_cell * seeded[None])
    wetting_bar = jnp.zeros_like(wetting)
    for number in reversed(range(STEPS)):
        red_saved, blue_saved, gradient = checkpoints[number]
        outgoing_bar = jnp.concatenate([red_bar, blue_bar]) * fluid_cell
        padded = extend(outgoing_bar)
        red_pre = unstream(padded[:19], outgoing_bar[:19], padded_fluid, fluid_cell, extent)
        blue_pre = unstream(padded[19:], outgoing_bar[19:], padded_fluid, fluid_cell, extent)
        _, collide_back = jax.vjp(collide_local, red_saved, blue_saved, gradient)
        red_bar, blue_bar, gradient_bar = collide_back((red_pre, blue_pre))
        padded_bar = extend(gradient_bar)
        field_bar = spread_back(padded_bar, extent)
        wetting_bar = wetting_bar + solid_cell * field_bar
        if number > 0:
            _, phase_back = jax.vjp(phase_pair, red_saved, blue_saved)
            extra_red, extra_blue = phase_back(fluid_cell * field_bar)
            red_bar = red_bar + extra_red
            blue_bar = blue_bar + extra_blue
    return (wetting_bar[:, None], found[None])


HALF = 128
GROUP = 32
ROW_TILES = 3
ROW_SLOTS = 120
CZ = [int(v[0]) for v in VELOCITIES]
CX = [int(v[1]) for v in VELOCITIES]
CY = [int(v[2]) for v in VELOCITIES]
GROUPS = [(gx, gy) for gx in (-1, 0, 1) for gy in (-1, 0, 1)]


def lanes():
    return lax.broadcasted_iota(jnp.int32, (8, HALF), 1)


def places():
    return (lanes() + GROUP // 2) & (HALF - 1)


def rows():
    return lax.broadcasted_iota(jnp.int32, (8, HALF), 0)


def turn(tile, by):
    by = by % HALF
    return pltpu.roll(tile, by, 1) if by else tile


def each(function, *fields):
    return [[function(*tiles) for tiles in zip(*units)] for units in zip(*fields)]


def add(a, b):
    return a + b


def sub(a, b):
    return a - b


def read(ref):
    return [[ref[r, u] for u in range(ref.shape[1])] for r in range(ref.shape[0])]


def narrow(field):
    near = rows() < 4
    return [field[0], [jnp.where(near, a, b) for a, b in zip(field[1], field[2])]]


def read_narrow(ref):
    return narrow(read(ref))


def z_shift(field, dz, fill=True):
    out = []
    for units in field:
        layers, side = units[:-1], units[-1]
        zero = jnp.zeros((8, HALF), jnp.float32)
        moved = layers[1:] + [zero] if dz == 1 else [zero] + layers[:-1]
        side = turn(side, -GROUP * dz)
        if fill:
            inside = places() < HALF - GROUP if dz == 1 else places() >= GROUP
            side = jnp.where(inside, side, 0.0)
        out.append(moved + [side])
    return out


class RowSpace:
    ref, used = None, 0

    @classmethod
    def start(cls, ref):
        cls.ref, cls.used = ref, 0

    @classmethod
    def put(cls, field):
        slot, cls.used = cls.used, cls.used + 1
        if len(field) == ROW_TILES:
            order = (2, 0, 1)
        else:
            order = (1, 0, 1)
        for u in range(len(field[0])):
            for k, r in enumerate(order):
                cls.ref[slot, u, 8 * (k + 1) : 8 * (k + 2), :] = field[r][u]
        return slot

    @classmethod
    def get(cls, slot, count, units, dx):
        if count == ROW_TILES:
            order = (2, 3, 1)
        else:
            order = (2, 1 if dx == 1 else 3)
        return [
            [cls.ref[slot, u, 8 * k + dx : 8 * (k + 1) + dx, :] for u in range(units)]
            for k in order
        ]


def x_shift(field, dx):
    return RowSpace.get(RowSpace.put(field), len(field), len(field[0]), dx)


def y_ends(units):
    layers, side = units[:-1], units[-1]
    place = places()
    beyond, ends = [], None
    for z, tile in enumerate(layers):
        beyond.append(turn(side, -(GROUP * z + 1)))
        turned = turn(tile, GROUP * z + 1)
        ends = turned if ends is None else jnp.where(place >= GROUP * z, turned, ends)
    return beyond, ends


def y_step(units, ready, dy):
    beyond, ends = ready
    at_end = lanes() == (HALF - 1 if dy == 1 else 0)
    at_side = (places() & (GROUP - 1)) == (GROUP // 2 + 1 if dy == 1 else GROUP // 2)
    out = [jnp.where(at_end, b, turn(t, -dy)) for t, b in zip(units, beyond)]
    return out + [jnp.where(at_side, ends, turn(units[-1], dy))]


def y_shift(field, dy):
    return [y_step(units, y_ends(units), dy) for units in field]


def y_both(field):
    ready = [y_ends(units) for units in field]
    return tuple([y_step(u, e, dy) for u, e in zip(field, ready)] for dy in (1, -1))


def x_both(field):
    slot = RowSpace.put(field)
    return tuple(RowSpace.get(slot, len(field), len(field[0]), dx) for dx in (1, -1))


def z_both(field):
    return z_shift(field, 1), z_shift(field, -1)


def gradient(field):
    two = each(lambda m, u, d: 2.0 * m + (u + d), field, *z_both(field))
    y_up, y_down = y_both(field)
    y_sum, y_slope = each(add, y_up, y_down), each(sub, y_up, y_down)
    x_sum = each(add, *x_both(field))
    along_x = each(sub, *x_both(each(add, two, y_sum)))
    flat = each(lambda m, a, b: 2.0 * m + (a + b), field, x_sum, y_sum)
    along_z = each(sub, *z_both(flat))
    along_y = each(
        lambda m, a, b, c, d: 2.0 * m + ((a + b) + (c + d)),
        y_slope, *z_both(y_slope), *x_both(y_slope),
    )
    return along_z, along_x, along_y


def gradient_back(gz, gx, gy):
    dx, dz = each(sub, *x_both(gx)), each(sub, *z_both(gz))
    level = each(
        lambda a, b, c, d, e, f: 2.0 * (a + b) + ((c + d) + (e + f)),
        dx, dz, *z_both(dx), *x_both(dz),
    )
    across = each(add, dx, dz)
    along = each(
        lambda m, a, b, c, d: 2.0 * m + ((a + b) + (c + d)), gy, *z_both(gy), *x_both(gy)
    )
    ahead = y_shift(each(add, across, along), 1)
    behind = y_shift(each(sub, across, along), -1)
    return each(lambda a, b, c: a + (b + c), level, ahead, behind)


def all_moved(field):
    ym = {0: field}
    ym[1], ym[-1] = y_both(field)
    xy = {(0, dy): ym[dy] for dy in ym}
    for dy in ym:
        xy[(1, dy)], xy[(-1, dy)] = x_both(ym[dy])
    out = []
    for i in range(19):
        moved = xy[(CX[i], CY[i])]
        out.append(z_shift(moved, CZ[i], fill=False) if CZ[i] else moved)
    return out


def moved_by(field, dz, dx):
    if dx:
        field = x_shift(field, dx)
    if dz:
        field = z_shift(field, dz, fill=False)
    return field


def even_part(base, quad):
    zz, xx, yy, zx, zy, xy = quad
    out = [2.0 * (base + zz), 2.0 * (base + xx), 2.0 * (base + yy)]
    for diagonal, cross in ((zz + xx, zx), (zz + yy, zy), (xx + yy, xy)):
        flat = base + diagonal
        out += [flat + cross, flat - cross]
    return out


def odd_part(vector):
    z, x, y = vector
    return [2.0 * z, 2.0 * x, 2.0 * y, z + x, z - x, z + y, z - y, x + y, x - y]


def squares(vector):
    z, x, y = vector
    return [z * z, x * x, y * y, 2.0 * (z * x), 2.0 * (z * y), 2.0 * (x * y)]


def squares_dot(a, b):
    az, ax, ay = a
    bz, bx, by = b
    return [
        2.0 * (az * bz),
        2.0 * (ax * bx),
        2.0 * (ay * by),
        2.0 * (az * bx + ax * bz),
        2.0 * (az * by + ay * bz),
        2.0 * (ax * by + ay * bx),
    ]


def dot(a, b):
    return a[0] * b[0] + a[1] * b[1] + a[2] * b[2]


def first_moment(values):
    d = [values[2 * p + 1] - values[2 * p + 2] for p in range(9)]
    return (
        d[0] + (d[3] + d[4]) + (d[5] + d[6]),
        d[1] + (d[3] - d[4]) + (d[7] + d[8]),
        d[2] + (d[5] - d[6]) + (d[7] - d[8]),
    )


def weighted_first(values):
    d = [values[2 * p + 1] - values[2 * p + 2] for p in range(9)]
    return (
        2.0 * d[0] + (d[3] + d[4]) + (d[5] + d[6]),
        2.0 * d[1] + (d[3] - d[4]) + (d[7] + d[8]),
        2.0 * d[2] + (d[5] - d[6]) + (d[7] - d[8]),
    )


def weighted_even(rest, pairs):
    axis = [2.0 * pairs[0], 2.0 * pairs[1], 2.0 * pairs[2]]
    zx, zy, xy = pairs[3] + pairs[4], pairs[5] + pairs[6], pairs[7] + pairs[8]
    second = [
        axis[0] + zx + zy,
        axis[1] + zx + xy,
        axis[2] + zy + xy,
        pairs[3] - pairs[4],
        pairs[5] - pairs[6],
        pairs[7] - pairs[8],
    ]
    zeroth = 12.0 * rest + axis[0] + axis[1] + axis[2] + zx + zy + xy
    return zeroth, second


def pair_sums(values):
    return [values[2 * p + 1] + values[2 * p + 2] for p in range(9)]


def times(matrix, vector):
    zz, xx, yy, zx, zy, xy = matrix
    z, x, y = vector
    return (zz * z + zx * x + zy * y, zx * z + xx * x + xy * y, zy * z + xy * x + yy * y)


def total(values):
    values = list(values)
    while len(values) > 1:
        values = [
            values[k] + values[k + 1] if k + 1 < len(values) else values[k]
            for k in range(0, len(values), 2)
        ]
    return values[0]


def norm_parts(g):
    g2 = dot(g, g)
    return g2, lax.rsqrt(1.0 + g2)


def fluid_of(dens):
    return jnp.where(dens == 0.0, 0.0, 1.0)


def scatter_groups(acc, r, u, values, stay):
    side = acc.shape[2] - 1
    for k, (gx, gy) in enumerate(GROUPS):
        level = {CZ[i]: values[i] for i in range(1, 19) if (CX[i], CY[i]) == (gx, gy)}
        if (gx, gy) == (0, 0):
            level[0] = values[0] + stay
        if 1 not in level:
            acc[k, r, u] = level[0]
        elif u == side:
            place = places()
            up = jnp.where(place >= GROUP, turn(level[1], GROUP), 0.0)
            down = jnp.where(place < HALF - GROUP, turn(level[-1], -GROUP), 0.0)
            acc[k, r, u] = level[0] + (up + down)
        else:
            acc[k, r, u] = acc[k, r, u] + level[0] if u else level[0]
            if u + 1 < side:
                acc[k, r, u + 1] = level[1]
            if u:
                acc[k, r, u - 1] = acc[k, r, u - 1] + level[-1]


def gathered_sum(acc, first, after_x=lambda field: field):
    by_y = []
    for gy in (-1, 0, 1):
        parts = [read(acc.at[first + GROUPS.index((0, gy))])]
        for gx in (-1, 1):
            parts.append(x_shift(read(acc.at[first + GROUPS.index((gx, gy))]), -gx))
        by_y.append(after_x(each(lambda a, b, c: a + (b + c), *parts)))
    return each(
        lambda a, b, c: b + (a + c), y_shift(by_y[0], 1), by_y[1], y_shift(by_y[2], -1)
    )


def toward_gradient(g, fluid, zeroth, second, first, beta):
    _, n = norm_parts(g)
    trace = zeroth * (1.0 / 3.0)
    shifted = [second[0] - trace, second[1] - trace, second[2] - trace] + list(second[3:])
    yg = times(shifted, g)
    gf = dot(g, first)
    nbar = (SURFACE_TENSION * fluid) * dot(g, yg) + beta * gf
    two_q = (2.0 * SURFACE_TENSION * fluid) * n
    bn = beta * n
    fall = nbar * n * n * n
    return [two_q * y + bn * f - fall * v for y, f, v in zip(yg, first, g)], n * gf


def main_kernel(nz, local_z, qp_ref, sl_ref, qm_ref, q_ref, map_ref, out_ref, read_ref,
                rho, p1, dp1, blk, t_st, dt_st, acc, pop, dpop, mac, p2, dp2, g1, g2, dg,
                a3, b3, adj, gbar, pbar2, row_space):
    RowSpace.start(row_space)
    thick = lax.axis_index("thick")
    even = lax.rem(lax.axis_index("plane"), 2) == 0
    units = nz + 1
    side = nz
    per = 3 * local_z + 1
    edge0 = 2 * per
    left_part = (places() & (GROUP - 1)) > GROUP // 2

    def edge(ref, k):
        if k == 3:
            return ref[edge0 + k]
        return ref[edge0 + k] + ref[edge0 + 4 + k]

    def beside(r, k):
        own, minus, plus = [functools.partial(edge, ref, k) for ref in (q_ref, qm_ref, qp_ref)]
        corner = functools.partial(edge, sl_ref, k)
        if r == 0:
            right, left = jnp.where(even, own(), plus()), jnp.where(even, minus(), own())
        elif r == 1:
            right, left = jnp.where(even, plus(), corner()), jnp.where(even, own(), plus())
        else:
            right, left = jnp.where(even, minus(), own()), jnp.where(even, corner(), minus())
        return jnp.where(left_part, left, right)

    counts = []
    for r, source in enumerate((q_ref, qp_ref, qm_ref)):
        for which, ref in enumerate((rho, p1, dp1)):
            for z in range(nz):
                slab, zl = divmod(z, local_z)
                start = jnp.where(thick == slab, 0, per)
                ref[r, z] = source[start + which * local_z + zl]
            ref[r, side] = beside(r, which)
        counts.append([source[per - 1], beside(r, 3)])
    counts = narrow(counts)

    fluid_field = each(fluid_of, read(rho))
    ym = {0: fluid_field}
    ym[1], ym[-1] = y_both(fluid_field)
    xy = {(0, dy): ym[dy] for dy in ym}
    for dy in ym:
        xy[(1, dy)], xy[(-1, dy)] = x_both(ym[dy])
    for i in range(1, 19):
        there = xy[(CX[i], CY[i])]
        if CZ[i]:
            there = z_shift(there, CZ[i])
        for r in range(ROW_TILES):
            for u in range(units):
                blk[i - 1, r, u] = 1.0 - fluid_field[r][u] * there[r][u]

    def store_gradient(ref, first, field):
        for k, part in enumerate(gradient(field)):
            for r in range(ROW_TILES):
                for u in range(units):
                    ref[first + k, r, u] = part[r][u] * (1.0 / 12.0)

    store_gradient(g1, 0, read(p1))
    store_gradient(dg, 0, read(dp1))
    across = {}
    for r in range(ROW_TILES):
        for u in range(units):
            dens, psi = rho[r, u], p1[r, u]
            fluid = fluid_of(dens)
            red = 0.5 * dens * (1.0 + psi)
            blue = 0.5 * dens * (1.0 - psi)
            alpha = red / (dens + (1.0 - fluid))
            beta = RECOLOURING_PACE * alpha * blue
            g = [g1[k, r, u] for k in range(3)]
            gd = [dg[k, r, u] for k in range(3)]
            gg, n = norm_parts(g)
            gdg = dot(g, gd)
            n2g = n * n * gdg
            dn = -n * n2g
            q = (SURFACE_TENSION * fluid) * n
            dq = -q * n2g
            sq, dsq = squares(g), squares_dot(g, gd)
            base = dens - q * gg * (1.0 / 3.0)
            dbase = (dq * gg + 2.0 * q * gdg) * (-1.0 / 3.0)
            ev = even_part(base, [q * v for v in sq])
            dev = even_part(dbase, [dq * v + q * d for v, d in zip(sq, dsq)])
            bn, bdn = beta * n, beta * dn
            od = odd_part([bn * v for v in g])
            dod = odd_part([bdn * v + bn * d for v, d in zip(g, gd)])
            for k in range(9):
                t_st[k, r, u] = ev[k]
                dt_st[k, r, u] = dev[k]
            pop[0, r, u] = 12.0 * base
            dpop[0, r, u] = 12.0 * dbase
            s = [None] + [blk[i, r, u] for i in range(18)]
            for first, rest, evens, odds in (
                (0, 12.0 * base, ev, od), (9, 12.0 * dbase, dev, dod)
            ):
                scaled = [alpha * v for v in evens]
                values = [alpha * rest]
                stay = []
                for k in range(9):
                    values += [scaled[k] + odds[k], scaled[k] - odds[k]]
                    stay += [s[2 * k + 1] * values[-2], s[2 * k + 2] * values[-1]]
                scatter_groups(acc.at[pl.ds(first, 9)], r, u, values, total(stay))
        for ref in (t_st, dt_st):
            for k in range(9):
                if CY[2 * k + 1]:
                    across[ref is t_st, k, r] = y_both([[ref[k, r, u] for u in range(units)]])

    for ref, store in ((t_st, pop), (dt_st, dpop)):
        for k in range(9):
            i = 2 * k + 1
            field = read(ref.at[k])
            ahead, behind = field, field
            if CY[i]:
                shifted = [across[ref is t_st, k, r] for r in range(ROW_TILES)]
                ahead, behind = [[pair[j][0] for pair in shifted] for j in (0, 1)]
                if CY[i] == -1:
                    ahead, behind = behind, ahead
            if CX[i]:
                ahead, behind = x_shift(ahead, CX[i]), x_shift(behind, -CX[i])
            if CZ[i]:
                ahead = z_shift(ahead, CZ[i], fill=False)
                behind = z_shift(behind, -CZ[i], fill=False)
            for r in range(ROW_TILES):
                for u in range(units):
                    here = field[r][u]
                    pop_i = jnp.where(blk[i, r, u] > 0.5, here, behind[r][u])
                    pop_o = jnp.where(blk[i - 1, r, u] > 0.5, here, ahead[r][u])
                    store[i, r, u] = pop_i
                    store[i + 1, r, u] = pop_o
    red_sum = gathered_sum(acc, 0)
    dred_sum = gathered_sum(acc, 9)
    for r in range(ROW_TILES):
        for u in range(units):
            fluid = fluid_of(rho[r, u])
            dens = total([pop[i, r, u] for i in range(19)]) * (1.0 / 36.0)
            ddens = total([dpop[i, r, u] for i in range(19)]) * (1.0 / 36.0)
            scale = fluid * (1.0 / 36.0)
            red = red_sum[r][u] * scale
            dred = dred_sum[r][u] * scale
            inv = 1.0 / (dens + (1.0 - fluid))
            psi = (2.0 * red - dens) * inv
            dpsi = (2.0 * dred - (1.0 + psi) * ddens) * inv
            for k, v in enumerate((dens, ddens, red, dred, inv, psi)):
                mac[k, r, u] = v
            p2[r, u] = jnp.where(fluid > 0.5, psi, p1[r, u])
            dp2[r, u] = jnp.where(fluid > 0.5, dpsi, dp1[r, u])

    store_gradient(g2, 0, read(p2))
    store_gradient(dg, 0, read(dp2))
    for r in range(ROW_TILES):
        for u in range(units):
            dens, ddens, red, dred, inv = [mac[k, r, u] for k in range(5)]
            fluid = fluid_of(rho[r, u])
            t = [pop[i, r, u] for i in range(19)]
            dt = [dpop[i, r, u] for i in range(19)]
            m = [v * (1.0 / 36.0) for v in first_moment(t)]
            dm = [v * (1.0 / 36.0) for v in first_moment(dt)]
            vel = [inv * v for v in m]
            shrink = inv * ddens
            dvel = [inv * b - shrink * a for a, b in zip(vel, dm)]
            g = [g2[k, r, u] for k in range(3)]
            gd = [dg[k, r, u] for k in range(3)]
            gg, n = norm_parts(g)
            gdg = dot(g, gd)
            n2g = n * n * gdg
            dn = -n * n2g
            q = (SURFACE_TENSION * fluid) * n
            dq = -q * n2g
            base = RELAX_RATE * dens - (1.5 * RELAX_RATE) * dot(m, vel) - q * gg * (1.0 / 3.0)
            dbase = (
                RELAX_RATE * ddens
                - (1.5 * RELAX_RATE) * (dot(dm, vel) + dot(m, dvel))
                + (dq * gg + 2.0 * q * gdg) * (-1.0 / 3.0)
            )
            lin = odd_part([(3.0 * RELAX_RATE) * v for v in m])
            dlin = odd_part([(3.0 * RELAX_RATE) * v for v in dm])
            mq = [(4.5 * RELAX_RATE) * v for v in m]
            dmq = [(4.5 * RELAX_RATE) * v for v in dm]
            order = ((0, 0), (1, 1), (2, 2), (0, 1), (0, 2), (1, 2))
            sq, dsq = squares(g), squares_dot(g, gd)
            quad, dquad = [], []
            for k, (a, b) in enumerate(order):
                flow = mq[a] * vel[b]
                dflow = dmq[a] * vel[b] + mq[a] * dvel[b]
                if a != b:
                    flow = 2.0 * flow
                    dflow = 2.0 * dflow
                quad.append(flow + q * sq[k])
                dquad.append(dflow + dq * sq[k] + q * dsq[k])
            ev, dev = even_part(base, quad), even_part(dbase, dquad)
            keep = 1.0 - RELAX_RATE
            after, dafter = [keep * t[0] + 12.0 * base], [keep * dt[0] + 12.0 * dbase]
            for k in range(9):
                after += [keep * t[2 * k + 1] + (ev[k] + lin[k]), keep * t[2 * k + 2] + (ev[k] - lin[k])]
                dafter += [
                    keep * dt[2 * k + 1] + (dev[k] + dlin[k]),
                    keep * dt[2 * k + 2] + (dev[k] - dlin[k]),
                ]
            alpha = red * inv
            dalpha = dred * inv - alpha * shrink
            blue, dblue = dens - red, ddens - dred
            beta = RECOLOURING_PACE * alpha * blue
            dbeta = RECOLOURING_PACE * (dalpha * blue + alpha * dblue)
            bn = beta * n
            dbn = dbeta * n + beta * dn
            od = odd_part([bn * v for v in g])
            dod = odd_part([dbn * v + bn * d for v, d in zip(g, gd)])
            reds, dreds = [alpha * after[0]], [dalpha * after[0] + alpha * dafter[0]]
            for i in range(1, 19):
                k = (i - 1) // 2
                side = od[k] if i % 2 else -od[k]
                dside = dod[k] if i % 2 else -dod[k]
                reds.append(alpha * after[i] + side)
                dreds.append(dalpha * after[i] + alpha * dafter[i] + dside)
            s = [None] + [blk[i, r, u] for i in range(18)]
            for k, values in enumerate((reds, dreds, after, dafter)):
                stay = total([s[i] * values[i] for i in range(1, 19)])
                scatter_groups(acc.at[pl.ds(9 * k, 9)], r, u, values, stay)

    red_s = gathered_sum(acc, 0, narrow)
    dred_s = gathered_sum(acc, 9, narrow)
    dens_s = gathered_sum(acc, 18, narrow)
    ddens_s = gathered_sum(acc, 27, narrow)
    rho_n = read_narrow(rho)
    seeds = []
    for r in range(2):
        found, pulls = [], []
        for u in range(units):
            fluid = fluid_of(rho_n[r][u])
            scale = fluid * (1.0 / 36.0)
            dens = dens_s[r][u] * scale
            inv = 1.0 / (dens + (1.0 - fluid))
            psi = (2.0 * (red_s[r][u] * scale) - dens) * inv
            a = 2.0 * (scale * inv)
            b = -(scale * inv) * (1.0 + psi)
            pulls.append((a, b))
            found.append(a * dred_s[r][u] + b * ddens_s[r][u])
        column = total(found[:-1])
        if r == 0:
            read_ref[...] = jnp.take_along_axis(column, map_ref[...], axis=1)
        beside_sum = found[-1] + turn(found[-1], GROUP)
        beside_sum = beside_sum + turn(beside_sum, 2 * GROUP)
        seed = [column * counts[r][0]] * nz + [beside_sum * counts[r][1]]
        for u in range(units):
            a3[r, u] = pulls[u][0] * seed[u]
            b3[r, u] = pulls[u][1] * seed[u]

    def pick(ref, k, r, u):
        if r == 0:
            return ref[k, 0, u]
        return jnp.where(rows() < 4, ref[k, 1, u], ref[k, 2, u])

    ahead_r = all_moved(read(a3))
    ahead_t = all_moved(read(b3))
    for r in range(2):
        for u in range(units):
            own_r, own_t = a3[r, u], b3[r, u]
            dens, red, inv = [pick(mac, k, r, u) for k in (0, 2, 4)]
            fluid = fluid_of(rho_n[r][u])
            alpha = red * inv
            blue = dens - red
            beta = RECOLOURING_PACE * alpha * blue
            r_hat, hat = [own_r], [own_t + alpha * own_r]
            for i in range(1, 19):
                blocked = pick(blk, i - 1, r, u) > 0.5
                r_i = jnp.where(blocked, own_r, ahead_r[i][r][u])
                t_i = jnp.where(blocked, own_t, ahead_t[i][r][u])
                r_hat.append(r_i)
                hat.append(t_i + alpha * r_i)
            t = [pick(pop, i, r, u) for i in range(19)]
            m = [v * (1.0 / 36.0) for v in first_moment(t)]
            vel = [inv * v for v in m]
            g = [pick(g2, k, r, u) for k in range(3)]
            _, n = norm_parts(g)
            q = (SURFACE_TENSION * fluid) * n
            h0, h2 = weighted_even(hat[0], pair_sums(hat))
            h1 = weighted_first(hat)
            k0, k2 = weighted_even(r_hat[0], pair_sums(r_hat))
            k1 = weighted_first(r_hat)
            bars, n_gk = toward_gradient(g, fluid, h0, h2, k1, beta)
            for k in range(3):
                gbar[k, r, u] = bars[k]
            uu = 1.5 * RELAX_RATE
            flow = [(4.5 * RELAX_RATE) * k2[j] - (uu * k0 if j < 3 else 0.0) for j in range(6)]
            surf = [k2[j] - (k0 * (1.0 / 3.0) if j < 3 else 0.0) for j in range(6)]
            alpha_bar = (
                (1.0 - RELAX_RATE) * total([a * b for a, b in zip(r_hat, t)])
                + RELAX_RATE * dens * k0
                + (3.0 * RELAX_RATE) * dot(m, k1)
                + dot(m, times(flow, vel))
                + q * dot(g, times(surf, g))
            )
            alpha_bar = alpha_bar + RECOLOURING_PACE * blue * n_gk
            blue_bar = RECOLOURING_PACE * alpha * n_gk
            flow_h = [(4.5 * RELAX_RATE) * h2[j] - (uu * h0 if j < 3 else 0.0) for j in range(6)]
            xu = times(flow_h, vel)
            red_bar = inv * alpha_bar - blue_bar
            dens_bar = RELAX_RATE * h0 - dot(vel, xu) + blue_bar - alpha * inv * alpha_bar
            adj[19, r, u] = red_bar
            adj[20, r, u] = dens_bar
            for k in range(3):
                adj[21 + k, r, u] = ((3.0 * RELAX_RATE) * h1[k] + 2.0 * xu[k]) * (1.0 / 36.0)
            for i in range(19):
                adj[i, r, u] = hat[i]

    field = gradient_back(*[read(gbar.at[k]) for k in range(3)])
    ahead = {i: [] for i in range(1, 19)}
    for r in range(2):
        for u in range(units):
            fluid = fluid_of(rho_n[r][u])
            inv, psi = pick(mac, 4, r, u), pick(mac, 5, r, u)
            bar = field[r][u] * (-1.0 / 12.0)
            if r == 0 and u < nz:
                pbar2[u] = bar
            psi_bar = fluid * bar * inv
            red_bar = adj[19, r, u] + 2.0 * psi_bar
            dens_bar = (adj[20, r, u] - (1.0 + psi) * psi_bar) * (1.0 / 36.0)
            pull = [adj[21 + k, r, u] for k in range(3)]
            push = pull + odd_part(pull)[3:]
            keep = 1.0 - RELAX_RATE
            adj[19, r, u] = red_bar * (1.0 / 36.0)
            adj[0, r, u] = keep * adj[0, r, u] + dens_bar
            for k in range(9):
                adj[2 * k + 1, r, u] = keep * adj[2 * k + 1, r, u] + (dens_bar + push[k])
                adj[2 * k + 2, r, u] = keep * adj[2 * k + 2, r, u] + (dens_bar - push[k])
        for i in range(1, 19):
            tiles = [[adj[i, r, u] for u in range(units)]]
            ahead[i] += y_shift(tiles, CY[i]) if CY[i] else tiles

    ahead_r = all_moved(read(adj.at[19]))
    ahead = {i: moved_by(ahead[i], CZ[i], CX[i]) for i in range(1, 19)}
    for r in range(2):
        for u in range(units):
            dens = rho_n[r][u]
            psi = jnp.where(rows() < 4, p1[1, u], p1[2, u]) if r else p1[0, u]
            fluid = fluid_of(dens)
            red = 0.5 * dens * (1.0 + psi)
            blue = 0.5 * dens * (1.0 - psi)
            alpha = red / (dens + (1.0 - fluid))
            beta = RECOLOURING_PACE * alpha * blue
            own = adj[19, r, u]
            r_hat, hat = [own], [adj[0, r, u] + alpha * own]
            for i in range(1, 19):
                blocked = pick(blk, i - 1, r, u) > 0.5
                r_i = jnp.where(blocked, own, ahead_r[i][r][u])
                r_hat.append(r_i)
                hat.append(
                    jnp.where(blocked, adj[OPPOSITE[i], r, u], ahead[i][r][u]) + alpha * r_i
                )
            h0, h2 = weighted_even(hat[0], pair_sums(hat))
            g = [pick(g1, k, r, u) for k in range(3)]
            bars, _ = toward_gradient(g, fluid, h0, h2, weighted_first(r_hat), beta)
            for k in range(3):
                gbar[k, r, u] = bars[k]

    field = gradient_back(*[read(gbar.at[k]) for k in range(3)])
    result = []
    for z in range(nz):
        bar = pbar2[z] + field[0][z] * (-1.0 / 12.0)
        result.append(jnp.where(rho[0, z] == 0.0, bar, 0.0))
    for zl in range(local_z):
        chosen = result[zl]
        for slab in range(1, nz // local_z):
            chosen = jnp.where(thick == slab, result[slab * local_z + zl], chosen)
        out_ref[zl] = chosen


def pack_kernel(nz, local_z, solid_ref, labels_ref, density_ref, wet_ref, dir_ref, map_ref,
                out_ref, edge_ref):
    thick = lax.axis_index("thick")
    lane = lanes()
    place = places()
    spot = place & (GROUP - 1)
    source = jnp.where(spot > GROUP // 2, HALF + GROUP // 2 - spot, GROUP // 2 - spot)
    zero = jnp.zeros((8, HALF), jnp.float32)
    edges = [zero, zero, zero]

    def ends(tile):
        return jnp.take_along_axis(tile, source, axis=1)

    for zl in range(local_z):
        solid = solid_ref[zl].astype(jnp.float32)
        label = labels_ref[zl].astype(jnp.float32)
        fluid = 1.0 - solid
        red = density_ref[zl] * label * fluid
        blue = density_ref[zl] * (1.0 - label) * fluid
        psi = (red - blue) / (red + blue + solid)
        values = (red + blue, fluid * psi + solid * wet_ref[zl], solid * dir_ref[zl])
        for k, value in enumerate(values):
            out_ref[k * local_z + zl] = value
            here = (place // GROUP) == thick * local_z + zl
            edges[k] = jnp.where(here, ends(value), edges[k])
    pixels = map_ref[...]
    counts = jnp.zeros(pixels.shape, jnp.int32)
    for k in range(pixels.shape[1]):
        counts = counts + (turn(pixels, k) == lane).astype(jnp.int32)
    counts = counts.astype(jnp.float32)
    out_ref[3 * local_z] = counts
    for k, tile in enumerate(edges + [ends(counts)]):
        edge_ref[k] = tile


def one_exchange(solid, labels, density, wettability, direction, pixel_map):
    local_z = solid.shape[0]
    planes, slabs = lax.axis_size("plane"), lax.axis_size("thick")
    nz = local_z * slabs
    per = 3 * local_z + 1
    vmem = pl.BlockSpec(memory_space=pltpu.VMEM)
    packed, edges = pl.pallas_call(
        functools.partial(pack_kernel, nz, local_z),
        out_shape=(
            jax.ShapeDtypeStruct((per, 8, HALF), jnp.float32),
            jax.ShapeDtypeStruct((4, 8, HALF), jnp.float32),
        ),
        in_specs=[vmem] * 6,
        out_specs=(vmem, vmem),
    )(solid[:, 0], labels[:, 0], density[:, 0], wettability[:, 0], direction[:, 0], pixel_map[0])

    def send(array, target):
        route = []
        for b in range(planes):
            for t in range(slabs):
                to_b, to_t = target(b, t)
                route.append((b * slabs + t, (to_b % planes) * slabs + to_t))
        return lax.ppermute(array, ("plane", "thick"), route)

    beside_z = send(packed, lambda b, t: (b, 1 - t))
    beside_y = send(edges, lambda b, t: (b ^ 1, t))
    beside_zy = send(edges, lambda b, t: (b ^ 1, 1 - t))
    quad = jnp.concatenate([packed, beside_z, beside_y, beside_zy])
    above = send(quad, lambda b, t: (b + 2, t))
    below = send(quad, lambda b, t: (b - 2, t))
    corner = send(quad, lambda b, t: (b + 4 if b % 2 == 0 else b - 4, t))

    def field(*lead, tiles=ROW_TILES):
        return pltpu.VMEM(lead + (tiles, nz + 1, 8, HALF), jnp.float32)

    return pl.pallas_call(
        functools.partial(main_kernel, nz, local_z),
        out_shape=(
            jax.ShapeDtypeStruct((local_z, 8, HALF), jnp.float32),
            jax.ShapeDtypeStruct((8, HALF), jnp.float32),
        ),
        in_specs=[vmem] * 5,
        out_specs=(vmem, vmem),
        scratch_shapes=[
            field(), field(), field(), field(18), field(9), field(9), field(36),
            field(19), field(19), field(6), field(), field(), field(3), field(3), field(3),
            field(tiles=2), field(tiles=2), field(24, tiles=2), field(3, tiles=2),
            pltpu.VMEM((nz, 8, HALF), jnp.float32),
            pltpu.VMEM((ROW_SLOTS, nz + 1, 8 * (ROW_TILES + 2), HALF), jnp.float32),
        ],
        compiler_params=pltpu.CompilerParams(vmem_limit_bytes=32 * 1024 * 1024),
    )(below, corner, above, quad, pixel_map[0])


def fits_one_exchange(mesh, solid):
    sizes = (mesh.shape["plane"], mesh.shape["thick"])
    return sizes == (2 * NBX, 2) and solid.shape[2:] == (8, HALF) and solid.shape[0] * GROUP == HALF


def solution(mesh):
    specs = (P("thick", "plane", None, None),) * 5 + (P("plane", None, None),)
    out_specs = (P("thick", "plane", None, None), P("plane", None, None))

    def program(solid, *rest):
        def with_bricks(*blocks):
            curvature, readings = one_exchange(*blocks)
            return curvature[:, None], readings[None]

        body = with_bricks if fits_one_exchange(mesh, solid) else per_device
        return jax.shard_map(
            body, mesh=mesh, in_specs=specs, out_specs=out_specs, check_vma=False
        )(solid, *rest)

    return program
```

```python
import functools

import jax
import jax.numpy as jnp
import numpy as np
from jax import lax
from jax.experimental import pallas as pl
from jax.experimental.pallas import tpu as pltpu
from jax.sharding import PartitionSpec as P

NBX = 8
STEPS = 2


VELOCITIES = np.array(
    [
        [0, 0, 0],
        [1, 0, 0],
        [-1, 0, 0],
        [0, 1, 0],
        [0, -1, 0],
        [0, 0, 1],
        [0, 0, -1],
        [1, 1, 0],
        [-1, -1, 0],
        [1, -1, 0],
        [-1, 1, 0],
        [1, 0, 1],
        [-1, 0, -1],
        [1, 0, -1],
        [-1, 0, 1],
        [0, 1, 1],
        [0, -1, -1],
        [0, 1, -1],
        [0, -1, 1],
    ]
)
WEIGHTS = np.array([1.0 / 3.0] + [1.0 / 18.0] * 6 + [1.0 / 36.0] * 12)
OPPOSITE = [int(np.argmin(np.abs(VELOCITIES + lattice_vec).sum(1))) for lattice_vec in VELOCITIES]
RELAX_RATE = 1.25
SURFACE_TENSION = 0.2
RECOLOURING_PACE = 0.7


def shifted(array, axis, by):
    devices = lax.axis_size(axis)
    pairs = [(i, i + by) for i in range(devices) if 0 <= i + by < devices]
    return lax.ppermute(array, axis, pairs)


def from_behind(block, axis, distance):
    devices = range(lax.axis_size(axis))
    route = [((i - distance) % len(devices), i) for i in devices]
    return lax.ppermute(block, axis, route)


def weights_like(array):
    return jnp.asarray(WEIGHTS, jnp.float32).reshape((19,) + (1,) * (array.ndim - 1))


def collide(red_pop, blue_pop, gradient, solid_cell):
    lattice_vel = jnp.asarray(VELOCITIES, jnp.float32)
    weight_column_vec = weights_like(red_pop)
    red_density_total = jnp.sum(red_pop, 0)
    blue_density_total = jnp.sum(blue_pop, 0)
    density = red_density_total + blue_density_total
    reciprocal_value = 1.0 / (density + solid_cell)
    total_pop = red_pop + blue_pop
    velocity = (
        jnp.einsum("qd,q...->d...", lattice_vel, total_pop, precision=lax.Precision.HIGHEST)
        * reciprocal_value
    )
    projected = jnp.einsum("qd,d...->q...", lattice_vel, velocity, precision=lax.Precision.HIGHEST)
    speed_sq = jnp.sum(velocity * velocity, 0)
    equilibrium = (
        weight_column_vec
        * density
        * (1.0 + 3.0 * projected + 4.5 * projected * projected - 1.5 * speed_sq)
    )
    relaxed_populations = total_pop + RELAX_RATE * (equilibrium - total_pop)
    along_gradient_dir = jnp.einsum(
        "qd,d...->q...", lattice_vel, gradient, precision=lax.Precision.HIGHEST
    )
    grad_sq = jnp.sum(gradient * gradient, 0)
    norm_scale_factor = 1.0 / jnp.sqrt(1.0 + grad_sq)
    relaxed_populations = (
        relaxed_populations
        + SURFACE_TENSION
        * weight_column_vec
        * (along_gradient_dir * along_gradient_dir - grad_sq / 3.0)
        * norm_scale_factor
    )
    red_output_pop = (
        red_density_total * reciprocal_value * relaxed_populations
        + RECOLOURING_PACE
        * red_density_total
        * blue_density_total
        * reciprocal_value
        * weight_column_vec
        * along_gradient_dir
        * norm_scale_factor
    )
    return (red_output_pop, relaxed_populations - red_output_pop)


def phase_of(red_pop, blue_pop, solid_cell):
    red_density_total = jnp.sum(red_pop, 0)
    blue_density_total = jnp.sum(blue_pop, 0)
    return (red_density_total - blue_density_total) / (
        red_density_total + blue_density_total + solid_cell
    )


def pull_from(padded, offset, extent):
    shift_z, shift_x, shift_y = (int(offset[0]), int(offset[1]), int(offset[2]))
    return padded[
        ...,
        1 - shift_z : 1 - shift_z + extent[0],
        1 - shift_x : 1 - shift_x + extent[1],
        1 - shift_y : 1 - shift_y + extent[2],
    ]


def gradient_of(padded, extent):
    components = [0.0, 0.0, 0.0]
    for number in range(1, 19):
        lattice_vec = VELOCITIES[number]
        pulled = pull_from(padded, -lattice_vec, extent)
        for axis_num in range(3):
            if lattice_vec[axis_num] != 0:
                components[axis_num] = (
                    components[axis_num]
                    + 3.0 * WEIGHTS[number] * float(lattice_vec[axis_num]) * pulled
                )
    return jnp.stack(components)


def spread_back(padded_bar, extent):
    total_bar = 0.0
    for number in range(1, 19):
        lattice_vec = VELOCITIES[number]
        for axis_num in range(3):
            if lattice_vec[axis_num] != 0:
                total_bar = total_bar + 3.0 * WEIGHTS[number] * float(
                    lattice_vec[axis_num]
                ) * pull_from(padded_bar[axis_num], lattice_vec, extent)
    return total_bar


def stream(padded_pop, local_pop, padded_fluid, fluid_cell, extent):
    outgoing = []
    for number in range(19):
        lattice_vec = VELOCITIES[number]
        source_fluid = pull_from(padded_fluid, lattice_vec, extent)
        arrived = pull_from(padded_pop[number], lattice_vec, extent)
        outgoing.append(
            fluid_cell
            * (source_fluid * arrived + (1.0 - source_fluid) * local_pop[OPPOSITE[number]])
        )
    return jnp.stack(outgoing)


def unstream(padded_bar, local_bar, padded_fluid, fluid_cell, extent):
    incoming = []
    for number in range(19):
        lattice_vec = VELOCITIES[number]
        ahead_fluid = pull_from(padded_fluid, -lattice_vec, extent)
        ahead_bar = pull_from(padded_bar[number], -lattice_vec, extent)
        incoming.append(fluid_cell * ahead_bar + (1.0 - ahead_fluid) * local_bar[OPPOSITE[number]])
    return jnp.stack(incoming)


def fill_border(received, chosen, channels):
    if len(chosen) == channels:
        return received
    return (
        jnp.zeros((channels,) + received.shape[1:], received.dtype)
        .at[np.array(chosen)]
        .set(received)
    )


def grow(stacked, axis_dim, chosen_low, chosen_high, sender):
    length = stacked.shape[axis_dim]
    channels = stacked.shape[0]
    borders = []
    for toward in (1, -1):
        chosen = chosen_low if toward == 1 else chosen_high
        source = length - 1 if toward == 1 else 0
        outer_layer = lax.slice_in_dim(stacked, source, source + 1, axis=axis_dim)
        if len(chosen) < channels:
            outer_layer = outer_layer[np.array(chosen)]
        borders.append(fill_border(sender(outer_layer, toward), chosen, channels))
    return jnp.concatenate([borders[0], stacked, borders[1]], axis_dim)


def per_device(solid, labels, density, wettability, direction, pixel_map):
    solid_cell = solid[:, 0].astype(jnp.float32)
    fluid_cell = 1.0 - solid_cell
    label_cell = labels[:, 0].astype(jnp.float32)
    density_cell = density[:, 0]
    wetting = wettability[:, 0]
    tangent = direction[:, 0]
    column_map = pixel_map[0]
    extent = solid_cell.shape
    bricks_y = lax.axis_size("plane") // NBX

    def extend(stacked):
        channels = stacked.shape[0]

        def chosen_for():
            return list(range(channels))

        stacked = grow(
            stacked,
            1,
            chosen_for(),
            chosen_for(),
            lambda outgoing, toward: shifted(outgoing, "thick", toward),
        )
        stacked = grow(
            stacked,
            2,
            chosen_for(),
            chosen_for(),
            lambda outgoing, toward: from_behind(outgoing, "plane", toward * bricks_y),
        )
        stacked = grow(
            stacked,
            3,
            chosen_for(),
            chosen_for(),
            lambda outgoing, toward: from_behind(outgoing, "plane", toward),
        )
        return stacked

    def phase_pair(red_in, blue_in):
        return phase_of(red_in, blue_in, solid_cell)

    def collide_local(red_in, blue_in, gradient):
        return collide(red_in, blue_in, gradient, solid_cell)

    padded_fluid = extend(fluid_cell[None])[0]
    weight_column_vec = weights_like(solid_cell[None])
    red_pop = weight_column_vec * (density_cell * label_cell * fluid_cell)[None]
    blue_pop = weight_column_vec * (density_cell * (1.0 - label_cell) * fluid_cell)[None]
    red_tan = jnp.zeros_like(red_pop)
    blue_tan = jnp.zeros_like(blue_pop)
    checkpoints = []
    for number in range(STEPS):
        phase_val, phase_tan = jax.jvp(phase_pair, (red_pop, blue_pop), (red_tan, blue_tan))
        phase_field = fluid_cell * phase_val + solid_cell * wetting
        field_tan = fluid_cell * phase_tan + solid_cell * tangent
        padded = extend(jnp.stack([phase_field, field_tan]))
        gradient = gradient_of(padded[0], extent)
        gradient_tan = gradient_of(padded[1], extent)
        checkpoints.append((red_pop, blue_pop, gradient))
        (red_post, blue_post), (red_dot, blue_dot) = jax.jvp(
            collide_local, (red_pop, blue_pop, gradient), (red_tan, blue_tan, gradient_tan)
        )
        posted = jnp.concatenate([red_post, blue_post, red_dot, blue_dot])
        moved = extend(posted)
        red_pop, blue_pop, red_tan, blue_tan = [
            stream(
                moved[19 * group : 19 * group + 19],
                posted[19 * group : 19 * group + 19],
                padded_fluid,
                fluid_cell,
                extent,
            )
            for group in range(4)
        ]
    _, phase_tan = jax.jvp(phase_pair, (red_pop, blue_pop), (red_tan, blue_tan))
    partial_sum = jnp.sum(fluid_cell * phase_tan, 0)
    column_sum = lax.psum(partial_sum, "thick")
    found = jnp.take_along_axis(column_sum, column_map, axis=1)
    row_ids = jnp.arange(column_map.shape[0])[:, None]
    seeded = jnp.zeros_like(column_sum).at[row_ids, column_map].add(found)
    _, phase_back = jax.vjp(phase_pair, red_pop, blue_pop)
    red_bar, blue_bar = phase_back(fluid_cell * seeded[None])
    wetting_bar = jnp.zeros_like(wetting)
    for number in reversed(range(STEPS)):
        red_saved, blue_saved, gradient = checkpoints[number]
        outgoing_bar = jnp.concatenate([red_bar, blue_bar]) * fluid_cell
        padded = extend(outgoing_bar)
        red_pre = unstream(padded[:19], outgoing_bar[:19], padded_fluid, fluid_cell, extent)
        blue_pre = unstream(padded[19:], outgoing_bar[19:], padded_fluid, fluid_cell, extent)
        _, collide_back = jax.vjp(collide_local, red_saved, blue_saved, gradient)
        red_bar, blue_bar, gradient_bar = collide_back((red_pre, blue_pre))
        padded_bar = extend(gradient_bar)
        field_bar = spread_back(padded_bar, extent)
        wetting_bar = wetting_bar + solid_cell * field_bar
        if number > 0:
            _, phase_back = jax.vjp(phase_pair, red_saved, blue_saved)
            extra_red, extra_blue = phase_back(fluid_cell * field_bar)
            red_bar = red_bar + extra_red
            blue_bar = blue_bar + extra_blue
    return (wetting_bar[:, None], found[None])


HALF = 128
GROUP = 32
ROW_TILES = 3
ROW_SLOTS = 120
CZ = [int(v[0]) for v in VELOCITIES]
CX = [int(v[1]) for v in VELOCITIES]
CY = [int(v[2]) for v in VELOCITIES]
GROUPS = [(gx, gy) for gx in (-1, 0, 1) for gy in (-1, 0, 1)]


def lanes():
    return lax.broadcasted_iota(jnp.int32, (8, HALF), 1)


def places():
    return (lanes() + GROUP // 2) & (HALF - 1)


def rows():
    return lax.broadcasted_iota(jnp.int32, (8, HALF), 0)


def turn(tile, by):
    by = by % HALF
    return pltpu.roll(tile, by, 1) if by else tile


def each(function, *fields):
    return [[function(*tiles) for tiles in zip(*units)] for units in zip(*fields)]


def add(a, b):
    return a + b


def sub(a, b):
    return a - b


def read(ref):
    return [[ref[r, u] for u in range(ref.shape[1])] for r in range(ref.shape[0])]


def narrow(field):
    near = rows() < 4
    return [field[0], [jnp.where(near, a, b) for a, b in zip(field[1], field[2])]]


def read_narrow(ref):
    return narrow(read(ref))


def z_shift(field, dz, fill=True):
    out = []
    for units in field:
        layers, side = units[:-1], units[-1]
        zero = jnp.zeros((8, HALF), jnp.float32)
        moved = layers[1:] + [zero] if dz == 1 else [zero] + layers[:-1]
        side = turn(side, -GROUP * dz)
        if fill:
            inside = places() < HALF - GROUP if dz == 1 else places() >= GROUP
            side = jnp.where(inside, side, 0.0)
        out.append(moved + [side])
    return out


class RowSpace:
    ref, used = None, 0

    @classmethod
    def start(cls, ref):
        cls.ref, cls.used = ref, 0

    @classmethod
    def put(cls, field):
        slot, cls.used = cls.used, cls.used + 1
        if len(field) == ROW_TILES:
            order = (2, 0, 1)
        else:
            order = (1, 0, 1)
        for u in range(len(field[0])):
            for k, r in enumerate(order):
                cls.ref[slot, u, 8 * (k + 1) : 8 * (k + 2), :] = field[r][u]
        return slot

    @classmethod
    def get(cls, slot, count, units, dx):
        if count == ROW_TILES:
            order = (2, 3, 1)
        else:
            order = (2, 1 if dx == 1 else 3)
        return [
            [cls.ref[slot, u, 8 * k + dx : 8 * (k + 1) + dx, :] for u in range(units)]
            for k in order
        ]


def x_shift(field, dx):
    return RowSpace.get(RowSpace.put(field), len(field), len(field[0]), dx)


def y_ends(units):
    layers, side = units[:-1], units[-1]
    place = places()
    beyond, ends = [], None
    for z, tile in enumerate(layers):
        beyond.append(turn(side, -(GROUP * z + 1)))
        turned = turn(tile, GROUP * z + 1)
        ends = turned if ends is None else jnp.where(place >= GROUP * z, turned, ends)
    return beyond, ends


def y_step(units, ready, dy):
    beyond, ends = ready
    at_end = lanes() == (HALF - 1 if dy == 1 else 0)
    at_side = (places() & (GROUP - 1)) == (GROUP // 2 + 1 if dy == 1 else GROUP // 2)
    out = [jnp.where(at_end, b, turn(t, -dy)) for t, b in zip(units, beyond)]
    return out + [jnp.where(at_side, ends, turn(units[-1], dy))]


def y_shift(field, dy):
    return [y_step(units, y_ends(units), dy) for units in field]


def y_both(field):
    ready = [y_ends(units) for units in field]
    return tuple([y_step(u, e, dy) for u, e in zip(field, ready)] for dy in (1, -1))


def x_both(field):
    slot = RowSpace.put(field)
    return tuple(RowSpace.get(slot, len(field), len(field[0]), dx) for dx in (1, -1))


def z_both(field):
    return z_shift(field, 1), z_shift(field, -1)


def gradient(field):
    two = each(lambda m, u, d: 2.0 * m + (u + d), field, *z_both(field))
    y_up, y_down = y_both(field)
    y_sum, y_slope = each(add, y_up, y_down), each(sub, y_up, y_down)
    x_sum = each(add, *x_both(field))
    along_x = each(sub, *x_both(each(add, two, y_sum)))
    flat = each(lambda m, a, b: 2.0 * m + (a + b), field, x_sum, y_sum)
    along_z = each(sub, *z_both(flat))
    along_y = each(
        lambda m, a, b, c, d: 2.0 * m + ((a + b) + (c + d)),
        y_slope, *z_both(y_slope), *x_both(y_slope),
    )
    return along_z, along_x, along_y


def gradient_back(gz, gx, gy):
    dx, dz = each(sub, *x_both(gx)), each(sub, *z_both(gz))
    level = each(
        lambda a, b, c, d, e, f: 2.0 * (a + b) + ((c + d) + (e + f)),
        dx, dz, *z_both(dx), *x_both(dz),
    )
    across = each(add, dx, dz)
    along = each(
        lambda m, a, b, c, d: 2.0 * m + ((a + b) + (c + d)), gy, *z_both(gy), *x_both(gy)
    )
    ahead = y_shift(each(add, across, along), 1)
    behind = y_shift(each(sub, across, along), -1)
    return each(lambda a, b, c: a + (b + c), level, ahead, behind)


def all_moved(field):
    ym = {0: field}
    ym[1], ym[-1] = y_both(field)
    xy = {(0, dy): ym[dy] for dy in ym}
    for dy in ym:
        xy[(1, dy)], xy[(-1, dy)] = x_both(ym[dy])
    out = []
    for i in range(19):
        moved = xy[(CX[i], CY[i])]
        out.append(z_shift(moved, CZ[i], fill=False) if CZ[i] else moved)
    return out


def moved_by(field, dz, dx):
    if dx:
        field = x_shift(field, dx)
    if dz:
        field = z_shift(field, dz, fill=False)
    return field


def even_part(base, quad):
    zz, xx, yy, zx, zy, xy = quad
    out = [2.0 * (base + zz), 2.0 * (base + xx), 2.0 * (base + yy)]
    for diagonal, cross in ((zz + xx, zx), (zz + yy, zy), (xx + yy, xy)):
        flat = base + diagonal
        out += [flat + cross, flat - cross]
    return out


def odd_part(vector):
    z, x, y = vector
    return [2.0 * z, 2.0 * x, 2.0 * y, z + x, z - x, z + y, z - y, x + y, x - y]


def squares(vector):
    z, x, y = vector
    return [z * z, x * x, y * y, 2.0 * (z * x), 2.0 * (z * y), 2.0 * (x * y)]


def squares_dot(a, b):
    az, ax, ay = a
    bz, bx, by = b
    return [
        2.0 * (az * bz),
        2.0 * (ax * bx),
        2.0 * (ay * by),
        2.0 * (az * bx + ax * bz),
        2.0 * (az * by + ay * bz),
        2.0 * (ax * by + ay * bx),
    ]


def dot(a, b):
    return a[0] * b[0] + a[1] * b[1] + a[2] * b[2]


def first_moment(values):
    d = [values[2 * p + 1] - values[2 * p + 2] for p in range(9)]
    return (
        d[0] + (d[3] + d[4]) + (d[5] + d[6]),
        d[1] + (d[3] - d[4]) + (d[7] + d[8]),
        d[2] + (d[5] - d[6]) + (d[7] - d[8]),
    )


def weighted_first(values):
    d = [values[2 * p + 1] - values[2 * p + 2] for p in range(9)]
    return (
        2.0 * d[0] + (d[3] + d[4]) + (d[5] + d[6]),
        2.0 * d[1] + (d[3] - d[4]) + (d[7] + d[8]),
        2.0 * d[2] + (d[5] - d[6]) + (d[7] - d[8]),
    )


def weighted_even(rest, pairs):
    axis = [2.0 * pairs[0], 2.0 * pairs[1], 2.0 * pairs[2]]
    zx, zy, xy = pairs[3] + pairs[4], pairs[5] + pairs[6], pairs[7] + pairs[8]
    second = [
        axis[0] + zx + zy,
        axis[1] + zx + xy,
        axis[2] + zy + xy,
        pairs[3] - pairs[4],
        pairs[5] - pairs[6],
        pairs[7] - pairs[8],
    ]
    zeroth = 12.0 * rest + axis[0] + axis[1] + axis[2] + zx + zy + xy
    return zeroth, second


def pair_sums(values):
    return [values[2 * p + 1] + values[2 * p + 2] for p in range(9)]


def times(matrix, vector):
    zz, xx, yy, zx, zy, xy = matrix
    z, x, y = vector
    return (zz * z + zx * x + zy * y, zx * z + xx * x + xy * y, zy * z + xy * x + yy * y)


def total(values):
    values = list(values)
    while len(values) > 1:
        values = [
            values[k] + values[k + 1] if k + 1 < len(values) else values[k]
            for k in range(0, len(values), 2)
        ]
    return values[0]


def norm_parts(g):
    g2 = dot(g, g)
    return g2, lax.rsqrt(1.0 + g2)


def fluid_of(dens):
    return jnp.where(dens == 0.0, 0.0, 1.0)


def scatter_groups(acc, r, u, values, stay):
    side = acc.shape[2] - 1
    for k, (gx, gy) in enumerate(GROUPS):
        level = {CZ[i]: values[i] for i in range(1, 19) if (CX[i], CY[i]) == (gx, gy)}
        if (gx, gy) == (0, 0):
            level[0] = values[0] + stay
        if 1 not in level:
            acc[k, r, u] = level[0]
        elif u == side:
            place = places()
            up = jnp.where(place >= GROUP, turn(level[1], GROUP), 0.0)
            down = jnp.where(place < HALF - GROUP, turn(level[-1], -GROUP), 0.0)
            acc[k, r, u] = level[0] + (up + down)
        else:
            acc[k, r, u] = acc[k, r, u] + level[0] if u else level[0]
            if u + 1 < side:
                acc[k, r, u + 1] = level[1]
            if u:
                acc[k, r, u - 1] = acc[k, r, u - 1] + level[-1]


def gathered_sum(acc, first, after_x=lambda field: field):
    by_y = []
    for gy in (-1, 0, 1):
        parts = [read(acc.at[first + GROUPS.index((0, gy))])]
        for gx in (-1, 1):
            parts.append(x_shift(read(acc.at[first + GROUPS.index((gx, gy))]), -gx))
        by_y.append(after_x(each(lambda a, b, c: a + (b + c), *parts)))
    return each(
        lambda a, b, c: b + (a + c), y_shift(by_y[0], 1), by_y[1], y_shift(by_y[2], -1)
    )


def toward_gradient(g, fluid, zeroth, second, first, beta):
    _, n = norm_parts(g)
    trace = zeroth * (1.0 / 3.0)
    shifted = [second[0] - trace, second[1] - trace, second[2] - trace] + list(second[3:])
    yg = times(shifted, g)
    gf = dot(g, first)
    nbar = (SURFACE_TENSION * fluid) * dot(g, yg) + beta * gf
    two_q = (2.0 * SURFACE_TENSION * fluid) * n
    bn = beta * n
    fall = nbar * n * n * n
    return [two_q * y + bn * f - fall * v for y, f, v in zip(yg, first, g)], n * gf


def main_kernel(nz, local_z, qp_ref, sl_ref, qm_ref, q_ref, map_ref, out_ref, read_ref,
                rho, p1, dp1, blk, t_st, dt_st, acc, pop, dpop, mac, p2, dp2, g1, g2, dg,
                a3, b3, adj, gbar, pbar2, row_space):
    RowSpace.start(row_space)
    thick = lax.axis_index("thick")
    even = lax.rem(lax.axis_index("plane"), 2) == 0
    units = nz + 1
    side = nz
    per = 3 * local_z
    edge0 = 2 * per
    left_part = (places() & (GROUP - 1)) > GROUP // 2

    def edge(ref, k):
        if k == 3:
            return ref[edge0 + k]
        return ref[edge0 + k] + ref[edge0 + 4 + k]

    def beside(r, k):
        own, minus, plus = [functools.partial(edge, ref, k) for ref in (q_ref, qm_ref, qp_ref)]
        corner = functools.partial(edge, sl_ref, k)
        if r == 0:
            right, left = jnp.where(even, own(), plus()), jnp.where(even, minus(), own())
        elif r == 1:
            right, left = jnp.where(even, plus(), corner()), jnp.where(even, own(), plus())
        else:
            right, left = jnp.where(even, minus(), own()), jnp.where(even, corner(), minus())
        return jnp.where(left_part, left, right)

    counts = []
    for r, source in enumerate((q_ref, qp_ref, qm_ref)):
        for which, ref in enumerate((rho, p1, dp1)):
            for z in range(nz):
                slab, zl = divmod(z, local_z)
                start = jnp.where(thick == slab, 0, per)
                ref[r, z] = source[start + which * local_z + zl]
            ref[r, side] = beside(r, which)
        counts.append([source[edge0 + 8], beside(r, 3)])
    counts = narrow(counts)

    fluid_field = each(fluid_of, read(rho))
    ym = {0: fluid_field}
    ym[1], ym[-1] = y_both(fluid_field)
    xy = {(0, dy): ym[dy] for dy in ym}
    for dy in ym:
        xy[(1, dy)], xy[(-1, dy)] = x_both(ym[dy])
    for i in range(1, 19):
        there = xy[(CX[i], CY[i])]
        if CZ[i]:
            there = z_shift(there, CZ[i])
        for r in range(ROW_TILES):
            for u in range(units):
                blk[i - 1, r, u] = 1.0 - fluid_field[r][u] * there[r][u]

    def store_gradient(ref, first, field):
        for k, part in enumerate(gradient(field)):
            for r in range(ROW_TILES):
                for u in range(units):
                    ref[first + k, r, u] = part[r][u] * (1.0 / 12.0)

    store_gradient(g1, 0, read(p1))
    store_gradient(dg, 0, read(dp1))
    across = {}
    for r in range(ROW_TILES):
        for u in range(units):
            dens, psi = rho[r, u], p1[r, u]
            fluid = fluid_of(dens)
            red = 0.5 * dens * (1.0 + psi)
            blue = 0.5 * dens * (1.0 - psi)
            alpha = red / (dens + (1.0 - fluid))
            beta = RECOLOURING_PACE * alpha * blue
            g = [g1[k, r, u] for k in range(3)]
            gd = [dg[k, r, u] for k in range(3)]
            gg, n = norm_parts(g)
            gdg = dot(g, gd)
            n2g = n * n * gdg
            dn = -n * n2g
            q = (SURFACE_TENSION * fluid) * n
            dq = -q * n2g
            sq, dsq = squares(g), squares_dot(g, gd)
            base = dens - q * gg * (1.0 / 3.0)
            dbase = (dq * gg + 2.0 * q * gdg) * (-1.0 / 3.0)
            ev = even_part(base, [q * v for v in sq])
            dev = even_part(dbase, [dq * v + q * d for v, d in zip(sq, dsq)])
            bn, bdn = beta * n, beta * dn
            od = odd_part([bn * v for v in g])
            dod = odd_part([bdn * v + bn * d for v, d in zip(g, gd)])
            for k in range(9):
                t_st[k, r, u] = ev[k]
                dt_st[k, r, u] = dev[k]
            pop[0, r, u] = 12.0 * base
            dpop[0, r, u] = 12.0 * dbase
            s = [None] + [blk[i, r, u] for i in range(18)]
            for first, rest, evens, odds in (
                (0, 12.0 * base, ev, od), (9, 12.0 * dbase, dev, dod)
            ):
                scaled = [alpha * v for v in evens]
                values = [alpha * rest]
                stay = []
                for k in range(9):
                    values += [scaled[k] + odds[k], scaled[k] - odds[k]]
                    stay += [s[2 * k + 1] * values[-2], s[2 * k + 2] * values[-1]]
                scatter_groups(acc.at[pl.ds(first, 9)], r, u, values, total(stay))
        for ref in (t_st, dt_st):
            for k in range(9):
                if CY[2 * k + 1]:
                    across[ref is t_st, k, r] = y_both([[ref[k, r, u] for u in range(units)]])

    for ref, store in ((t_st, pop), (dt_st, dpop)):
        for k in range(9):
            i = 2 * k + 1
            field = read(ref.at[k])
            ahead, behind = field, field
            if CY[i]:
                shifted = [across[ref is t_st, k, r] for r in range(ROW_TILES)]
                ahead, behind = [[pair[j][0] for pair in shifted] for j in (0, 1)]
                if CY[i] == -1:
                    ahead, behind = behind, ahead
            if CX[i]:
                ahead, behind = x_shift(ahead, CX[i]), x_shift(behind, -CX[i])
            if CZ[i]:
                ahead = z_shift(ahead, CZ[i], fill=False)
                behind = z_shift(behind, -CZ[i], fill=False)
            for r in range(ROW_TILES):
                for u in range(units):
                    here = field[r][u]
                    pop_i = jnp.where(blk[i, r, u] > 0.5, here, behind[r][u])
                    pop_o = jnp.where(blk[i - 1, r, u] > 0.5, here, ahead[r][u])
                    store[i, r, u] = pop_i
                    store[i + 1, r, u] = pop_o
    red_sum = gathered_sum(acc, 0)
    dred_sum = gathered_sum(acc, 9)
    for r in range(ROW_TILES):
        for u in range(units):
            fluid = fluid_of(rho[r, u])
            dens = total([pop[i, r, u] for i in range(19)]) * (1.0 / 36.0)
            ddens = total([dpop[i, r, u] for i in range(19)]) * (1.0 / 36.0)
            scale = fluid * (1.0 / 36.0)
            red = red_sum[r][u] * scale
            dred = dred_sum[r][u] * scale
            inv = 1.0 / (dens + (1.0 - fluid))
            psi = (2.0 * red - dens) * inv
            dpsi = (2.0 * dred - (1.0 + psi) * ddens) * inv
            for k, v in enumerate((dens, ddens, red, dred, inv, psi)):
                mac[k, r, u] = v
            p2[r, u] = jnp.where(fluid > 0.5, psi, p1[r, u])
            dp2[r, u] = jnp.where(fluid > 0.5, dpsi, dp1[r, u])

    store_gradient(g2, 0, read(p2))
    store_gradient(dg, 0, read(dp2))
    for r in range(ROW_TILES):
        for u in range(units):
            dens, ddens, red, dred, inv = [mac[k, r, u] for k in range(5)]
            fluid = fluid_of(rho[r, u])
            t = [pop[i, r, u] for i in range(19)]
            dt = [dpop[i, r, u] for i in range(19)]
            m = [v * (1.0 / 36.0) for v in first_moment(t)]
            dm = [v * (1.0 / 36.0) for v in first_moment(dt)]
            vel = [inv * v for v in m]
            shrink = inv * ddens
            dvel = [inv * b - shrink * a for a, b in zip(vel, dm)]
            g = [g2[k, r, u] for k in range(3)]
            gd = [dg[k, r, u] for k in range(3)]
            gg, n = norm_parts(g)
            gdg = dot(g, gd)
            n2g = n * n * gdg
            dn = -n * n2g
            q = (SURFACE_TENSION * fluid) * n
            dq = -q * n2g
            base = RELAX_RATE * dens - (1.5 * RELAX_RATE) * dot(m, vel) - q * gg * (1.0 / 3.0)
            dbase = (
                RELAX_RATE * ddens
                - (1.5 * RELAX_RATE) * (dot(dm, vel) + dot(m, dvel))
                + (dq * gg + 2.0 * q * gdg) * (-1.0 / 3.0)
            )
            lin = odd_part([(3.0 * RELAX_RATE) * v for v in m])
            dlin = odd_part([(3.0 * RELAX_RATE) * v for v in dm])
            mq = [(4.5 * RELAX_RATE) * v for v in m]
            dmq = [(4.5 * RELAX_RATE) * v for v in dm]
            order = ((0, 0), (1, 1), (2, 2), (0, 1), (0, 2), (1, 2))
            sq, dsq = squares(g), squares_dot(g, gd)
            quad, dquad = [], []
            for k, (a, b) in enumerate(order):
                flow = mq[a] * vel[b]
                dflow = dmq[a] * vel[b] + mq[a] * dvel[b]
                if a != b:
                    flow = 2.0 * flow
                    dflow = 2.0 * dflow
                quad.append(flow + q * sq[k])
                dquad.append(dflow + dq * sq[k] + q * dsq[k])
            ev, dev = even_part(base, quad), even_part(dbase, dquad)
            keep = 1.0 - RELAX_RATE
            after, dafter = [keep * t[0] + 12.0 * base], [keep * dt[0] + 12.0 * dbase]
            for k in range(9):
                after += [keep * t[2 * k + 1] + (ev[k] + lin[k]), keep * t[2 * k + 2] + (ev[k] - lin[k])]
                dafter += [
                    keep * dt[2 * k + 1] + (dev[k] + dlin[k]),
                    keep * dt[2 * k + 2] + (dev[k] - dlin[k]),
                ]
            alpha = red * inv
            dalpha = dred * inv - alpha * shrink
            blue, dblue = dens - red, ddens - dred
            beta = RECOLOURING_PACE * alpha * blue
            dbeta = RECOLOURING_PACE * (dalpha * blue + alpha * dblue)
            bn = beta * n
            dbn = dbeta * n + beta * dn
            od = odd_part([bn * v for v in g])
            dod = odd_part([dbn * v + bn * d for v, d in zip(g, gd)])
            reds, dreds = [alpha * after[0]], [dalpha * after[0] + alpha * dafter[0]]
            for i in range(1, 19):
                k = (i - 1) // 2
                side = od[k] if i % 2 else -od[k]
                dside = dod[k] if i % 2 else -dod[k]
                reds.append(alpha * after[i] + side)
                dreds.append(dalpha * after[i] + alpha * dafter[i] + dside)
            s = [None] + [blk[i, r, u] for i in range(18)]
            for k, values in enumerate((reds, dreds, after, dafter)):
                stay = total([s[i] * values[i] for i in range(1, 19)])
                scatter_groups(acc.at[pl.ds(9 * k, 9)], r, u, values, stay)

    red_s = gathered_sum(acc, 0, narrow)
    dred_s = gathered_sum(acc, 9, narrow)
    dens_s = gathered_sum(acc, 18, narrow)
    ddens_s = gathered_sum(acc, 27, narrow)
    rho_n = read_narrow(rho)
    seeds = []
    for r in range(2):
        found, pulls = [], []
        for u in range(units):
            fluid = fluid_of(rho_n[r][u])
            scale = fluid * (1.0 / 36.0)
            dens = dens_s[r][u] * scale
            inv = 1.0 / (dens + (1.0 - fluid))
            psi = (2.0 * (red_s[r][u] * scale) - dens) * inv
            a = 2.0 * (scale * inv)
            b = -(scale * inv) * (1.0 + psi)
            pulls.append((a, b))
            found.append(a * dred_s[r][u] + b * ddens_s[r][u])
        column = total(found[:-1])
        if r == 0:
            read_ref[...] = jnp.take_along_axis(column, map_ref[...], axis=1)
        beside_sum = found[-1] + turn(found[-1], GROUP)
        beside_sum = beside_sum + turn(beside_sum, 2 * GROUP)
        seed = [column * counts[r][0]] * nz + [beside_sum * counts[r][1]]
        for u in range(units):
            a3[r, u] = pulls[u][0] * seed[u]
            b3[r, u] = pulls[u][1] * seed[u]

    def pick(ref, k, r, u):
        if r == 0:
            return ref[k, 0, u]
        return jnp.where(rows() < 4, ref[k, 1, u], ref[k, 2, u])

    ahead_r = all_moved(read(a3))
    ahead_t = all_moved(read(b3))
    for r in range(2):
        for u in range(units):
            own_r, own_t = a3[r, u], b3[r, u]
            dens, red, inv = [pick(mac, k, r, u) for k in (0, 2, 4)]
            fluid = fluid_of(rho_n[r][u])
            alpha = red * inv
            blue = dens - red
            beta = RECOLOURING_PACE * alpha * blue
            r_hat, hat = [own_r], [own_t + alpha * own_r]
            for i in range(1, 19):
                blocked = pick(blk, i - 1, r, u) > 0.5
                r_i = jnp.where(blocked, own_r, ahead_r[i][r][u])
                t_i = jnp.where(blocked, own_t, ahead_t[i][r][u])
                r_hat.append(r_i)
                hat.append(t_i + alpha * r_i)
            t = [pick(pop, i, r, u) for i in range(19)]
            m = [v * (1.0 / 36.0) for v in first_moment(t)]
            vel = [inv * v for v in m]
            g = [pick(g2, k, r, u) for k in range(3)]
            _, n = norm_parts(g)
            q = (SURFACE_TENSION * fluid) * n
            h0, h2 = weighted_even(hat[0], pair_sums(hat))
            h1 = weighted_first(hat)
            k0, k2 = weighted_even(r_hat[0], pair_sums(r_hat))
            k1 = weighted_first(r_hat)
            bars, n_gk = toward_gradient(g, fluid, h0, h2, k1, beta)
            for k in range(3):
                gbar[k, r, u] = bars[k]
            uu = 1.5 * RELAX_RATE
            flow = [(4.5 * RELAX_RATE) * k2[j] - (uu * k0 if j < 3 else 0.0) for j in range(6)]
            surf = [k2[j] - (k0 * (1.0 / 3.0) if j < 3 else 0.0) for j in range(6)]
            alpha_bar = (
                (1.0 - RELAX_RATE) * total([a * b for a, b in zip(r_hat, t)])
                + RELAX_RATE * dens * k0
                + (3.0 * RELAX_RATE) * dot(m, k1)
                + dot(m, times(flow, vel))
                + q * dot(g, times(surf, g))
            )
            alpha_bar = alpha_bar + RECOLOURING_PACE * blue * n_gk
            blue_bar = RECOLOURING_PACE * alpha * n_gk
            flow_h = [(4.5 * RELAX_RATE) * h2[j] - (uu * h0 if j < 3 else 0.0) for j in range(6)]
            xu = times(flow_h, vel)
            red_bar = inv * alpha_bar - blue_bar
            dens_bar = RELAX_RATE * h0 - dot(vel, xu) + blue_bar - alpha * inv * alpha_bar
            adj[19, r, u] = red_bar
            adj[20, r, u] = dens_bar
            for k in range(3):
                adj[21 + k, r, u] = ((3.0 * RELAX_RATE) * h1[k] + 2.0 * xu[k]) * (1.0 / 36.0)
            for i in range(19):
                adj[i, r, u] = hat[i]

    field = gradient_back(*[read(gbar.at[k]) for k in range(3)])
    ahead = {i: [] for i in range(1, 19)}
    for r in range(2):
        for u in range(units):
            fluid = fluid_of(rho_n[r][u])
            inv, psi = pick(mac, 4, r, u), pick(mac, 5, r, u)
            bar = field[r][u] * (-1.0 / 12.0)
            if r == 0 and u < nz:
                pbar2[u] = bar
            psi_bar = fluid * bar * inv
            red_bar = adj[19, r, u] + 2.0 * psi_bar
            dens_bar = (adj[20, r, u] - (1.0 + psi) * psi_bar) * (1.0 / 36.0)
            pull = [adj[21 + k, r, u] for k in range(3)]
            push = pull + odd_part(pull)[3:]
            keep = 1.0 - RELAX_RATE
            adj[19, r, u] = red_bar * (1.0 / 36.0)
            adj[0, r, u] = keep * adj[0, r, u] + dens_bar
            for k in range(9):
                adj[2 * k + 1, r, u] = keep * adj[2 * k + 1, r, u] + (dens_bar + push[k])
                adj[2 * k + 2, r, u] = keep * adj[2 * k + 2, r, u] + (dens_bar - push[k])
        for i in range(1, 19):
            tiles = [[adj[i, r, u] for u in range(units)]]
            ahead[i] += y_shift(tiles, CY[i]) if CY[i] else tiles

    ahead_r = all_moved(read(adj.at[19]))
    ahead = {i: moved_by(ahead[i], CZ[i], CX[i]) for i in range(1, 19)}
    for r in range(2):
        for u in range(units):
            dens = rho_n[r][u]
            psi = jnp.where(rows() < 4, p1[1, u], p1[2, u]) if r else p1[0, u]
            fluid = fluid_of(dens)
            red = 0.5 * dens * (1.0 + psi)
            blue = 0.5 * dens * (1.0 - psi)
            alpha = red / (dens + (1.0 - fluid))
            beta = RECOLOURING_PACE * alpha * blue
            own = adj[19, r, u]
            r_hat, hat = [own], [adj[0, r, u] + alpha * own]
            for i in range(1, 19):
                blocked = pick(blk, i - 1, r, u) > 0.5
                r_i = jnp.where(blocked, own, ahead_r[i][r][u])
                r_hat.append(r_i)
                hat.append(
                    jnp.where(blocked, adj[OPPOSITE[i], r, u], ahead[i][r][u]) + alpha * r_i
                )
            h0, h2 = weighted_even(hat[0], pair_sums(hat))
            g = [pick(g1, k, r, u) for k in range(3)]
            bars, _ = toward_gradient(g, fluid, h0, h2, weighted_first(r_hat), beta)
            for k in range(3):
                gbar[k, r, u] = bars[k]

    field = gradient_back(*[read(gbar.at[k]) for k in range(3)])
    result = []
    for z in range(nz):
        bar = pbar2[z] + field[0][z] * (-1.0 / 12.0)
        result.append(jnp.where(rho[0, z] == 0.0, bar, 0.0))
    for zl in range(local_z):
        chosen = result[zl]
        for slab in range(1, nz // local_z):
            chosen = jnp.where(thick == slab, result[slab * local_z + zl], chosen)
        out_ref[zl] = chosen


def edge_kernel(local_z, values_ref, map_ref, edge_ref, count_ref):
    thick = lax.axis_index("thick")
    lane = lanes()
    place = places()
    spot = place & (GROUP - 1)
    source = jnp.where(spot > GROUP // 2, HALF + GROUP // 2 - spot, GROUP // 2 - spot)

    def ends(tile):
        return jnp.take_along_axis(tile, source, axis=1)

    for k in range(3):
        edges = jnp.zeros((8, HALF), jnp.float32)
        for zl in range(local_z):
            here = (place // GROUP) == thick * local_z + zl
            edges = jnp.where(here, ends(values_ref[k * local_z + zl]), edges)
        edge_ref[k] = edges
    pixels = map_ref[...]
    counts = jnp.zeros(pixels.shape, jnp.int32)
    for k in range(pixels.shape[1]):
        counts = counts + (turn(pixels, k) == lane).astype(jnp.int32)
    counts = counts.astype(jnp.float32)
    edge_ref[3] = ends(counts)
    count_ref[0] = counts


def one_exchange(solid, labels, density, wettability, direction, pixel_map):
    local_z = solid.shape[0]
    planes, slabs = lax.axis_size("plane"), lax.axis_size("thick")
    nz = local_z * slabs
    vmem = pl.BlockSpec(memory_space=pltpu.VMEM)
    solid_cell, label = solid[:, 0].astype(jnp.float32), labels[:, 0].astype(jnp.float32)
    fluid = 1.0 - solid_cell
    red = density[:, 0] * label * fluid
    blue = density[:, 0] * (1.0 - label) * fluid
    psi = (red - blue) / (red + blue + solid_cell)
    packed = jnp.concatenate(
        [red + blue, fluid * psi + solid_cell * wettability[:, 0], solid_cell * direction[:, 0]]
    )
    edges, counts = pl.pallas_call(
        functools.partial(edge_kernel, local_z),
        out_shape=(
            jax.ShapeDtypeStruct((4, 8, HALF), jnp.float32),
            jax.ShapeDtypeStruct((1, 8, HALF), jnp.float32),
        ),
        in_specs=[vmem] * 2,
        out_specs=(vmem, vmem),
        compiler_params=pltpu.CompilerParams(vmem_limit_bytes=1024 * 1024),
    )(packed, pixel_map[0])

    def send(array, target):
        route = []
        for b in range(planes):
            for t in range(slabs):
                to_b, to_t = target(b, t)
                route.append((b * slabs + t, (to_b % planes) * slabs + to_t))
        return lax.ppermute(array, ("plane", "thick"), route)

    beside_z = send(packed, lambda b, t: (b, 1 - t))
    beside_y = send(edges, lambda b, t: (b ^ 1, t))
    beside_zy = send(edges, lambda b, t: (b ^ 1, 1 - t))
    quad = jnp.concatenate([packed, beside_z, beside_y, beside_zy, counts])
    above = send(quad, lambda b, t: (b + 2, t))
    below = send(quad, lambda b, t: (b - 2, t))
    corner = send(quad, lambda b, t: (b + 4 if b % 2 == 0 else b - 4, t))

    def field(*lead, tiles=ROW_TILES):
        return pltpu.VMEM(lead + (tiles, nz + 1, 8, HALF), jnp.float32)

    return pl.pallas_call(
        functools.partial(main_kernel, nz, local_z),
        out_shape=(
            jax.ShapeDtypeStruct((local_z, 8, HALF), jnp.float32),
            jax.ShapeDtypeStruct((8, HALF), jnp.float32),
        ),
        in_specs=[vmem] * 5,
        out_specs=(vmem, vmem),
        scratch_shapes=[
            field(), field(), field(), field(18), field(9), field(9), field(36),
            field(19), field(19), field(6), field(), field(), field(3), field(3), field(3),
            field(tiles=2), field(tiles=2), field(24, tiles=2), field(3, tiles=2),
            pltpu.VMEM((nz, 8, HALF), jnp.float32),
            pltpu.VMEM((ROW_SLOTS, nz + 1, 8 * (ROW_TILES + 2), HALF), jnp.float32),
        ],
        compiler_params=pltpu.CompilerParams(vmem_limit_bytes=32 * 1024 * 1024),
    )(below, corner, above, quad, pixel_map[0])


def fits_one_exchange(mesh, solid):
    sizes = (mesh.shape["plane"], mesh.shape["thick"])
    return sizes == (2 * NBX, 2) and solid.shape[2:] == (8, HALF) and solid.shape[0] * GROUP == HALF


def solution(mesh):
    specs = (P("thick", "plane", None, None),) * 5 + (P("plane", None, None),)
    out_specs = (P("thick", "plane", None, None), P("plane", None, None))

    def program(solid, *rest):
        def with_bricks(*blocks):
            curvature, readings = one_exchange(*blocks)
            return curvature[:, None], readings[None]

        body = with_bricks if fits_one_exchange(mesh, solid) else per_device
        return jax.shard_map(
            body, mesh=mesh, in_specs=specs, out_specs=out_specs, check_vma=False
        )(solid, *rest)

    return program
```
